32 devices in a mesh: section: 2 (over y), tensor: 4 (over x, core), dp: 4 (over z).
Axes of the slice: x: 2, y: 2, z: 4, core: 2. Of those that a mesh axis runs over, the one named last changes fastest.
Arguments:
- inputs: bfloat16 [8, 1024, 1024], P('dp', 'tensor'), may hold values from -6 to 6
- out_grad: bfloat16 [8, 1024, 1024], P('dp', 'tensor'), may hold values from -6 to 6
- lang_ids: int32 [8], P('dp'), may hold values from 0 to 45
- lang_weights: int32 [46], replicated, may hold values from 1 to 64
- ln1_gain: float32 [2, 1024], P('section'), may hold values from 0.5 to 1.5
- ln1_bias: float32 [2, 1024], P('section'), may hold values from -1.2 to 1.2
- w_qkv: bfloat16 [2, 1024, 3, 1024], P('section', 'dp', None, 'tensor'), may hold values from -0.1875 to 0.1875
- b_qv: float32 [2, 2, 1024], P('section', None, 'tensor'), may hold values from -1.2 to 1.2
- w_out: bfloat16 [2, 1024, 1024], P('section', 'tensor', 'dp'), may hold values from -0.75 to 0.75
- b_out: float32 [2, 1024], P('section'), may hold values from -1.2 to 1.2
- ln2_gain: float32 [2, 1024], P('section'), may hold values from 0.5 to 1.5
- ln2_bias: float32 [2, 1024], P('section'), may hold values from -1.2 to 1.2
- w_up: bfloat16 [2, 1024, 4096], P('section', 'dp', 'tensor'), may hold values from -0.1875 to 0.1875
- b_up: float32 [2, 4096], P('section', 'tensor'), may hold values from -1.2 to 1.2
- w_down: bfloat16 [2, 4096, 1024], P('section', 'tensor', 'dp'), may hold values from -0.125 to 0.125
- b_down: float32 [2, 1024], P('section'), may hold values from -1.2 to 1.2
Outputs:
- acts: bfloat16 [2, 8, 1024, 1024], P('section', 'dp', 'tensor')
- in_grads: float32 [2, 8, 1024, 1024], P('section', 'dp', 'tensor')
- grad_ln1_gain: float32 [2, 1024], P('section', ('tensor', 'dp'))
- grad_ln1_bias: float32 [2, 1024], P('section', ('tensor', 'dp'))
- grad_w_qkv: float32 [2, 1024, 3, 1024], P('section', 'dp', None, 'tensor')
- grad_b_qv: float32 [2, 2, 1024], P('section', None, ('tensor', 'dp'))
- grad_w_out: float32 [2, 1024, 1024], P('section', 'tensor', 'dp')
- grad_b_out: float32 [2, 1024], P('section', ('tensor', 'dp'))
- grad_ln2_gain: float32 [2, 1024], P('section', ('tensor', 'dp'))
- grad_ln2_bias: float32 [2, 1024], P('section', ('tensor', 'dp'))
- grad_w_up: float32 [2, 1024, 4096], P('section', 'dp', 'tensor')
- grad_b_up: float32 [2, 4096], P('section', ('tensor', 'dp'))
- grad_w_down: float32 [2, 4096, 1024], P('section', 'tensor', 'dp')
- grad_b_down: float32 [2, 1024], P('section', ('tensor', 'dp'))
The draws below stay inside these ranges and needn't reach their ends.
Inputs may be any that keep to these rules, and one draw needn't show every extreme that they name: `lang_ids`: each row's language.
All inputs are finite; a program needn't handle non-finite values.
Results may differ from the reference program's by a relative error of at most 0.024.
Values may be sent and summed in bfloat16 or wider, within the bound.
A program may use at most 256 MiB of HBM per device.

```python
import jax
import jax.numpy as jnp
from jax import lax

D = 1024
HEADS = 16
HEAD = 64
FF = 4096
L = 1024
LANGS = 46
QBLOCK = 512
LAYERS = 2
ROWS = 8


def touch_ends(entries, stream_key, least, largest):
    longest = entries.shape.index(max(entries.shape))
    spots = []
    for shift in (0, 1):
        where = [jax.random.randint(jax.random.fold_in(stream_key, axis), (), 0, length) for axis, length in enumerate(entries.shape)]
        where[longest] = (where[longest] + shift) % entries.shape[longest]
        spots.append(tuple(where))
    return entries.at[spots[0]].set(least).at[spots[1]].set(largest)


def steps_of(rng, dims, pieces, least, largest):
    def one(position, parts):
        draws = jax.random.uniform(jax.random.fold_in(jax.random.fold_in(rng, 6), position), (parts,), jnp.float32, least / len(pieces), largest / len(pieces))
        return jnp.repeat(jnp.exp(draws), dims[position] // parts).reshape((-1,) + (1,) * (len(dims) - position - 1))

    factor_of = one(*pieces[0])
    for cut in pieces[1:]:
        factor_of = factor_of * one(*cut)
    return factor_of


def centred(stream_key, dims, scale, most, pieces=(), kind=jnp.bfloat16):
    array = jax.random.normal(stream_key, dims, jnp.float32) * scale
    if len(pieces) > 0:
        array = steps_of(stream_key, dims, pieces, -0.22, 0.18) * array
    return jnp.clip(array, min=-most, max=most).astype(kind)


def setup_inputs(seed: int = 0) -> dict:
    key_of = jax.random.split(jax.random.key(seed), 17)
    inputs = centred(key_of[0], (ROWS, L, D), 1.0, 6.0, ((0, 4), (1, 4)))
    out_grad = centred(key_of[1], (ROWS, L, D), 1.0, 6.0, ((0, 4), (1, 4)))
    lang_ids = touch_ends(jax.random.randint(key_of[2], (ROWS,), 0, LANGS), jax.random.fold_in(key_of[2], 1), 0, LANGS - 1).astype(jnp.int32)
    lang_weights = touch_ends(jax.random.randint(key_of[3], (LANGS,), 1, 65), jax.random.fold_in(key_of[3], 1), 1, 64).astype(jnp.int32)
    ln1_gain = jnp.clip(1.0 + 0.1 * jax.random.normal(key_of[4], (LAYERS, D), jnp.float32), 0.5, 1.5)
    ln1_bias = centred(key_of[5], (LAYERS, D), 0.2, 1.2, ((0, 2),), jnp.float32)
    w_qkv = centred(key_of[6], (LAYERS, D, 3, D), D ** -0.5, 0.1875, ((0, 2), (1, 4), (3, 4)))
    b_qv = centred(key_of[7], (LAYERS, 2, D), 0.2, 1.2, ((0, 2), (2, 4)), jnp.float32)
    w_out = centred(key_of[8], (LAYERS, D, D), (D // 16) ** -0.5, 0.75, ((0, 2), (1, 4), (2, 4)))
    b_out = centred(key_of[9], (LAYERS, D), 0.2, 1.2, ((0, 2),), jnp.float32)
    ln2_gain = jnp.clip(1.0 + 0.1 * jax.random.normal(key_of[10], (LAYERS, D), jnp.float32), 0.5, 1.5)
    ln2_bias = centred(key_of[11], (LAYERS, D), 0.2, 1.2, ((0, 2),), jnp.float32)
    w_up = centred(key_of[12], (LAYERS, D, FF), D ** -0.5, 0.1875, ((0, 2), (1, 4), (2, 4)))
    b_up = centred(key_of[13], (LAYERS, FF), 0.2, 1.2, ((0, 2), (1, 4)), jnp.float32)
    w_down = centred(key_of[14], (LAYERS, FF, D), (FF // 2) ** -0.5, 0.125, ((0, 2), (1, 4), (2, 4)))
    b_down = centred(key_of[15], (LAYERS, D), 0.2, 1.2, ((0, 2),), jnp.float32)
    return dict(inputs=inputs, out_grad=out_grad, lang_ids=lang_ids, lang_weights=lang_weights, ln1_gain=ln1_gain, ln1_bias=ln1_bias, w_qkv=w_qkv, b_qv=b_qv, w_out=w_out, b_out=b_out, ln2_gain=ln2_gain, ln2_bias=ln2_bias, w_up=w_up, b_up=b_up, w_down=w_down, b_down=b_down)


@jax.custom_vjp
def low(v):
    return lax.optimization_barrier(v.astype(jnp.bfloat16)).astype(jnp.float32)

@jax.custom_vjp
def low_back(v):
    return v

def low_keep(v):
    return (low(v), None)

def low_pass(kept, grad):
    return (grad,)

def back_keep(v):
    return (v, None)

def back_low(kept, grad):
    return (low(grad),)
low.defvjp(low_keep, low_pass)
low_back.defvjp(back_keep, back_low)
HIGHEST = lax.Precision.HIGHEST
EPSILON = 1e-05
GELU_SCALE = 0.7978845608028654

def layer_norm(values, gain, shift):
    center = values - lax.optimization_barrier(jnp.mean(values, axis=-1, keepdims=True))
    spread = lax.optimization_barrier(jnp.mean(center * center, axis=-1, keepdims=True))
    return center * lax.rsqrt(spread + EPSILON) * gain + shift

def gelu_tanh(values):
    return 0.5 * values * (1.0 + jnp.tanh(GELU_SCALE * (values + 0.044715 * values * values * values)))

def attend(queries, keys, values, slopes):
    block_total = L // QBLOCK
    query_blocks = queries.reshape(block_total, QBLOCK, HEADS, HEAD)
    starts = jnp.arange(block_total, dtype=jnp.int32) * QBLOCK
    columns = jnp.arange(L, dtype=jnp.int32)

    def one_block(item):
        block_queries, start = item
        rows = start + jnp.arange(QBLOCK, dtype=jnp.int32)
        offset = rows[:, None] - columns[None, :]
        scores = jnp.einsum('qhe,khe->hqk', block_queries, keys, precision=HIGHEST) * 0.125
        scores = scores - slopes[:, None, None] * offset.astype(jnp.float32)[None]
        scores = low_back(scores)
        scores = jnp.where(offset[None] >= 0, scores, -1e+30)
        highest = lax.optimization_barrier(jnp.max(scores, axis=-1, keepdims=True))
        weights = jnp.exp(scores - highest)
        probs = low(weights / lax.optimization_barrier(jnp.sum(weights, axis=-1, keepdims=True)))
        return jnp.einsum('hqk,khe->qhe', probs, values, precision=HIGHEST)
    mixed = lax.map(jax.checkpoint(one_block), (query_blocks, starts))
    return mixed.reshape(L, HEADS * HEAD)

def layer(hidden, params):
    first_gain, first_shift, qkv_weight, qkv_bias, out_weight, out_bias, second_gain, second_shift, up_weight, up_bias, down_weight, down_bias = params
    normed = low(layer_norm(hidden, first_gain, first_shift))
    projected = jnp.einsum('td,dch->tch', normed, qkv_weight, precision=HIGHEST)
    bias_rows = jnp.stack([qkv_bias[0], jnp.zeros_like(qkv_bias[0]), qkv_bias[1]])
    projected = low_back(low(projected + bias_rows))
    queries = projected[:, 0].reshape(L, HEADS, HEAD)
    keys = projected[:, 1].reshape(L, HEADS, HEAD)
    values = projected[:, 2].reshape(L, HEADS, HEAD)
    slopes = jnp.exp2(-8.0 * (jnp.arange(HEADS, dtype=jnp.float32) + 1.0) / HEADS)
    context = low_back(low(attend(queries, keys, values, slopes)))
    attended = low_back(jnp.dot(context, out_weight, precision=HIGHEST))
    middle = hidden + attended + out_bias
    second = low(layer_norm(middle, second_gain, second_shift))
    upward = low_back(jnp.dot(second, up_weight, precision=HIGHEST) + up_bias)
    activated = low(gelu_tanh(upward))
    downward = low_back(jnp.dot(activated, down_weight, precision=HIGHEST))
    return middle + downward + down_bias

def reference(inputs, out_grad, lang_ids, lang_weights, ln1_gain, ln1_bias, w_qkv, b_qv, w_out, b_out, ln2_gain, ln2_bias, w_up, b_up, w_down, b_down):
    stacked = tuple((item.astype(jnp.float32) for item in (ln1_gain, ln1_bias, w_qkv, b_qv, w_out, b_out, ln2_gain, ln2_bias, w_up, b_up, w_down, b_down)))
    first_params = tuple((item[0] for item in stacked))
    second_params = tuple((item[1] for item in stacked))
    matches = lang_ids[:, None] == jnp.arange(LANGS, dtype=jnp.int32)[None, :]
    row_scale = lax.optimization_barrier(jnp.sum(jnp.where(matches, lang_weights[None, :], 0), axis=1)).astype(jnp.float32) / 64.0

    def whole(tokens, params_first, params_second, probe):
        first_out = low(layer(tokens, params_first))
        passed = low_back(first_out) + probe
        return (first_out, low(layer(passed, params_second)))

    def row_step(totals, item):
        tokens, target, scale = item
        probe = jnp.zeros((L, D), jnp.float32)
        outputs, pull = jax.vjp(whole, tokens.astype(jnp.float32), first_params, second_params, probe)
        grads = pull((jnp.zeros((L, D), jnp.float32), target.astype(jnp.float32) * scale))
        totals = jax.tree.map(lambda left, right: left + right, totals, (grads[1], grads[2]))
        return (totals, (outputs[0].astype(jnp.bfloat16), outputs[1].astype(jnp.bfloat16), grads[0], grads[3]))
    zero_totals = jax.tree.map(jnp.zeros_like, (first_params, second_params))
    totals, outs = lax.scan(row_step, zero_totals, (inputs, out_grad, row_scale))
    acts = jnp.stack([outs[0], outs[1]])
    in_grads = jnp.stack([outs[2], outs[3]])
    layer_grads = [jnp.stack([first, second]) for first, second in zip(totals[0], totals[1])]
    return (acts, in_grads, layer_grads[0], layer_grads[1], layer_grads[2], layer_grads[3], layer_grads[4], layer_grads[5], layer_grads[6], layer_grads[7], layer_grads[8], layer_grads[9], layer_grads[10], layer_grads[11])
```

```python
import jax
import jax.numpy as jnp
from jax import lax
from jax.sharding import PartitionSpec as P

HEADS = 16
HEAD = 64

EPSILON = 1e-05
GELU_SCALE = 0.7978845608028654


def layer_norm(values, gain, shift):
    center = values - jnp.mean(values, axis=-1, keepdims=True)
    spread = jnp.mean(center * center, axis=-1, keepdims=True)
    return center * lax.rsqrt(spread + EPSILON) * gain + shift


def gelu_tanh(values):
    return (
        0.5 * values * (1.0 + jnp.tanh(GELU_SCALE * (values + 0.044715 * values * values * values)))
    )


def swapped(value):
    count = lax.axis_size("section")
    return lax.ppermute(value, "section", [(i, (i + 1) % count) for i in range(count)])


def gather_tokens(value):
    return lax.all_gather(value, "tensor", axis=0, tiled=True)


def scatter_tokens(value):
    return lax.psum_scatter(
        value.astype(jnp.bfloat16), "tensor", scatter_dimension=0, tiled=True
    ).astype(jnp.float32)


def score_bias(slopes, start, rows, columns):
    offset = (start + jnp.arange(rows, dtype=jnp.int32))[:, None] - jnp.arange(
        columns, dtype=jnp.int32
    )[None, :]
    return (offset[None] >= 0, -slopes[:, None, None] * offset.astype(jnp.float32)[None])


def block_scores(queries, keys, slopes, start):
    allowed, penalty = score_bias(slopes, start, queries.shape[0], keys.shape[0])
    scores = (
        jnp.einsum("qhe,khe->hqk", queries, keys, preferred_element_type=jnp.float32) * 0.125
        + penalty
    )
    return jnp.where(allowed, scores, -1e30)


def layer_forward(entering, weights, slopes, query_block):
    hidden = entering.astype(jnp.float32)
    normed = layer_norm(hidden, weights["ln1_gain"], weights["ln1_bias"]).astype(jnp.bfloat16)
    gathered = gather_tokens(normed)
    length = gathered.shape[0]
    local_width = weights["qkv"].shape[2]
    local_heads = local_width // HEAD
    projected = jnp.einsum("td,dch->tch", gathered, weights["qkv"], preferred_element_type=jnp.float32)
    projected = (projected + weights["bias_rows"]).astype(jnp.bfloat16)
    queries, keys, values = [
        projected[:, c].reshape(length, local_heads, HEAD) for c in range(3)
    ]
    totals, parts = [], []
    for start in range(0, length, query_block):
        stop = start + query_block
        scores = block_scores(queries[start:stop], keys[:stop], slopes, start)
        highest = jnp.max(scores, axis=-1, keepdims=True)
        grown = jnp.exp(scores - highest)
        total = jnp.sum(grown, axis=-1, keepdims=True)
        totals.append(highest + jnp.log(total))
        parts.append(
            jnp.einsum(
                "hqk,khe->qhe",
                (grown / total).astype(jnp.bfloat16),
                values[:stop],
                preferred_element_type=jnp.float32,
            )
        )
    context = jnp.concatenate(parts, 0).reshape(length, local_width).astype(jnp.bfloat16)
    attended = scatter_tokens(jnp.dot(context, weights["out"], preferred_element_type=jnp.float32))
    middle = hidden + attended + weights["b_out"]
    second = layer_norm(middle, weights["ln2_gain"], weights["ln2_bias"]).astype(jnp.bfloat16)
    second_all = gather_tokens(second)
    upward = jnp.dot(second_all, weights["up"], preferred_element_type=jnp.float32) + weights["b_up"]
    activated = gelu_tanh(upward).astype(jnp.bfloat16)
    downward = scatter_tokens(
        jnp.dot(activated, weights["down"], preferred_element_type=jnp.float32)
    )
    leaving = (middle + downward + weights["b_down"]).astype(jnp.bfloat16)
    saved = dict(
        hidden=hidden,
        middle=middle,
        normed=gathered,
        projected=projected,
        totals=totals,
        context=context,
        second=second_all,
        upward=upward,
        activated=activated,
    )
    return leaving, saved


def layer_backward(incoming, weights, saved, slopes, query_block):
    down_rows = gather_tokens(incoming.astype(jnp.bfloat16))
    length = down_rows.shape[0]
    grad_act = jnp.einsum("td,fd->tf", down_rows, weights["down"], preferred_element_type=jnp.float32)
    grad_up = jax.vjp(gelu_tanh, saved["upward"])[1](grad_act)[0].astype(jnp.bfloat16)
    grad_second = scatter_tokens(
        jnp.einsum("tf,df->td", grad_up, weights["up"], preferred_element_type=jnp.float32)
    )
    pull = jax.vjp(layer_norm, saved["middle"], weights["ln2_gain"], weights["ln2_bias"])[1]
    grad_norm, grad_gain2, grad_shift2 = pull(grad_second)
    grad_middle = incoming + grad_norm
    attn_rows = gather_tokens(grad_middle.astype(jnp.bfloat16))
    grad_context = jnp.einsum(
        "td,hd->th", attn_rows, weights["out"], preferred_element_type=jnp.float32
    ).astype(jnp.bfloat16)
    local_width = grad_context.shape[1]
    local_heads = local_width // HEAD
    grad_context = grad_context.reshape(length, local_heads, HEAD)
    queries, keys, values = [
        saved["projected"][:, c].reshape(length, local_heads, HEAD) for c in range(3)
    ]
    query_parts = []
    grad_keys = jnp.zeros((length, local_heads, HEAD), jnp.float32)
    grad_values = jnp.zeros((length, local_heads, HEAD), jnp.float32)
    for index, start in enumerate(range(0, length, query_block)):
        stop = start + query_block
        probs = jnp.exp(
            block_scores(queries[start:stop], keys[:stop], slopes, start) - saved["totals"][index]
        )
        block_grad = grad_context[start:stop]
        grad_probs = jnp.einsum(
            "qhe,khe->hqk", block_grad, values[:stop], preferred_element_type=jnp.float32
        )
        inner = jnp.sum(probs * grad_probs, axis=-1, keepdims=True)
        grad_scores = (probs * (grad_probs - inner)).astype(jnp.bfloat16)
        query_parts.append(
            jnp.einsum("hqk,khe->qhe", grad_scores, keys[:stop], preferred_element_type=jnp.float32)
            * 0.125
        )
        tail = ((0, length - stop), (0, 0), (0, 0))
        grad_keys = grad_keys + jnp.pad(
            jnp.einsum(
                "hqk,qhe->khe", grad_scores, queries[start:stop], preferred_element_type=jnp.float32
            )
            * 0.125,
            tail,
        )
        grad_values = grad_values + jnp.pad(
            jnp.einsum(
                "hqk,qhe->khe",
                probs.astype(jnp.bfloat16),
                block_grad,
                preferred_element_type=jnp.float32,
            ),
            tail,
        )
    grad_projected = jnp.stack(
        [
            part.reshape(length, local_width)
            for part in (jnp.concatenate(query_parts, 0), grad_keys, grad_values)
        ],
        axis=1,
    ).astype(jnp.bfloat16)
    grad_normed = scatter_tokens(
        jnp.einsum("tch,dch->td", grad_projected, weights["qkv"], preferred_element_type=jnp.float32)
    )
    pull = jax.vjp(layer_norm, saved["hidden"], weights["ln1_gain"], weights["ln1_bias"])[1]
    grad_norm, grad_gain1, grad_shift1 = pull(grad_normed)
    grad_hidden = grad_middle + grad_norm
    small = jnp.stack(
        [
            grad_gain1,
            grad_shift1,
            jnp.sum(grad_middle, axis=0),
            grad_gain2,
            grad_shift2,
            jnp.sum(incoming, axis=0),
        ]
    )
    large = dict(
        qkv=jnp.einsum("td,tch->dch", saved["normed"], grad_projected, preferred_element_type=jnp.float32),
        out=jnp.einsum("th,td->hd", saved["context"], attn_rows, preferred_element_type=jnp.float32),
        up=jnp.einsum("td,tf->df", saved["second"], grad_up, preferred_element_type=jnp.float32),
        down=jnp.einsum("tf,td->fd", saved["activated"], down_rows, preferred_element_type=jnp.float32),
        b_qv=jnp.sum(grad_projected[:, 0::2].astype(jnp.float32), axis=0),
        b_up=jnp.sum(grad_up.astype(jnp.float32), axis=0),
    )
    return grad_hidden, small, large


def per_device(
    inputs,
    out_grad,
    lang_ids,
    lang_weights,
    ln1_gain,
    ln1_bias,
    w_qkv,
    b_qv,
    w_out,
    b_out,
    ln2_gain,
    ln2_bias,
    w_up,
    b_up,
    w_down,
    b_down,
):
    section = lax.axis_index("section")
    tensor_count = lax.axis_size("tensor")
    layer_count = lax.axis_size("section")
    length = inputs.shape[1] * tensor_count
    query_block = min(512, length // 2)
    local_heads = w_qkv.shape[3] // HEAD
    head_ids = lax.axis_index("tensor") * local_heads + jnp.arange(local_heads, dtype=jnp.int32)
    slopes = jnp.exp2(-8.0 * (head_ids.astype(jnp.float32) + 1.0) / HEADS)

    def both(value):
        other = swapped(value)
        return [jnp.where(section == l, value, other) for l in range(layer_count)]

    def over_dp(value, axis):
        return both(lax.all_gather(value, "dp", axis=axis, tiled=True))

    qkv_all, up_all = over_dp(w_qkv[0], 0), over_dp(w_up[0], 0)
    out_all, down_all = over_dp(w_out[0], 1), over_dp(w_down[0], 1)
    vectors = [
        both(item[0]) for item in (ln1_gain, ln1_bias, b_qv, b_out, ln2_gain, ln2_bias, b_up, b_down)
    ]
    layers = []
    for l in range(layer_count):
        gain1, bias1, qv, bout, gain2, bias2, bup, bdown = [item[l] for item in vectors]
        layers.append(
            dict(
                ln1_gain=gain1,
                ln1_bias=bias1,
                ln2_gain=gain2,
                ln2_bias=bias2,
                qkv=qkv_all[l],
                out=out_all[l],
                up=up_all[l],
                down=down_all[l],
                bias_rows=jnp.stack([qv[0], jnp.zeros_like(qv[0]), qv[1]]),
                b_out=bout,
                b_up=bup,
                b_down=bdown,
            )
        )
    row = lax.dynamic_index_in_dim(inputs, section, 0, keepdims=False)
    target = lax.dynamic_index_in_dim(out_grad, section, 0, keepdims=False)
    lang = lax.dynamic_index_in_dim(lang_ids, section, 0, keepdims=False)
    matches = lang == jnp.arange(lang_weights.shape[0], dtype=jnp.int32)
    scale = jnp.sum(jnp.where(matches, lang_weights, 0)).astype(jnp.float32) / 64.0

    acts, saved = [], []
    for l in range(layer_count):
        row, kept = layer_forward(row, layers[l], slopes, query_block)
        acts.append(row)
        saved.append(kept)
    grads, small, large = [None] * layer_count, [None] * layer_count, [None] * layer_count
    incoming = target.astype(jnp.float32) * scale
    for l in reversed(range(layer_count)):
        grads[l], small[l], large[l] = layer_backward(
            incoming, layers[l], saved[l], slopes, query_block
        )
        incoming = grads[l].astype(jnp.bfloat16).astype(jnp.float32)

    def mine(items):
        return jnp.where(section == 0, items[0], items[1])

    def theirs(items):
        return jnp.where(section == 0, items[1], items[0])

    def rows_of(items):
        own, other = mine(items), swapped(theirs(items))
        return jnp.stack([jnp.where(section == r, own, other) for r in range(layer_count)])[None]

    def reduced(name, axis):
        items = [item[name].astype(jnp.bfloat16) for item in large]
        total = mine(items) + swapped(theirs(items))
        return lax.psum_scatter(total, "dp", scatter_dimension=axis, tiled=True).astype(
            jnp.float32
        )[None]

    small_total = mine(small) + swapped(theirs(small))
    small_shards = lax.psum_scatter(small_total, ("tensor", "dp"), scatter_dimension=1, tiled=True)
    return (
        rows_of(acts),
        rows_of([item.astype(jnp.bfloat16) for item in grads]).astype(jnp.float32),
        small_shards[0][None],
        small_shards[1][None],
        reduced("qkv", 0),
        reduced("b_qv", 1),
        reduced("out", 1),
        small_shards[2][None],
        small_shards[3][None],
        small_shards[4][None],
        reduced("up", 0),
        reduced("b_up", 0),
        reduced("down", 1),
        small_shards[5][None],
    )


def solution(mesh):
    return jax.shard_map(
        per_device,
        mesh=mesh,
        in_specs=(
            P("dp", "tensor", None),
            P("dp", "tensor", None),
            P("dp"),
            P(),
            P("section", None),
            P("section", None),
            P("section", "dp", None, "tensor"),
            P("section", None, "tensor"),
            P("section", "tensor", "dp"),
            P("section", None),
            P("section", None),
            P("section", None),
            P("section", "dp", "tensor"),
            P("section", "tensor"),
            P("section", "tensor", "dp"),
            P("section", None),
        ),
        out_specs=(
            P("section", "dp", "tensor", None),
            P("section", "dp", "tensor", None),
            P("section", ("tensor", "dp")),
            P("section", ("tensor", "dp")),
            P("section", "dp", None, "tensor"),
            P("section", None, ("tensor", "dp")),
            P("section", "tensor", "dp"),
            P("section", ("tensor", "dp")),
            P("section", ("tensor", "dp")),
            P("section", ("tensor", "dp")),
            P("section", "dp", "tensor"),
            P("section", ("tensor", "dp")),
            P("section", "tensor", "dp"),
            P("section", ("tensor", "dp")),
        ),
        check_vma=False,
    )
```

```python
import functools

import jax
import jax.numpy as jnp
from jax import lax
from jax.experimental import pallas as pl
from jax.experimental.pallas import tpu as pltpu
from jax.sharding import PartitionSpec as P

HEADS = 16
HEAD = 64
PAIR = 2 * HEAD

EPSILON = 1e-05
GELU_SCALE = 0.7978845608028654

MESH = pl.DeviceIdType.MESH
F32 = jnp.float32
BF16 = jnp.bfloat16
CHUNKS = 2
VMEM_LIMIT = 60 * 1024 * 1024


def rows_at(start, size):
    return pl.ds(pl.multiple_of(start, size), size)


def mm(left, right):
    return lax.dot_general(left, right, (((1,), (0,)), ((), ())), preferred_element_type=F32)


def mm_t(left, right):
    return lax.dot_general(left, right, (((1,), (1,)), ((), ())), preferred_element_type=F32)


class Ring:
    def __init__(self, block):
        self.block = block
        self.chunk = block // CHUNKS
        self.me = lax.axis_index("tensor")
        core, chip = lax.rem(self.me, 2), self.me // 2
        self.mate = self.me + 1 - 2 * core
        self.peer = self.me + 2 - 4 * chip
        self.far = self.peer + 1 - 2 * core

    def greet(self):
        barrier = pltpu.get_barrier_semaphore()
        for other in (self.mate, self.peer):
            pl.semaphore_signal(barrier, inc=1, device_id={"tensor": other}, device_id_type=MESH)
        pl.semaphore_wait(barrier, 2)

    def rows(self, owner, c):
        return rows_at(owner * self.block + c * self.chunk, self.chunk)

    def send(self, src, dst, sems, kind, c, other):
        return pltpu.make_async_remote_copy(
            src_ref=src,
            dst_ref=dst,
            send_sem=sems.at[0, kind, c],
            recv_sem=sems.at[1, kind, c],
            device_id={"tensor": other},
            device_id_type=MESH,
        )


class Gather:
    def __init__(self, ring, every, sems):
        self.ring, self.every, self.sems = ring, every, sems

    def copy(self, kind, owner, c):
        ring = self.ring
        at = self.every.at[ring.rows(owner, c)]
        return ring.send(at, at, self.sems, kind, c, ring.peer if kind == 1 else ring.mate)

    def start(self, c):
        self.copy(1, self.ring.me, c).start()
        self.copy(0, self.ring.me, c).start()

    def arrived_mate(self, c):
        self.copy(0, self.ring.mate, c).wait_recv()

    def arrived_peer(self, c):
        self.copy(1, self.ring.peer, c).wait_recv()
        self.copy(2, self.ring.peer, c).start()

    def arrived_far(self, c):
        self.copy(2, self.ring.far, c).wait_recv()

    def finish(self):
        for c in range(CHUNKS):
            for kind, owner in ((0, self.ring.me), (1, self.ring.me), (2, self.ring.peer)):
                self.copy(kind, owner, c).wait_send()


class Scatter:
    def __init__(self, ring, stage, land, sems):
        self.ring, self.stage, self.land, self.sems = ring, stage, land, sems

    def copy(self, kind, c):
        ring = self.ring
        at = pl.ds(c * ring.chunk, ring.chunk)
        return ring.send(
            self.stage.at[kind, at],
            self.land.at[kind, at],
            self.sems,
            kind,
            c,
            ring.peer if kind == 1 else ring.mate,
        )

    def put(self, kind, c, value):
        self.stage[kind, pl.ds(c * self.ring.chunk, self.ring.chunk)] = value.astype(BF16)
        self.copy(kind, c).start()

    def take(self, kind, c):
        self.copy(kind, c).wait_recv()
        return self.land[kind, pl.ds(c * self.ring.chunk, self.ring.chunk)].astype(F32)

    def to_peer(self, c, far_part, peer_part):
        self.put(0, c, far_part)
        self.put(1, c, peer_part + self.take(0, c))

    def finish(self):
        for kind in range(3):
            for c in range(CHUNKS):
                self.copy(kind, c).wait_send()


def normalize(values):
    center = values - jnp.mean(values, axis=-1, keepdims=True)
    scale = lax.rsqrt(jnp.mean(center * center, axis=-1, keepdims=True) + EPSILON)
    return center * scale, scale


def norm_pull(values, gain, grad):
    unit, scale = normalize(values)
    scaled = grad * gain
    pulled = scale * (
        scaled
        - jnp.mean(scaled, axis=-1, keepdims=True)
        - unit * jnp.mean(scaled * unit, axis=-1, keepdims=True)
    )
    return pulled, jnp.sum(grad * unit, axis=0, keepdims=True), jnp.sum(grad, axis=0, keepdims=True)


def scores_of(keys, queries, slope, penalty_ref, start):
    stop, count = keys.shape[0], queries.shape[0]
    scores = mm_t(keys, queries) + slope * penalty_ref[:stop]
    last = scores[start:]
    allowed = lax.broadcasted_iota(jnp.int32, (count, count), 0) <= lax.broadcasted_iota(
        jnp.int32, (count, count), 1
    )
    last = jnp.where(allowed, last, -1e30)
    return last if start == 0 else jnp.concatenate([scores[:start], last], axis=0)


def head_mask(value, which):
    lane = lax.broadcasted_iota(jnp.int32, value.shape, 1)
    inside = lane < HEAD if which == 0 else lane >= HEAD
    return jnp.where(inside, value, jnp.zeros_like(value))


def fill_penalty(penalty_ref):
    penalty_ref[...] = lax.broadcasted_iota(jnp.int32, penalty_ref.shape, 0).astype(F32)


def attend_forward(proj, context, totals, slopes, penalty, block):
    length, width = context.shape

    def pair_step(pair, carry):
        lanes = pl.ds(pl.multiple_of(pair * PAIR, PAIR), PAIR)
        for start in range(0, length, block):
            stop = start + block
            queries = proj[0, start:stop, lanes] * jnp.asarray(0.125, BF16)
            keys = proj[1, :stop, lanes]
            values_t = proj[2, :stop, lanes].T
            outs = []
            for which in range(2):
                head = pair * 2 + which
                slope = slopes[pl.ds(head, 1), :]
                scores = scores_of(keys, head_mask(queries, which), slope, penalty, start)
                highest = jnp.max(scores, axis=0, keepdims=True)
                grown = jnp.exp(scores - highest)
                total = jnp.sum(grown, axis=0, keepdims=True)
                mixed = mm(values_t[which * HEAD : (which + 1) * HEAD], grown.astype(BF16))
                outs.append(mixed / total)
                totals[pl.ds(head, 1), start:stop] = highest + jnp.log(total)
            context[start:stop, lanes] = jnp.concatenate(outs, axis=0).T.astype(BF16)
        return carry

    lax.fori_loop(0, width // PAIR, pair_step, 0)


def attend_backward(proj, grad_context, totals, slopes, penalty, grad_proj, sums, block):
    length, width = grad_context.shape

    def pair_step(pair, carry):
        lanes = pl.ds(pl.multiple_of(pair * PAIR, PAIR), PAIR)
        for start in range(0, length, block):
            stop = start + block
            queries = proj[0, start:stop, lanes] * jnp.asarray(0.125, BF16)
            keys = proj[1, :stop, lanes]
            keys_t = keys.T
            values = proj[2, :stop, lanes]
            grads = grad_context[start:stop, lanes]
            outs = []
            for which in range(2):
                head = pair * 2 + which
                slope = slopes[pl.ds(head, 1), :]
                one_query = head_mask(queries, which)
                one_grad = head_mask(grads, which)
                scores = scores_of(keys, one_query, slope, penalty, start)
                probs = jnp.exp(scores - totals[pl.ds(head, 1), start:stop])
                pulled = probs * mm_t(values, one_grad)
                inner = jnp.sum(pulled, axis=0, keepdims=True)
                grad_scores = (pulled - probs * inner).astype(BF16)
                outs.append(mm(keys_t[which * HEAD : (which + 1) * HEAD], grad_scores) * 0.125)
                grad_keys = mm(grad_scores, one_query)
                grad_values = mm(probs.astype(BF16), one_grad)
                if which == 0:
                    first_keys, first_values = grad_keys, grad_values
                else:
                    grad_keys, grad_values = grad_keys + first_keys, grad_values + first_values
            grad_proj[0, start:stop, lanes] = jnp.concatenate(outs, axis=0).T.astype(BF16)
            if start > 0:
                sums[0, :start] += grad_keys[:start]
                sums[1, :start] += grad_values[:start]
            sums[0, start:stop] = grad_keys[start:]
            sums[1, start:stop] = grad_values[start:]
        grad_proj[1, :, lanes] = sums[0].astype(BF16)
        grad_proj[2, :, lanes] = sums[1].astype(BF16)
        return carry

    lax.fori_loop(0, width // PAIR, pair_step, 0)


def attention_forward_kernel(
    x, gain, shift, w_qkv, b_qkv, w_out, b_out, slopes,
    normed, proj, context, totals, middle,
    penalty, stage, land, gather_sems, scatter_sems,
):
    block = x.shape[0]
    ring = Ring(block)
    ring.greet()
    gather = Gather(ring, normed, gather_sems)
    chunk = ring.chunk
    for c in range(CHUNKS):
        at = pl.ds(c * chunk, chunk)
        unit, _ = normalize(x[at].astype(F32))
        normed[ring.rows(ring.me, c)] = (unit * gain[...] + shift[...]).astype(BF16)
        gather.start(c)
    fill_penalty(penalty)

    def project(owner, c, size):
        at = rows_at(owner * block + c * chunk, size)
        rows = normed[at]
        for part in range(3):
            proj[part, at] = (mm(rows, w_qkv[part]) + b_qkv[part]).astype(BF16)

    project(ring.me, 0, block)
    for c in range(CHUNKS):
        gather.arrived_mate(c)
    project(ring.mate, 0, block)
    for c in range(CHUNKS):
        gather.arrived_peer(c)
        project(ring.peer, c, chunk)
        gather.arrived_far(c)
        project(ring.far, c, chunk)
    attend_forward(proj, context, totals, slopes, penalty, block)
    scatter = Scatter(ring, stage, land, scatter_sems)

    def part_of(owner, c):
        return mm(context[ring.rows(owner, c)], w_out[...])

    for c in range(CHUNKS):
        scatter.put(0, c, part_of(ring.far, c))
        scatter.put(1, c, part_of(ring.peer, c) + scatter.take(0, c))
    for c in range(CHUNKS):
        scatter.put(2, c, part_of(ring.mate, c))
    for c in range(CHUNKS):
        at = pl.ds(c * chunk, chunk)
        total = part_of(ring.me, c) + scatter.take(2, c) + scatter.take(1, c)
        middle[at] = x[at].astype(F32) + total + b_out[...]
    gather.finish()
    scatter.finish()


def mlp_forward_kernel(
    middle, gain, shift, w_up, b_up, w_down, b_down,
    second, activated, slope_of, leaving,
    own, stage, land, gather_sems, scatter_sems,
):
    block = middle.shape[0]
    ring = Ring(block)
    ring.greet()
    gather = Gather(ring, second, gather_sems)
    scatter = Scatter(ring, stage, land, scatter_sems)
    chunk = ring.chunk
    for c in range(CHUNKS):
        at = pl.ds(c * chunk, chunk)
        unit, _ = normalize(middle[at])
        second[ring.rows(ring.me, c)] = (unit * gain[...] + shift[...]).astype(BF16)
        gather.start(c)

    def expand(at):
        upward = mm(second[at], w_up[...]) + b_up[...]
        inner = jnp.tanh(GELU_SCALE * (upward + 0.044715 * upward * upward * upward))
        half = 0.5 * (1.0 + inner)
        value = upward * half
        slope = half + 0.5 * upward * (1.0 - inner * inner) * GELU_SCALE * (
            1.0 + 3 * 0.044715 * upward * upward
        )
        value = value.astype(BF16)
        activated[at] = value
        slope_of[at] = slope.astype(BF16)
        return mm(value, w_down[...])

    own[...] = expand(rows_at(ring.me * block, block))
    for c in range(CHUNKS):
        gather.arrived_mate(c)
    part = expand(rows_at(ring.mate * block, block))
    for c in range(CHUNKS):
        scatter.put(2, c, part[c * chunk : (c + 1) * chunk])
    for c in range(CHUNKS):
        gather.arrived_peer(c)
        peer_part = expand(ring.rows(ring.peer, c))
        gather.arrived_far(c)
        scatter.put(0, c, expand(ring.rows(ring.far, c)))
        scatter.put(1, c, peer_part + scatter.take(0, c))
    for c in range(CHUNKS):
        at = pl.ds(c * chunk, chunk)
        total = own[at] + scatter.take(2, c) + scatter.take(1, c)
        leaving[at] = (middle[at] + total + b_down[...]).astype(BF16)
    gather.finish()
    scatter.finish()


def mlp_backward_kernel(
    incoming, middle, gain, w_up, w_down, slope_of,
    down_rows, grad_up, grad_middle, small, up_sum,
    own, stage, land, gather_sems, scatter_sems,
):
    block = middle.shape[0]
    ring = Ring(block)
    ring.greet()
    gather = Gather(ring, down_rows, gather_sems)
    scatter = Scatter(ring, stage, land, scatter_sems)
    chunk = ring.chunk
    for c in range(CHUNKS):
        down_rows[ring.rows(ring.me, c)] = incoming[pl.ds(c * chunk, chunk)].astype(BF16)
        gather.start(c)
    up_sum[...] = jnp.zeros_like(up_sum)

    def pull(at):
        grad = mm_t(down_rows[at], w_down[...]) * slope_of[at].astype(F32)
        grad = grad.astype(BF16)
        grad_up[at] = grad
        up_sum[...] += jnp.sum(grad.astype(F32), axis=0, keepdims=True)
        return mm_t(grad, w_up[...])

    own[...] = pull(rows_at(ring.me * block, block))
    for c in range(CHUNKS):
        gather.arrived_mate(c)
    part = pull(rows_at(ring.mate * block, block))
    for c in range(CHUNKS):
        scatter.put(2, c, part[c * chunk : (c + 1) * chunk])
    for c in range(CHUNKS):
        gather.arrived_peer(c)
        peer_part = pull(ring.rows(ring.peer, c))
        gather.arrived_far(c)
        scatter.put(0, c, pull(ring.rows(ring.far, c)))
        scatter.put(1, c, peer_part + scatter.take(0, c))
    small[...] = jnp.zeros_like(small)
    for c in range(CHUNKS):
        at = pl.ds(c * chunk, chunk)
        total = own[at] + scatter.take(2, c) + scatter.take(1, c)
        pulled, grad_gain, grad_shift = norm_pull(middle[at], gain[...], total)
        before = incoming[at]
        after = before + pulled
        grad_middle[at] = after
        small[0:1] += jnp.sum(after, axis=0, keepdims=True)
        small[1:2] += grad_gain
        small[2:3] += grad_shift
        small[3:4] += jnp.sum(before, axis=0, keepdims=True)
    gather.finish()
    scatter.finish()


def attention_backward_kernel(
    grad_middle, x, gain, w_qkv, w_out, slopes, proj, totals,
    attn_rows, grad_proj, grad_hidden, small, qv_sum,
    grad_context, sums, penalty, stage, land, gather_sems, scatter_sems,
):
    block = x.shape[0]
    ring = Ring(block)
    ring.greet()
    gather = Gather(ring, attn_rows, gather_sems)
    scatter = Scatter(ring, stage, land, scatter_sems)
    chunk = ring.chunk
    for c in range(CHUNKS):
        attn_rows[ring.rows(ring.me, c)] = grad_middle[pl.ds(c * chunk, chunk)].astype(BF16)
        gather.start(c)
    fill_penalty(penalty)

    def pull(at):
        grad_context[at] = mm_t(attn_rows[at], w_out[...]).astype(BF16)

    pull(rows_at(ring.me * block, block))
    for c in range(CHUNKS):
        gather.arrived_mate(c)
    pull(rows_at(ring.mate * block, block))
    for c in range(CHUNKS):
        gather.arrived_peer(c)
        pull(ring.rows(ring.peer, c))
        gather.arrived_far(c)
        pull(ring.rows(ring.far, c))
    attend_backward(proj, grad_context, totals, slopes, penalty, grad_proj, sums, block)
    qv_sum[...] = jnp.zeros_like(qv_sum)
    qv_sum[0:1] = jnp.sum(grad_proj[0].astype(F32), axis=0, keepdims=True)
    qv_sum[1:2] = jnp.sum(grad_proj[2].astype(F32), axis=0, keepdims=True)

    def part_of(owner, c):
        at = ring.rows(owner, c)
        total = mm_t(grad_proj[0, at], w_qkv[0])
        for part in range(1, 3):
            total += mm_t(grad_proj[part, at], w_qkv[part])
        return total

    for c in range(CHUNKS):
        scatter.put(0, c, part_of(ring.far, c))
        scatter.put(1, c, part_of(ring.peer, c) + scatter.take(0, c))
    for c in range(CHUNKS):
        scatter.put(2, c, part_of(ring.mate, c))
    small[...] = jnp.zeros_like(small)
    for c in range(CHUNKS):
        at = pl.ds(c * chunk, chunk)
        total = part_of(ring.me, c) + scatter.take(2, c) + scatter.take(1, c)
        pulled, grad_gain, grad_shift = norm_pull(x[at].astype(F32), gain[...], total)
        grad_hidden[at] = grad_middle[at] + pulled
        small[0:1] += grad_gain
        small[1:2] += grad_shift
    gather.finish()
    scatter.finish()


def call(kernel, name, number, args, outs, scratch):
    vmem = pl.BlockSpec(memory_space=pltpu.VMEM)
    return pl.pallas_call(
        kernel,
        out_shape=[jax.ShapeDtypeStruct(shape, dtype) for shape, dtype in outs],
        in_specs=[vmem] * len(args),
        out_specs=[vmem] * len(outs),
        scratch_shapes=scratch,
        compiler_params=pltpu.CompilerParams(
            collective_id=number, has_side_effects=True, vmem_limit_bytes=VMEM_LIMIT
        ),
        name=name,
    )(*args)


def link_scratch(block, width):
    return [
        pltpu.VMEM((3, block, width), BF16),
        pltpu.VMEM((3, block, width), BF16),
        pltpu.SemaphoreType.DMA((2, 3, CHUNKS)),
        pltpu.SemaphoreType.DMA((2, 3, CHUNKS)),
    ]


def row_vector(value):
    return value.reshape(1, -1)


def layer_forward(x, w, slopes):
    block, width = x.shape
    length = block * lax.axis_size("tensor")
    local = w["out"].shape[0]
    heads = local // HEAD
    normed, proj, context, totals, middle = call(
        attention_forward_kernel,
        "attention_forward",
        1,
        (x, row_vector(w["ln1_gain"]), row_vector(w["ln1_bias"]), w["qkv"], w["b_qkv"], w["out"], row_vector(w["b_out"]), slopes),
        [((length, width), BF16), ((3, length, local), BF16), ((length, local), BF16), ((heads, length), F32), ((block, width), F32)],
        [pltpu.VMEM((length, block), F32)] + link_scratch(block, width),
    )
    units = w["up"].shape[1]
    second, activated, slope_of, leaving = call(
        mlp_forward_kernel,
        "mlp_forward",
        2,
        (middle, row_vector(w["ln2_gain"]), row_vector(w["ln2_bias"]), w["up"], row_vector(w["b_up"]), w["down"], row_vector(w["b_down"])),
        [((length, width), BF16), ((length, units), BF16), ((length, units), BF16), ((block, width), BF16)],
        [pltpu.VMEM((block, width), F32)] + link_scratch(block, width),
    )
    saved = dict(x=x, normed=normed, proj=proj, context=context, totals=totals, middle=middle, second=second, activated=activated, slope_of=slope_of)
    return leaving, saved


def layer_backward(incoming, w, s, slopes):
    block, width = incoming.shape
    length = block * lax.axis_size("tensor")
    local, units = w["out"].shape[0], w["up"].shape[1]
    down_rows, grad_up, grad_middle, small_a, up_sum = call(
        mlp_backward_kernel,
        "mlp_backward",
        3,
        (incoming, s["middle"], row_vector(w["ln2_gain"]), w["up"], w["down"], s["slope_of"]),
        [((length, width), BF16), ((length, units), BF16), ((block, width), F32), ((8, width), F32), ((1, units), F32)],
        [pltpu.VMEM((block, width), F32)] + link_scratch(block, width),
    )
    attn_rows, grad_proj, grad_hidden, small_b, qv_sum = call(
        attention_backward_kernel,
        "attention_backward",
        4,
        (grad_middle, s["x"], row_vector(w["ln1_gain"]), w["qkv"], w["out"], slopes, s["proj"], s["totals"]),
        [((length, width), BF16), ((3, length, local), BF16), ((block, width), F32), ((8, width), F32), ((8, local), F32)],
        [pltpu.VMEM((length, local), BF16), pltpu.VMEM((2, length, PAIR), F32), pltpu.VMEM((length, block), F32)]
        + link_scratch(block, width),
    )
    small = jnp.stack([small_b[0], small_b[1], small_a[0], small_a[1], small_a[2], small_a[3]])
    large = dict(
        qkv=jnp.einsum("td,cth->cdh", s["normed"], grad_proj, preferred_element_type=F32),
        out=jnp.einsum("th,td->hd", s["context"], attn_rows, preferred_element_type=F32),
        up=jnp.einsum("td,tf->df", s["second"], grad_up, preferred_element_type=F32),
        down=jnp.einsum("tf,td->fd", s["activated"], down_rows, preferred_element_type=F32),
        b_qv=qv_sum[:2],
        b_up=up_sum[0],
    )
    return grad_hidden, small, large


def swapped(value):
    count = lax.axis_size("section")
    return lax.ppermute(value, "section", [(i, (i + 1) % count) for i in range(count)])


def per_device(
    inputs,
    out_grad,
    lang_ids,
    lang_weights,
    ln1_gain,
    ln1_bias,
    w_qkv,
    b_qv,
    w_out,
    b_out,
    ln2_gain,
    ln2_bias,
    w_up,
    b_up,
    w_down,
    b_down,
):
    section = lax.axis_index("section")
    layer_count = lax.axis_size("section")
    local_heads = w_qkv.shape[3] // HEAD
    head_ids = lax.axis_index("tensor") * local_heads + jnp.arange(local_heads, dtype=jnp.int32)
    slopes = jnp.exp2(-8.0 * (head_ids.astype(jnp.float32) + 1.0) / HEADS)
    slopes = jnp.broadcast_to(slopes[:, None], (local_heads, inputs.shape[1]))

    def both(value):
        other = swapped(value)
        return [jnp.where(section == l, value, other) for l in range(layer_count)]

    def over_dp(value, axis):
        return both(lax.all_gather(value, "dp", axis=axis, tiled=True))

    qkv_all, up_all = over_dp(jnp.transpose(w_qkv[0], (1, 0, 2)), 1), over_dp(w_up[0], 0)
    out_all, down_all = over_dp(w_out[0], 1), over_dp(w_down[0], 1)
    vectors = [
        both(item[0]) for item in (ln1_gain, ln1_bias, b_qv, b_out, ln2_gain, ln2_bias, b_up, b_down)
    ]
    layers = []
    for l in range(layer_count):
        gain1, bias1, qv, bout, gain2, bias2, bup, bdown = [item[l] for item in vectors]
        layers.append(
            dict(
                ln1_gain=gain1,
                ln1_bias=bias1,
                ln2_gain=gain2,
                ln2_bias=bias2,
                qkv=qkv_all[l],
                out=out_all[l],
                up=up_all[l],
                down=down_all[l],
                b_qkv=jnp.stack([qv[0], jnp.zeros_like(qv[0]), qv[1]])[:, None, :],
                b_out=bout,
                b_up=bup,
                b_down=bdown,
            )
        )
    row = lax.dynamic_index_in_dim(inputs, section, 0, keepdims=False)
    target = lax.dynamic_index_in_dim(out_grad, section, 0, keepdims=False)
    lang = lax.dynamic_index_in_dim(lang_ids, section, 0, keepdims=False)
    matches = lang == jnp.arange(lang_weights.shape[0], dtype=jnp.int32)
    scale = jnp.sum(jnp.where(matches, lang_weights, 0)).astype(jnp.float32) / 64.0

    acts, saved = [], []
    for l in range(layer_count):
        row, kept = layer_forward(row, layers[l], slopes)
        acts.append(row)
        saved.append(kept)
    grads, small, large = [None] * layer_count, [None] * layer_count, [None] * layer_count
    incoming = target.astype(jnp.float32) * scale
    for l in reversed(range(layer_count)):
        grads[l], small[l], large[l] = layer_backward(
            incoming, layers[l], saved[l], slopes
        )
        incoming = grads[l].astype(jnp.bfloat16).astype(jnp.float32)

    def mine(items):
        return jnp.where(section == 0, items[0], items[1])

    def theirs(items):
        return jnp.where(section == 0, items[1], items[0])

    def rows_of(items):
        own, other = mine(items), swapped(theirs(items))
        return jnp.stack([jnp.where(section == r, own, other) for r in range(layer_count)])[None]

    def reduced(name, axis):
        items = [item[name].astype(jnp.bfloat16) for item in large]
        total = mine(items) + swapped(theirs(items))
        return lax.psum_scatter(total, "dp", scatter_dimension=axis, tiled=True).astype(
            jnp.float32
        )[None]

    small_total = mine(small) + swapped(theirs(small))
    small_shards = lax.psum_scatter(small_total, ("tensor", "dp"), scatter_dimension=1, tiled=True)
    return (
        rows_of(acts),
        rows_of([item.astype(jnp.bfloat16) for item in grads]).astype(jnp.float32),
        small_shards[0][None],
        small_shards[1][None],
        jnp.transpose(reduced("qkv", 1), (0, 2, 1, 3)),
        reduced("b_qv", 1),
        reduced("out", 1),
        small_shards[2][None],
        small_shards[3][None],
        small_shards[4][None],
        reduced("up", 0),
        reduced("b_up", 0),
        reduced("down", 1),
        small_shards[5][None],
    )


def solution(mesh):
    return jax.shard_map(
        per_device,
        mesh=mesh,
        in_specs=(
            P("dp", "tensor", None),
            P("dp", "tensor", None),
            P("dp"),
            P(),
            P("section", None),
            P("section", None),
            P("section", "dp", None, "tensor"),
            P("section", None, "tensor"),
            P("section", "tensor", "dp"),
            P("section", None),
            P("section", None),
            P("section", None),
            P("section", "dp", "tensor"),
            P("section", "tensor"),
            P("section", "tensor", "dp"),
            P("section", None),
        ),
        out_specs=(
            P("section", "dp", "tensor", None),
            P("section", "dp", "tensor", None),
            P("section", ("tensor", "dp")),
            P("section", ("tensor", "dp")),
            P("section", "dp", None, "tensor"),
            P("section", None, ("tensor", "dp")),
            P("section", "tensor", "dp"),
            P("section", ("tensor", "dp")),
            P("section", ("tensor", "dp")),
            P("section", ("tensor", "dp")),
            P("section", "dp", "tensor"),
            P("section", ("tensor", "dp")),
            P("section", "tensor", "dp"),
            P("section", ("tensor", "dp")),
        ),
        check_vma=False,
    )
```

```python
import functools

import jax
import jax.numpy as jnp
from jax import lax
from jax.experimental import pallas as pl
from jax.experimental.pallas import tpu as pltpu
from jax.sharding import PartitionSpec as P

HEADS = 16
HEAD = 64
PAIR = 2 * HEAD

EPSILON = 1e-05
GELU_SCALE = 0.7978845608028654

MESH = pl.DeviceIdType.MESH
F32 = jnp.float32
BF16 = jnp.bfloat16
CHUNKS = 2
VMEM_LIMIT = 60 * 1024 * 1024


def rows_at(start, size):
    return pl.ds(pl.multiple_of(start, size), size)


def mm(left, right):
    return lax.dot_general(left, right, (((1,), (0,)), ((), ())), preferred_element_type=F32)


def mm_t(left, right):
    return lax.dot_general(left, right, (((1,), (1,)), ((), ())), preferred_element_type=F32)


class Ring:
    def __init__(self, block):
        self.block = block
        self.chunk = block // CHUNKS
        self.me = lax.axis_index("tensor")
        core, chip = lax.rem(self.me, 2), self.me // 2
        self.mate = self.me + 1 - 2 * core
        self.peer = self.me + 2 - 4 * chip
        self.far = self.peer + 1 - 2 * core

    def greet(self):
        barrier = pltpu.get_barrier_semaphore()
        for other in (self.mate, self.peer):
            pl.semaphore_signal(barrier, inc=1, device_id={"tensor": other}, device_id_type=MESH)
        pl.semaphore_wait(barrier, 2)

    def rows(self, owner, c):
        return rows_at(owner * self.block + c * self.chunk, self.chunk)

    def send(self, src, dst, sems, kind, c, other):
        return pltpu.make_async_remote_copy(
            src_ref=src,
            dst_ref=dst,
            send_sem=sems.at[0, kind, c],
            recv_sem=sems.at[1, kind, c],
            device_id={"tensor": other},
            device_id_type=MESH,
        )


class Gather:
    def __init__(self, ring, every, sems):
        self.ring, self.every, self.sems = ring, every, sems

    def copy(self, kind, owner, c):
        ring = self.ring
        at = self.every.at[ring.rows(owner, c)]
        return ring.send(at, at, self.sems, kind, c, ring.peer if kind == 1 else ring.mate)

    def start(self, c):
        self.copy(1, self.ring.me, c).start()
        self.copy(0, self.ring.me, c).start()

    def arrived_mate(self, c):
        self.copy(0, self.ring.mate, c).wait_recv()

    def arrived_peer(self, c):
        self.copy(1, self.ring.peer, c).wait_recv()
        self.copy(2, self.ring.peer, c).start()

    def arrived_far(self, c):
        self.copy(2, self.ring.far, c).wait_recv()

    def finish(self):
        for c in range(CHUNKS):
            for kind, owner in ((0, self.ring.me), (1, self.ring.me), (2, self.ring.peer)):
                self.copy(kind, owner, c).wait_send()


class Scatter:
    def __init__(self, ring, stage, land, sems):
        self.ring, self.stage, self.land, self.sems = ring, stage, land, sems

    def copy(self, kind, c):
        ring = self.ring
        at = pl.ds(c * ring.chunk, ring.chunk)
        return ring.send(
            self.stage.at[kind, at],
            self.land.at[kind, at],
            self.sems,
            kind,
            c,
            ring.peer if kind == 1 else ring.mate,
        )

    def put(self, kind, c, value):
        self.stage[kind, pl.ds(c * self.ring.chunk, self.ring.chunk)] = value.astype(BF16)
        self.copy(kind, c).start()

    def take(self, kind, c):
        self.copy(kind, c).wait_recv()
        return self.land[kind, pl.ds(c * self.ring.chunk, self.ring.chunk)].astype(F32)

    def to_peer(self, c, far_part, peer_part):
        self.put(0, c, far_part)
        self.put(1, c, peer_part + self.take(0, c))

    def finish(self):
        for kind in range(3):
            for c in range(CHUNKS):
                self.copy(kind, c).wait_send()


def normalize(values):
    center = values - jnp.mean(values, axis=-1, keepdims=True)
    scale = lax.rsqrt(jnp.mean(center * center, axis=-1, keepdims=True) + EPSILON)
    return center * scale, scale


def norm_pull(values, gain, grad):
    unit, scale = normalize(values)
    scaled = grad * gain
    pulled = scale * (
        scaled
        - jnp.mean(scaled, axis=-1, keepdims=True)
        - unit * jnp.mean(scaled * unit, axis=-1, keepdims=True)
    )
    return pulled, jnp.sum(grad * unit, axis=0, keepdims=True), jnp.sum(grad, axis=0, keepdims=True)


def scores_of(keys, queries, slope, penalty_ref, start):
    stop, count = keys.shape[0], queries.shape[0]
    scores = mm_t(keys, queries) + slope * penalty_ref[:stop]
    last = scores[start:]
    allowed = lax.broadcasted_iota(jnp.int32, (count, count), 0) <= lax.broadcasted_iota(
        jnp.int32, (count, count), 1
    )
    last = jnp.where(allowed, last, -1e30)
    return last if start == 0 else jnp.concatenate([scores[:start], last], axis=0)


def head_mask(value, which):
    lane = lax.broadcasted_iota(jnp.int32, value.shape, 1)
    inside = lane < HEAD if which == 0 else lane >= HEAD
    return jnp.where(inside, value, jnp.zeros_like(value))


def fill_penalty(penalty_ref):
    penalty_ref[...] = lax.broadcasted_iota(jnp.int32, penalty_ref.shape, 0).astype(F32)


def nothing():
    pass


def attend_forward(proj, context, totals, slopes, penalty, block, tick=nothing):
    length, width = context.shape
    for pair in range(width // PAIR):
        lanes = pl.ds(pair * PAIR, PAIR)
        for start in range(0, length, block):
            tick()
            stop = start + block
            queries = proj[0, start:stop, lanes] * jnp.asarray(0.125, BF16)
            keys = proj[1, :stop, lanes]
            values_t = proj[2, :stop, lanes].T
            outs = []
            for which in range(2):
                head = pair * 2 + which
                slope = slopes[pl.ds(head, 1), :]
                scores = scores_of(keys, head_mask(queries, which), slope, penalty, start)
                highest = jnp.max(scores, axis=0, keepdims=True)
                grown = jnp.exp(scores - highest)
                total = jnp.sum(grown, axis=0, keepdims=True)
                mixed = mm(values_t[which * HEAD : (which + 1) * HEAD], grown.astype(BF16))
                outs.append(mixed / total)
                totals[pl.ds(head, 1), start:stop] = highest + jnp.log(total)
            context[start:stop, lanes] = jnp.concatenate(outs, axis=0).T.astype(BF16)


def attend_backward(proj, grad_context, totals, slopes, penalty, grad_proj, sums, block):
    length, width = grad_context.shape

    def pair_step(pair, carry):
        lanes = pl.ds(pl.multiple_of(pair * PAIR, PAIR), PAIR)
        for start in range(0, length, block):
            stop = start + block
            queries = proj[0, start:stop, lanes] * jnp.asarray(0.125, BF16)
            keys = proj[1, :stop, lanes]
            keys_t = keys.T
            values = proj[2, :stop, lanes]
            grads = grad_context[start:stop, lanes]
            outs = []
            for which in range(2):
                head = pair * 2 + which
                slope = slopes[pl.ds(head, 1), :]
                one_query = head_mask(queries, which)
                one_grad = head_mask(grads, which)
                scores = scores_of(keys, one_query, slope, penalty, start)
                probs = jnp.exp(scores - totals[pl.ds(head, 1), start:stop])
                pulled = probs * mm_t(values, one_grad)
                inner = jnp.sum(pulled, axis=0, keepdims=True)
                grad_scores = (pulled - probs * inner).astype(BF16)
                outs.append(mm(keys_t[which * HEAD : (which + 1) * HEAD], grad_scores) * 0.125)
                grad_keys = mm(grad_scores, one_query)
                grad_values = mm(probs.astype(BF16), one_grad)
                if which == 0:
                    first_keys, first_values = grad_keys, grad_values
                else:
                    grad_keys, grad_values = grad_keys + first_keys, grad_values + first_values
            grad_proj[0, start:stop, lanes] = jnp.concatenate(outs, axis=0).T.astype(BF16)
            if start > 0:
                sums[0, :start] += grad_keys[:start]
                sums[1, :start] += grad_values[:start]
            sums[0, start:stop] = grad_keys[start:]
            sums[1, start:stop] = grad_values[start:]
        grad_proj[1, :, lanes] = sums[0].astype(BF16)
        grad_proj[2, :, lanes] = sums[1].astype(BF16)
        return carry

    lax.fori_loop(0, width // PAIR, pair_step, 0)


def attention_forward_body(
    ring, gather, scatter, x, gain, shift, w_qkv, b_qkv, w_out, b_out, slopes,
    normed, proj, context, totals, middle, penalty,
    qkv_ready=nothing, out_ready=nothing, tick=nothing,
):
    block, chunk = ring.block, ring.chunk
    for c in range(CHUNKS):
        at = pl.ds(c * chunk, chunk)
        unit, _ = normalize(x[at].astype(F32))
        normed[ring.rows(ring.me, c)] = (unit * gain() + shift()).astype(BF16)
        gather.start(c)
    qkv_ready()

    def project(owner, c, size):
        at = rows_at(owner * block + c * chunk, size)
        rows = normed[at]
        for part in range(3):
            made = mm(rows, w_qkv[part])
            proj[part, at] = (made if part == 1 else made + b_qkv(part)).astype(BF16)

    project(ring.me, 0, block)
    for c in range(CHUNKS):
        gather.arrived_mate(c)
    project(ring.mate, 0, block)
    for c in range(CHUNKS):
        gather.arrived_peer(c)
        project(ring.peer, c, chunk)
        gather.arrived_far(c)
        project(ring.far, c, chunk)
    attend_forward(proj, context, totals, slopes, penalty, block, tick)
    out_ready()

    def part_of(owner, c):
        return mm(context[ring.rows(owner, c)], w_out[...])

    for c in range(CHUNKS):
        scatter.put(0, c, part_of(ring.far, c))
        scatter.put(1, c, part_of(ring.peer, c) + scatter.take(0, c))
    for c in range(CHUNKS):
        scatter.put(2, c, part_of(ring.mate, c))
    for c in range(CHUNKS):
        at = pl.ds(c * chunk, chunk)
        total = part_of(ring.me, c) + scatter.take(2, c) + scatter.take(1, c)
        middle[at] = x[at].astype(F32) + total + b_out()


def mlp_forward_body(
    ring, gather, scatter, middle, gain, shift, w_up, b_up, w_down, b_down,
    second, activated, slope_of, leaving, own,
    ready=nothing, tick=nothing,
):
    block, chunk = ring.block, ring.chunk
    for c in range(CHUNKS):
        at = pl.ds(c * chunk, chunk)
        unit, _ = normalize(middle[at])
        second[ring.rows(ring.me, c)] = (unit * gain() + shift()).astype(BF16)
        gather.start(c)

    def expand(at):
        upward = mm(second[at], w_up[...]) + b_up()
        inner = jnp.tanh(GELU_SCALE * (upward + 0.044715 * upward * upward * upward))
        half = 0.5 * (1.0 + inner)
        value = upward * half
        slope = half + 0.5 * upward * (1.0 - inner * inner) * GELU_SCALE * (
            1.0 + 3 * 0.044715 * upward * upward
        )
        value = value.astype(BF16)
        activated[at] = value
        slope_of[at] = slope.astype(BF16)
        return mm(value, w_down[...])

    ready()
    own[...] = expand(rows_at(ring.me * block, block))
    tick()
    for c in range(CHUNKS):
        gather.arrived_mate(c)
    part = expand(rows_at(ring.mate * block, block))
    for c in range(CHUNKS):
        scatter.put(2, c, part[c * chunk : (c + 1) * chunk])
    tick()
    for c in range(CHUNKS):
        gather.arrived_peer(c)
        peer_part = expand(ring.rows(ring.peer, c))
        gather.arrived_far(c)
        scatter.put(0, c, expand(ring.rows(ring.far, c)))
        scatter.put(1, c, peer_part + scatter.take(0, c))
        tick()
    for c in range(CHUNKS):
        at = pl.ds(c * chunk, chunk)
        total = own[at] + scatter.take(2, c) + scatter.take(1, c)
        leaving[at] = (middle[at] + total + b_down()).astype(BF16)


def attention_forward_kernel(
    x, gain, shift, w_qkv, b_qkv, w_out, b_out, slopes,
    normed, proj, context, totals, middle,
    penalty, stage, land, gather_sems, scatter_sems,
):
    ring = Ring(x.shape[0])
    ring.greet()
    gather = Gather(ring, normed, gather_sems)
    scatter = Scatter(ring, stage, land, scatter_sems)
    fill_penalty(penalty)
    attention_forward_body(
        ring, gather, scatter, x, lambda: gain[...], lambda: shift[...], w_qkv,
        lambda part: b_qkv[part], w_out, lambda: b_out[...], slopes,
        normed, proj, context, totals, middle, penalty,
    )
    gather.finish()
    scatter.finish()


def mlp_forward_kernel(
    middle, gain, shift, w_up, b_up, w_down, b_down,
    second, activated, slope_of, leaving,
    own, stage, land, gather_sems, scatter_sems,
):
    ring = Ring(middle.shape[0])
    ring.greet()
    gather = Gather(ring, second, gather_sems)
    scatter = Scatter(ring, stage, land, scatter_sems)
    mlp_forward_body(
        ring, gather, scatter, middle, lambda: gain[...], lambda: shift[...], w_up,
        lambda: b_up[...], w_down, lambda: b_down[...],
        second, activated, slope_of, leaving, own,
    )
    gather.finish()
    scatter.finish()


def mlp_backward_kernel(
    incoming, middle, gain, w_up, w_down, slope_of,
    down_rows, grad_up, grad_middle, small, up_sum,
    own, stage, land, gather_sems, scatter_sems,
):
    block = middle.shape[0]
    ring = Ring(block)
    ring.greet()
    gather = Gather(ring, down_rows, gather_sems)
    scatter = Scatter(ring, stage, land, scatter_sems)
    chunk = ring.chunk
    for c in range(CHUNKS):
        down_rows[ring.rows(ring.me, c)] = incoming[pl.ds(c * chunk, chunk)].astype(BF16)
        gather.start(c)
    up_sum[...] = jnp.zeros_like(up_sum)

    def pull(at):
        grad = mm_t(down_rows[at], w_down[...]) * slope_of[at].astype(F32)
        grad = grad.astype(BF16)
        grad_up[at] = grad
        up_sum[...] += jnp.sum(grad.astype(F32), axis=0, keepdims=True)
        return mm_t(grad, w_up[...])

    own[...] = pull(rows_at(ring.me * block, block))
    for c in range(CHUNKS):
        gather.arrived_mate(c)
    part = pull(rows_at(ring.mate * block, block))
    for c in range(CHUNKS):
        scatter.put(2, c, part[c * chunk : (c + 1) * chunk])
    for c in range(CHUNKS):
        gather.arrived_peer(c)
        peer_part = pull(ring.rows(ring.peer, c))
        gather.arrived_far(c)
        scatter.put(0, c, pull(ring.rows(ring.far, c)))
        scatter.put(1, c, peer_part + scatter.take(0, c))
    small[...] = jnp.zeros_like(small)
    for c in range(CHUNKS):
        at = pl.ds(c * chunk, chunk)
        total = own[at] + scatter.take(2, c) + scatter.take(1, c)
        pulled, grad_gain, grad_shift = norm_pull(middle[at], gain[...], total)
        before = incoming[at]
        after = before + pulled
        grad_middle[at] = after
        small[0:1] += jnp.sum(after, axis=0, keepdims=True)
        small[1:2] += grad_gain
        small[2:3] += grad_shift
        small[3:4] += jnp.sum(before, axis=0, keepdims=True)
    gather.finish()
    scatter.finish()


def attention_backward_kernel(
    grad_middle, x, gain, w_qkv, w_out, slopes, proj, totals,
    attn_rows, grad_proj, grad_hidden, small, qv_sum,
    grad_context, sums, penalty, stage, land, gather_sems, scatter_sems,
):
    block = x.shape[0]
    ring = Ring(block)
    ring.greet()
    gather = Gather(ring, attn_rows, gather_sems)
    scatter = Scatter(ring, stage, land, scatter_sems)
    chunk = ring.chunk
    for c in range(CHUNKS):
        attn_rows[ring.rows(ring.me, c)] = grad_middle[pl.ds(c * chunk, chunk)].astype(BF16)
        gather.start(c)
    fill_penalty(penalty)

    def pull(at):
        grad_context[at] = mm_t(attn_rows[at], w_out[...]).astype(BF16)

    pull(rows_at(ring.me * block, block))
    for c in range(CHUNKS):
        gather.arrived_mate(c)
    pull(rows_at(ring.mate * block, block))
    for c in range(CHUNKS):
        gather.arrived_peer(c)
        pull(ring.rows(ring.peer, c))
        gather.arrived_far(c)
        pull(ring.rows(ring.far, c))
    attend_backward(proj, grad_context, totals, slopes, penalty, grad_proj, sums, block)
    qv_sum[...] = jnp.zeros_like(qv_sum)
    qv_sum[0:1] = jnp.sum(grad_proj[0].astype(F32), axis=0, keepdims=True)
    qv_sum[1:2] = jnp.sum(grad_proj[2].astype(F32), axis=0, keepdims=True)

    def part_of(owner, c):
        at = ring.rows(owner, c)
        total = mm_t(grad_proj[0, at], w_qkv[0])
        for part in range(1, 3):
            total += mm_t(grad_proj[part, at], w_qkv[part])
        return total

    for c in range(CHUNKS):
        scatter.put(0, c, part_of(ring.far, c))
        scatter.put(1, c, part_of(ring.peer, c) + scatter.take(0, c))
    for c in range(CHUNKS):
        scatter.put(2, c, part_of(ring.mate, c))
    small[...] = jnp.zeros_like(small)
    for c in range(CHUNKS):
        at = pl.ds(c * chunk, chunk)
        total = part_of(ring.me, c) + scatter.take(2, c) + scatter.take(1, c)
        pulled, grad_gain, grad_shift = norm_pull(x[at].astype(F32), gain[...], total)
        grad_hidden[at] = grad_middle[at] + pulled
        small[0:1] += grad_gain
        small[1:2] += grad_shift
    gather.finish()
    scatter.finish()


def call(kernel, name, number, args, outs, scratch):
    vmem = pl.BlockSpec(memory_space=pltpu.VMEM)
    return pl.pallas_call(
        kernel,
        out_shape=[jax.ShapeDtypeStruct(shape, dtype) for shape, dtype in outs],
        in_specs=[vmem] * len(args),
        out_specs=[vmem] * len(outs),
        scratch_shapes=scratch,
        compiler_params=pltpu.CompilerParams(
            collective_id=number, has_side_effects=True, vmem_limit_bytes=VMEM_LIMIT
        ),
        name=name,
    )(*args)


def link_scratch(block, width):
    return [
        pltpu.VMEM((3, block, width), BF16),
        pltpu.VMEM((3, block, width), BF16),
        pltpu.SemaphoreType.DMA((2, 3, CHUNKS)),
        pltpu.SemaphoreType.DMA((2, 3, CHUNKS)),
    ]


def row_vector(value):
    return value.reshape(1, -1)


def layer_forward(x, w, slopes):
    block, width = x.shape
    length = block * lax.axis_size("tensor")
    local = w["out"].shape[0]
    heads = local // HEAD
    normed, proj, context, totals, middle = call(
        attention_forward_kernel,
        "attention_forward",
        1,
        (x, row_vector(w["ln1_gain"]), row_vector(w["ln1_bias"]), w["qkv"], w["b_qkv"], w["out"], row_vector(w["b_out"]), slopes),
        [((length, width), BF16), ((3, length, local), BF16), ((length, local), BF16), ((heads, length), F32), ((block, width), F32)],
        [pltpu.VMEM((length, block), F32)] + link_scratch(block, width),
    )
    units = w["up"].shape[1]
    second, activated, slope_of, leaving = call(
        mlp_forward_kernel,
        "mlp_forward",
        2,
        (middle, row_vector(w["ln2_gain"]), row_vector(w["ln2_bias"]), w["up"], row_vector(w["b_up"]), w["down"], row_vector(w["b_down"])),
        [((length, width), BF16), ((length, units), BF16), ((length, units), BF16), ((block, width), BF16)],
        [pltpu.VMEM((block, width), F32)] + link_scratch(block, width),
    )
    saved = dict(x=x, normed=normed, proj=proj, context=context, totals=totals, middle=middle, second=second, activated=activated, slope_of=slope_of)
    return leaving, saved


def layer_backward(incoming, w, s, slopes):
    block, width = incoming.shape
    length = block * lax.axis_size("tensor")
    local, units = w["out"].shape[0], w["up"].shape[1]
    down_rows, grad_up, grad_middle, small_a, up_sum = call(
        mlp_backward_kernel,
        "mlp_backward",
        3,
        (incoming, s["middle"], row_vector(w["ln2_gain"]), w["up"], w["down"], s["slope_of"]),
        [((length, width), BF16), ((length, units), BF16), ((block, width), F32), ((8, width), F32), ((1, units), F32)],
        [pltpu.VMEM((block, width), F32)] + link_scratch(block, width),
    )
    attn_rows, grad_proj, grad_hidden, small_b, qv_sum = call(
        attention_backward_kernel,
        "attention_backward",
        4,
        (grad_middle, s["x"], row_vector(w["ln1_gain"]), w["qkv"], w["out"], slopes, s["proj"], s["totals"]),
        [((length, width), BF16), ((3, length, local), BF16), ((block, width), F32), ((8, width), F32), ((8, local), F32)],
        [pltpu.VMEM((length, local), BF16), pltpu.VMEM((2, length, PAIR), F32), pltpu.VMEM((length, block), F32)]
        + link_scratch(block, width),
    )
    small = jnp.stack([small_b[0], small_b[1], small_a[0], small_a[1], small_a[2], small_a[3]])
    large = dict(
        qkv=jnp.einsum("td,cth->cdh", s["normed"], grad_proj, preferred_element_type=F32),
        out=jnp.einsum("th,td->hd", s["context"], attn_rows, preferred_element_type=F32),
        up=jnp.einsum("td,tf->df", s["second"], grad_up, preferred_element_type=F32),
        down=jnp.einsum("tf,td->fd", s["activated"], down_rows, preferred_element_type=F32),
        b_qv=qv_sum[:2],
        b_up=up_sum[0],
    )
    return grad_hidden, small, large


class Cross:
    def __init__(self, layer, shards, whole, sems):
        self.layer, self.shards, self.whole = layer, shards, whole
        self.first, self.line, self.last, self.local = sems
        self.section, self.place = lax.axis_index("section"), lax.axis_index("dp")
        self.count = lax.axis_size("dp")
        self.other = 1 - self.section
        self.owner = self.section == layer
        self.half = jnp.where(self.owner, 0, 1)

    def at(self, i, half, place):
        ref = self.whole[i]
        if i == 0:
            rows = self.shards[i].shape[1] // 2
            return ref.at[:, rows_at((place * 2 + half) * rows, rows), :]
        rows = self.shards[i].shape[0] // 2
        if i == 2:
            return ref.at[rows_at((place * 2 + half) * rows, rows), :]
        return ref.at[rows_at(half * rows, rows), rows_at(place * self.shards[i].shape[1], self.shards[i].shape[1])]

    def mine(self, i, half):
        ref = self.shards[i]
        rows = ref.shape[1 if i == 0 else 0] // 2
        return ref.at[:, pl.ds(half * rows, rows), :] if i == 0 else ref.at[pl.ds(half * rows, rows), :]

    def copy(self, src, dst, sems, where, device):
        return pltpu.make_async_remote_copy(
            src_ref=src,
            dst_ref=dst,
            send_sem=sems.at[(0,) + where],
            recv_sem=sems.at[(1,) + where],
            device_id=device,
            device_id_type=MESH,
        )

    def over_first(self, i):
        return self.copy(
            self.mine(i, 1), self.at(i, 1, self.place), self.first, (i,), {"section": self.other}
        )

    def over_last(self, i, place, src=None):
        at = self.at(i, self.half, place)
        return self.copy(at if src is None else src, at, self.last, (i, place), {"section": self.other})

    def from_last(self, i, place):
        at = self.at(i, 1 - self.half, place)
        return self.copy(at, at, self.last, (i, place), {"section": self.other})

    def along(self, i, place, right, src=None):
        at = self.at(i, self.half, place)
        return self.copy(
            at if src is None else src,
            at,
            self.line,
            (i, place, int(right)),
            {"dp": self.place + (1 if right else -1)},
        )

    def onward(self, i, place, right, src=None):
        @pl.when(self.place + 1 < self.count if right else self.place > 0)
        def _():
            self.along(i, place, right, src).start()

    def keep(self, i, half):
        return pltpu.make_async_copy(
            self.mine(i, half), self.at(i, half, self.place), self.local.at[i, half]
        )

    def begin(self, i):
        @pl.when(self.owner)
        def _():
            self.over_first(i).start()

    def start(self, i):
        @pl.when(self.owner)
        def _():
            for right in (True, False):
                self.onward(i, self.place, right, self.mine(i, 0))
            self.over_last(i, self.place, self.mine(i, 0)).start()
            for half in range(2):
                self.keep(i, half).start()

        @pl.when(jnp.logical_not(self.owner))
        def _():
            self.over_first(i).wait_recv()
            for right in (True, False):
                self.onward(i, self.place, right)

    def step(self, i, hops):
        for right in (True, False):
            place = self.place - hops if right else self.place + hops

            @pl.when(place >= 0 if right else place < self.count)
            def _():
                self.along(i, place, right).wait_recv()
                self.over_last(i, place).start()
                self.onward(i, place, right)

    def finish(self, i):
        @pl.when(self.owner)
        def _():
            for half in range(2):
                self.keep(i, half).wait()

        for place in range(self.count):

            @pl.when(jnp.logical_or(jnp.logical_not(self.owner), place != self.place))
            def _():
                self.from_last(i, place).wait_recv()

    def drain(self, i):
        @pl.when(self.owner)
        def _():
            self.over_first(i).wait_send()

        for place in range(self.count):

            @pl.when(jnp.logical_or(self.owner, place != self.place))
            def _():
                self.over_last(i, place).wait_send()

            @pl.when(jnp.logical_and(place <= self.place, self.place + 1 < self.count))
            def _():
                self.along(i, place, True).wait_send()

            @pl.when(jnp.logical_and(place >= self.place, self.place > 0))
            def _():
                self.along(i, place, False).wait_send()


def cross_scratch(layers, count):
    pieces = 4
    return [
        pltpu.SemaphoreType.DMA((layers, 2, pieces)),
        pltpu.SemaphoreType.DMA((layers, 2, pieces, count, 2)),
        pltpu.SemaphoreType.DMA((layers, 2, pieces, count)),
        pltpu.SemaphoreType.DMA((layers, pieces, 2)),
    ]


def greet_all(ring):
    barrier = pltpu.get_barrier_semaphore()
    section, place, count = lax.axis_index("section"), lax.axis_index("dp"), lax.axis_size("dp")
    for device in ({"tensor": ring.mate}, {"tensor": ring.peer}, {"section": 1 - section}):
        pl.semaphore_signal(barrier, inc=1, device_id=device, device_id_type=MESH)

    @pl.when(place > 0)
    def _():
        pl.semaphore_signal(barrier, inc=1, device_id={"dp": place - 1}, device_id_type=MESH)

    @pl.when(place + 1 < count)
    def _():
        pl.semaphore_signal(barrier, inc=1, device_id={"dp": place + 1}, device_id_type=MESH)

    pl.semaphore_wait(barrier, 3 + jnp.where(place > 0, 1, 0) + jnp.where(place + 1 < count, 1, 0))


class Pump:
    def __init__(self, crossings):
        self.pieces = [(crossing, i) for crossing in crossings for i in range(4)]
        self.hops = crossings[0].count
        self.done = 0
        for piece in range(2):
            self.begin(piece)

    def begin(self, piece):
        if piece < len(self.pieces):
            crossing, i = self.pieces[piece]
            crossing.begin(i)

    def stage(self, number):
        self.begin(number + 2)
        for hops in range(self.hops):
            if 0 <= number - hops < len(self.pieces):
                crossing, i = self.pieces[number - hops]
                if hops == 0:
                    crossing.start(i)
                else:
                    crossing.step(i, hops)

    def until(self, number):
        while self.done <= min(number, len(self.pieces) + self.hops - 2):
            self.stage(self.done)
            self.done += 1

    def tick(self):
        self.until(self.done)

    def have(self, piece):
        self.until(piece + self.hops - 1)
        crossing, i = self.pieces[piece]
        crossing.finish(i)

    def drain(self):
        for crossing, i in self.pieces:
            crossing.drain(i)


KEPT = 6
SMALL_ROWS = 8


def forward_kernel(layers, *refs):
    (x, vector, *shards), refs = refs[:6], refs[6:]
    slopes, refs = refs[0], refs[1:]
    outs, refs = [refs[j * 13 : (j + 1) * 13] for j in range(layers)], refs[13 * layers :]
    vectors, refs = refs[0], refs[1:]
    held, refs = [refs[j * 10 : (j + 1) * 10] for j in range(layers)], refs[10 * layers :]
    penalty, own, stage, land, gather_sems, scatter_sems, save_sems, vector_sems = refs[:8]
    cross_sems = refs[8:]
    ring = Ring(x.shape[0])
    section = lax.axis_index("section")
    greet_all(ring)
    crossings = [
        Cross(l, shards, held[l][6:10], [sem.at[l] for sem in cross_sems]) for l in range(layers)
    ]
    pump = Pump(crossings)
    vector_out = pltpu.make_async_remote_copy(
        src_ref=vector,
        dst_ref=vectors.at[section],
        send_sem=vector_sems.at[0],
        recv_sem=vector_sems.at[1],
        device_id={"section": 1 - section},
        device_id_type=MESH,
    )
    vector_in = pltpu.make_async_remote_copy(
        src_ref=vector,
        dst_ref=vectors.at[1 - section],
        send_sem=vector_sems.at[0],
        recv_sem=vector_sems.at[1],
        device_id={"section": 1 - section},
        device_id_type=MESH,
    )
    vector_out.start()
    vectors[section] = vector[...]
    fill_penalty(penalty)
    vector_in.wait_recv()
    saves = []

    def save(l, i, src):
        copy = pltpu.make_async_copy(src, outs[l][i], save_sems.at[l, i])
        copy.start()
        saves.append(copy)

    links = []
    entering = x
    for l in range(layers):
        normed, proj, context, second, activated, slope_of, wq, wo, wu, wd = held[l]
        totals, middle, leaving = outs[l][10:13]

        def row(i):
            return lambda: vectors[l, pl.ds(i, 1), :]

        def qv(part):
            local = context.shape[1]
            return vectors[l, pl.ds(7, 1), pl.ds((part // 2) * local, local)]

        def link(every, phase):
            gather = Gather(ring, every, gather_sems.at[phase])
            scatter = Scatter(ring, stage.at[phase], land.at[phase], scatter_sems.at[phase])
            links.append((gather, scatter))
            return gather, scatter

        def have(i):
            pump.have(l * 4 + i)
            save(l, 6 + i, held[l][6 + i])

        gather, scatter = link(normed, 0)
        attention_forward_body(
            ring, gather, scatter, entering, row(0), row(1), wq, qv, wo, row(2), slopes,
            normed, proj, context, totals, middle, penalty,
            qkv_ready=lambda: have(0), out_ready=lambda: have(1), tick=pump.tick,
        )
        save(l, 0, normed)
        save(l, 1, proj)
        save(l, 2, context)
        gather.finish()
        scatter.finish()
        gather, scatter = link(second, 1)

        def ready():
            have(2)
            have(3)

        mlp_forward_body(
            ring, gather, scatter, middle, row(3), row(4), wu, row(5), wd, row(6),
            second, activated, slope_of, leaving, own,
            ready=ready, tick=pump.tick,
        )
        save(l, 3, second)
        save(l, 4, activated)
        save(l, 5, slope_of)
        gather.finish()
        scatter.finish()
        entering = leaving
    vector_out.wait_send()
    pump.drain()
    for copy in saves:
        copy.wait()


def forward_call(x, vector, shards, slopes):
    layers, places = lax.axis_size("section"), lax.axis_size("dp")
    block, width = x.shape
    length = block * lax.axis_size("tensor")
    sq, so, su, sd = shards
    local, units = so.shape[0], sd.shape[0]
    heads = local // HEAD
    kept = [
        ((length, width), BF16),
        ((3, length, local), BF16),
        ((length, local), BF16),
        ((length, width), BF16),
        ((length, units), BF16),
        ((length, units), BF16),
        ((3, width, local), BF16),
        ((local, width), BF16),
        ((width, units), BF16),
        ((units, width), BF16),
    ]
    near = [((heads, length), F32), ((block, width), F32), ((block, width), BF16)]
    vmem, far = pl.BlockSpec(memory_space=pltpu.VMEM), pl.BlockSpec(memory_space=pl.ANY)
    made = pl.pallas_call(
        functools.partial(forward_kernel, layers),
        out_shape=[jax.ShapeDtypeStruct(shape, dtype) for _ in range(layers) for shape, dtype in kept + near]
        + [jax.ShapeDtypeStruct((layers,) + vector.shape, F32)],
        in_specs=[vmem, vmem] + [far] * 4 + [vmem],
        out_specs=([far] * len(kept) + [vmem] * len(near)) * layers + [vmem],
        scratch_shapes=[pltpu.VMEM(shape, dtype) for _ in range(layers) for shape, dtype in kept]
        + [
            pltpu.VMEM((length, block), F32),
            pltpu.VMEM((block, width), F32),
            pltpu.VMEM((2, 3, block, width), BF16),
            pltpu.VMEM((2, 3, block, width), BF16),
            pltpu.SemaphoreType.DMA((2, 2, 3, CHUNKS)),
            pltpu.SemaphoreType.DMA((2, 2, 3, CHUNKS)),
            pltpu.SemaphoreType.DMA((layers, len(kept))),
            pltpu.SemaphoreType.DMA((2,)),
        ]
        + cross_scratch(layers, places),
        compiler_params=pltpu.CompilerParams(
            collective_id=5, has_side_effects=True, vmem_limit_bytes=VMEM_LIMIT
        ),
        name="forward",
    )(x, vector, sq, so, su, sd, slopes)
    saved, weights = [], []
    entering = x
    vectors = made[-1]
    for l in range(layers):
        normed, proj, context, second, activated, slope_of, wq, wo, wu, wd, totals, middle, leaving = made[13 * l : 13 * l + 13]
        saved.append(dict(x=entering, normed=normed, proj=proj, context=context, totals=totals, middle=middle, second=second, activated=activated, slope_of=slope_of))
        weights.append(dict(qkv=wq, out=wo, up=wu, down=wd, ln1_gain=vectors[l, 0], ln2_gain=vectors[l, 3]))
        entering = leaving
    return [made[13 * l + 12] for l in range(layers)], saved, weights


def swapped(value):
    count = lax.axis_size("section")
    return lax.ppermute(value, "section", [(i, (i + 1) % count) for i in range(count)])


def near_shards(depth, block):
    return depth % 256 == 0 and block % 256 == 0


def gathered_layers(section, layer_count, w_qkv, w_out, w_up, w_down, small_ones):
    def both(value):
        other = swapped(value)
        return [jnp.where(section == l, value, other) for l in range(layer_count)]

    def over_dp(value, axis):
        return both(lax.all_gather(value, "dp", axis=axis, tiled=True))

    qkv_all, up_all = over_dp(jnp.transpose(w_qkv[0], (1, 0, 2)), 1), over_dp(w_up[0], 0)
    out_all, down_all = over_dp(w_out[0], 1), over_dp(w_down[0], 1)
    vectors = [
        both(item[0]) for item in small_ones
    ]
    layers = []
    for l in range(layer_count):
        gain1, bias1, qv, bout, gain2, bias2, bup, bdown = [item[l] for item in vectors]
        layers.append(
            dict(
                ln1_gain=gain1,
                ln1_bias=bias1,
                ln2_gain=gain2,
                ln2_bias=bias2,
                qkv=qkv_all[l],
                out=out_all[l],
                up=up_all[l],
                down=down_all[l],
                b_qkv=jnp.stack([qv[0], jnp.zeros_like(qv[0]), qv[1]])[:, None, :],
                b_out=bout,
                b_up=bup,
                b_down=bdown,
            )
        )
    return layers


def per_device(
    inputs,
    out_grad,
    lang_ids,
    lang_weights,
    ln1_gain,
    ln1_bias,
    w_qkv,
    b_qv,
    w_out,
    b_out,
    ln2_gain,
    ln2_bias,
    w_up,
    b_up,
    w_down,
    b_down,
):
    section = lax.axis_index("section")
    layer_count = lax.axis_size("section")
    local_heads = w_qkv.shape[3] // HEAD
    head_ids = lax.axis_index("tensor") * local_heads + jnp.arange(local_heads, dtype=jnp.int32)
    slopes = jnp.exp2(-8.0 * (head_ids.astype(jnp.float32) + 1.0) / HEADS)
    slopes = jnp.broadcast_to(slopes[:, None], (local_heads, inputs.shape[1]))

    row = lax.dynamic_index_in_dim(inputs, section, 0, keepdims=False)
    target = lax.dynamic_index_in_dim(out_grad, section, 0, keepdims=False)
    lang = lax.dynamic_index_in_dim(lang_ids, section, 0, keepdims=False)
    matches = lang == jnp.arange(lang_weights.shape[0], dtype=jnp.int32)
    scale = jnp.sum(jnp.where(matches, lang_weights, 0)).astype(jnp.float32) / 64.0

    if near_shards(w_qkv[0].shape[0], inputs.shape[1]):
        vector = jnp.stack(
            [item[0] for item in (ln1_gain, ln1_bias, b_out, ln2_gain, ln2_bias)]
            + [b_up[0], b_down[0], jnp.pad(b_qv[0].reshape(-1), (0, b_out.shape[1] - 2 * b_qv.shape[2]))]
        )
        shards = (jnp.transpose(w_qkv[0], (1, 0, 2)), w_out[0], w_up[0], w_down[0])
        acts, saved, layers = forward_call(row, vector, shards, slopes)
    else:
        layers = gathered_layers(
            section, layer_count, w_qkv, w_out, w_up, w_down,
            (ln1_gain, ln1_bias, b_qv, b_out, ln2_gain, ln2_bias, b_up, b_down),
        )
        acts, saved = [], []
        for l in range(layer_count):
            row, kept = layer_forward(row, layers[l], slopes)
            acts.append(row)
            saved.append(kept)
    grads, small, large = [None] * layer_count, [None] * layer_count, [None] * layer_count
    incoming = target.astype(jnp.float32) * scale
    for l in reversed(range(layer_count)):
        grads[l], small[l], large[l] = layer_backward(
            incoming, layers[l], saved[l], slopes
        )
        incoming = grads[l].astype(jnp.bfloat16).astype(jnp.float32)

    def mine(items):
        return jnp.where(section == 0, items[0], items[1])

    def theirs(items):
        return jnp.where(section == 0, items[1], items[0])

    def rows_of(items):
        own, other = mine(items), swapped(theirs(items))
        return jnp.stack([jnp.where(section == r, own, other) for r in range(layer_count)])[None]

    def reduced(name, axis):
        items = [item[name].astype(jnp.bfloat16) for item in large]
        total = mine(items) + swapped(theirs(items))
        return lax.psum_scatter(total, "dp", scatter_dimension=axis, tiled=True).astype(
            jnp.float32
        )[None]

    small_total = mine(small) + swapped(theirs(small))
    small_shards = lax.psum_scatter(small_total, ("tensor", "dp"), scatter_dimension=1, tiled=True)
    return (
        rows_of(acts),
        rows_of([item.astype(jnp.bfloat16) for item in grads]).astype(jnp.float32),
        small_shards[0][None],
        small_shards[1][None],
        jnp.transpose(reduced("qkv", 1), (0, 2, 1, 3)),
        reduced("b_qv", 1),
        reduced("out", 1),
        small_shards[2][None],
        small_shards[3][None],
        small_shards[4][None],
        reduced("up", 0),
        reduced("b_up", 0),
        reduced("down", 1),
        small_shards[5][None],
    )


def solution(mesh):
    return jax.shard_map(
        per_device,
        mesh=mesh,
        in_specs=(
            P("dp", "tensor", None),
            P("dp", "tensor", None),
            P("dp"),
            P(),
            P("section", None),
            P("section", None),
            P("section", "dp", None, "tensor"),
            P("section", None, "tensor"),
            P("section", "tensor", "dp"),
            P("section", None),
            P("section", None),
            P("section", None),
            P("section", "dp", "tensor"),
            P("section", "tensor"),
            P("section", "tensor", "dp"),
            P("section", None),
        ),
        out_specs=(
            P("section", "dp", "tensor", None),
            P("section", "dp", "tensor", None),
            P("section", ("tensor", "dp")),
            P("section", ("tensor", "dp")),
            P("section", "dp", None, "tensor"),
            P("section", None, ("tensor", "dp")),
            P("section", "tensor", "dp"),
            P("section", ("tensor", "dp")),
            P("section", ("tensor", "dp")),
            P("section", ("tensor", "dp")),
            P("section", "dp", "tensor"),
            P("section", ("tensor", "dp")),
            P("section", "tensor", "dp"),
            P("section", ("tensor", "dp")),
        ),
        check_vma=False,
    )
```

```python
import functools

import jax
import jax.numpy as jnp
from jax import lax
from jax.experimental import pallas as pl
from jax.experimental.pallas import tpu as pltpu
from jax.sharding import PartitionSpec as P

HEADS = 16
HEAD = 64
PAIR = 2 * HEAD

EPSILON = 1e-05
GELU_SCALE = 0.7978845608028654

SECTION, TENSOR, DP = "section", "tensor", "dp"
MESH = pl.DeviceIdType.MESH
F32 = jnp.float32
BF16 = jnp.bfloat16
CHUNKS = 2
LANES = 128
VMEM_LIMIT = 61 * 1024 * 1024


def rows_at(start, size):
    return pl.ds(pl.multiple_of(start, size), size)


def mm(left, right):
    return lax.dot_general(left, right, (((1,), (0,)), ((), ())), preferred_element_type=F32)


def mm_t(left, right):
    return lax.dot_general(left, right, (((1,), (1,)), ((), ())), preferred_element_type=F32)


class Ring:
    def __init__(self, block):
        self.block = block
        self.chunk = block // CHUNKS
        self.me = lax.axis_index(TENSOR)
        core, chip = lax.rem(self.me, 2), self.me // 2
        self.mate = self.me + 1 - 2 * core
        self.peer = self.me + 2 - 4 * chip
        self.far = self.peer + 1 - 2 * core

    def greet(self):
        barrier = pltpu.get_barrier_semaphore()
        for other in (self.mate, self.peer):
            pl.semaphore_signal(barrier, inc=1, device_id={TENSOR: other}, device_id_type=MESH)
        pl.semaphore_wait(barrier, 2)

    def rows(self, owner, c):
        return rows_at(owner * self.block + c * self.chunk, self.chunk)

    def send(self, src, dst, sems, kind, c, other):
        return pltpu.make_async_remote_copy(
            src_ref=src,
            dst_ref=dst,
            send_sem=sems.at[0, kind, c],
            recv_sem=sems.at[1, kind, c],
            device_id={TENSOR: other},
            device_id_type=MESH,
        )


class Gather:
    def __init__(self, ring, every, sems):
        self.ring, self.every, self.sems = ring, every, sems

    def copy(self, kind, owner, c):
        ring = self.ring
        at = self.every.at[ring.rows(owner, c)]
        return ring.send(at, at, self.sems, kind, c, ring.peer if kind == 1 else ring.mate)

    def start(self, c):
        self.copy(1, self.ring.me, c).start()
        self.copy(0, self.ring.me, c).start()

    def arrived_mate(self, c):
        self.copy(0, self.ring.mate, c).wait_recv()

    def arrived_peer(self, c):
        self.copy(1, self.ring.peer, c).wait_recv()
        self.copy(2, self.ring.peer, c).start()

    def arrived_far(self, c):
        self.copy(2, self.ring.far, c).wait_recv()

    def finish(self):
        for c in range(CHUNKS):
            for kind, owner in ((0, self.ring.me), (1, self.ring.me), (2, self.ring.peer)):
                self.copy(kind, owner, c).wait_send()


class Scatter:
    def __init__(self, ring, stage, land, sems):
        self.ring, self.stage, self.land, self.sems = ring, stage, land, sems

    def copy(self, kind, c):
        ring = self.ring
        at = pl.ds(c * ring.chunk, ring.chunk)
        return ring.send(
            self.stage.at[kind, at],
            self.land.at[kind, at],
            self.sems,
            kind,
            c,
            ring.peer if kind == 1 else ring.mate,
        )

    def put(self, kind, c, value):
        self.stage[kind, pl.ds(c * self.ring.chunk, self.ring.chunk)] = value.astype(BF16)
        self.copy(kind, c).start()

    def take(self, kind, c):
        self.copy(kind, c).wait_recv()
        return self.land[kind, pl.ds(c * self.ring.chunk, self.ring.chunk)].astype(F32)

    def to_peer(self, c, far_part, peer_part):
        self.put(0, c, far_part)
        self.put(1, c, peer_part + self.take(0, c))

    def finish(self):
        for kind in range(3):
            for c in range(CHUNKS):
                self.copy(kind, c).wait_send()


def normalize(values):
    center = values - jnp.mean(values, axis=-1, keepdims=True)
    scale = lax.rsqrt(jnp.mean(center * center, axis=-1, keepdims=True) + EPSILON)
    return center * scale, scale


def norm_pull(values, gain, grad):
    unit, scale = normalize(values)
    scaled = grad * gain
    pulled = scale * (
        scaled
        - jnp.mean(scaled, axis=-1, keepdims=True)
        - unit * jnp.mean(scaled * unit, axis=-1, keepdims=True)
    )
    return pulled, jnp.sum(grad * unit, axis=0, keepdims=True), jnp.sum(grad, axis=0, keepdims=True)


def scores_of(keys, queries, slope, penalty_ref, start):
    stop, count = keys.shape[0], queries.shape[0]
    scores = mm_t(keys, queries) + slope * jnp.concatenate([penalty_ref[:stop]] * (count // LANES), axis=1)
    last = scores[start:]
    allowed = lax.broadcasted_iota(jnp.int32, (count, count), 0) <= lax.broadcasted_iota(
        jnp.int32, (count, count), 1
    )
    last = jnp.where(allowed, last, -1e30)
    return last if start == 0 else jnp.concatenate([scores[:start], last], axis=0)


def head_mask(value, which):
    lane = lax.broadcasted_iota(jnp.int32, value.shape, 1)
    inside = lane < HEAD if which == 0 else lane >= HEAD
    return jnp.where(inside, value, jnp.zeros_like(value))


def fill_penalty(penalty_ref):
    penalty_ref[...] = lax.broadcasted_iota(jnp.int32, penalty_ref.shape, 0).astype(F32)


def nothing(point=0):
    pass


def attend_forward(proj, context, totals, slopes, penalty, block, tick=nothing):
    length, width = context.shape
    for pair in range(width // PAIR):
        lanes = pl.ds(pair * PAIR, PAIR)
        for start in range(0, length, block):
            tick(pair * 4 + start // block)
            stop = start + block
            queries = proj[0, start:stop, lanes] * jnp.asarray(0.125, BF16)
            keys = proj[1, :stop, lanes]
            values_t = proj[2, :stop, lanes].T
            outs = []
            for which in range(2):
                head = pair * 2 + which
                slope = slopes[pl.ds(head, 1), :]
                scores = scores_of(keys, head_mask(queries, which), slope, penalty, start)
                highest = jnp.max(scores, axis=0, keepdims=True)
                grown = jnp.exp(scores - highest)
                total = jnp.sum(grown, axis=0, keepdims=True)
                mixed = mm(values_t[which * HEAD : (which + 1) * HEAD], grown.astype(BF16))
                outs.append(mixed / total)
                totals[pl.ds(head, 1), start:stop] = highest + jnp.log(total)
            context[start:stop, lanes] = jnp.concatenate(outs, axis=0).T.astype(BF16)


def attend_backward(proj, grad_context, totals, slopes, penalty, grad_proj, sums, block, tick=nothing):
    length, width = grad_context.shape
    for pair in range(width // PAIR):
        lanes = pl.ds(pair * PAIR, PAIR)
        for start in range(0, length, block):
            tick()
            stop = start + block
            queries = proj[0, start:stop, lanes] * jnp.asarray(0.125, BF16)
            keys = proj[1, :stop, lanes]
            keys_t = keys.T
            values = proj[2, :stop, lanes]
            grads = grad_context[start:stop, lanes]
            outs = []
            for which in range(2):
                head = pair * 2 + which
                slope = slopes[pl.ds(head, 1), :]
                one_query = head_mask(queries, which)
                one_grad = head_mask(grads, which)
                scores = scores_of(keys, one_query, slope, penalty, start)
                probs = jnp.exp(scores - totals[pl.ds(head, 1), start:stop])
                pulled = probs * mm_t(values, one_grad)
                inner = jnp.sum(pulled, axis=0, keepdims=True)
                grad_scores = (pulled - probs * inner).astype(BF16)
                outs.append(mm(keys_t[which * HEAD : (which + 1) * HEAD], grad_scores) * 0.125)
                grad_keys = mm(grad_scores, one_query)
                grad_values = mm(probs.astype(BF16), one_grad)
                if which == 0:
                    first_keys, first_values = grad_keys, grad_values
                else:
                    grad_keys, grad_values = grad_keys + first_keys, grad_values + first_values
            grad_proj[0, start:stop, lanes] = jnp.concatenate(outs, axis=0).T.astype(BF16)
            if start > 0:
                sums[0, :start] += grad_keys[:start]
                sums[1, :start] += grad_values[:start]
            sums[0, start:stop] = grad_keys[start:]
            sums[1, start:stop] = grad_values[start:]
        grad_proj[1, :, lanes] = sums[0].astype(BF16)
        grad_proj[2, :, lanes] = sums[1].astype(BF16)


def attention_forward_body(
    ring, gather, scatter, x, gain, shift, w_qkv, b_qkv, w_out, b_out, slopes,
    normed, proj, context, totals, middle, penalty,
    qkv_ready=nothing, out_ready=nothing, tick=nothing,
):
    block, chunk = ring.block, ring.chunk
    for c in range(CHUNKS):
        at = pl.ds(c * chunk, chunk)
        unit, _ = normalize(x[at].astype(F32))
        normed[ring.rows(ring.me, c)] = (unit * gain() + shift()).astype(BF16)
        gather.start(c)
    qkv_ready()

    def project(owner, c, size):
        at = rows_at(owner * block + c * chunk, size)
        rows = normed[at]
        for part in range(3):
            made = mm(rows, w_qkv[part])
            proj[part, at] = (made if part == 1 else made + b_qkv(part)).astype(BF16)

    project(ring.me, 0, block)
    for c in range(CHUNKS):
        gather.arrived_mate(c)
    project(ring.mate, 0, block)
    for c in range(CHUNKS):
        gather.arrived_peer(c)
        project(ring.peer, c, chunk)
        gather.arrived_far(c)
        project(ring.far, c, chunk)
    attend_forward(proj, context, totals, slopes, penalty, block, tick)
    out_ready()

    def part_of(owner, c):
        return mm(context[ring.rows(owner, c)], w_out[...])

    for c in range(CHUNKS):
        scatter.put(0, c, part_of(ring.far, c))
        scatter.put(1, c, part_of(ring.peer, c) + scatter.take(0, c))
        tick(8 + c)
    for c in range(CHUNKS):
        scatter.put(2, c, part_of(ring.mate, c))
    tick(10)
    for c in range(CHUNKS):
        at = pl.ds(c * chunk, chunk)
        total = part_of(ring.me, c) + scatter.take(2, c) + scatter.take(1, c)
        middle[at] = x[at].astype(F32) + total + b_out()


def mlp_forward_body(
    ring, gather, scatter, middle, gain, shift, w_up, b_up, w_down, b_down,
    second, activated, slope_of, leaving, own,
    ready=nothing, tick=nothing,
):
    block, chunk = ring.block, ring.chunk
    for c in range(CHUNKS):
        at = pl.ds(c * chunk, chunk)
        unit, _ = normalize(middle[at])
        second[ring.rows(ring.me, c)] = (unit * gain() + shift()).astype(BF16)
        gather.start(c)

    def expand(at):
        upward = mm(second[at], w_up[...]) + b_up()
        inner = jnp.tanh(GELU_SCALE * (upward + 0.044715 * upward * upward * upward))
        half = 0.5 * (1.0 + inner)
        value = upward * half
        slope = half + 0.5 * upward * (1.0 - inner * inner) * GELU_SCALE * (
            1.0 + 3 * 0.044715 * upward * upward
        )
        value = value.astype(BF16)
        activated[at] = value
        slope_of[at] = slope.astype(BF16)
        return mm(value, w_down[...])

    tick(11)
    ready()
    own[...] = expand(rows_at(ring.me * block, block))
    tick(12)
    for c in range(CHUNKS):
        gather.arrived_mate(c)
    part = expand(rows_at(ring.mate * block, block))
    for c in range(CHUNKS):
        scatter.put(2, c, part[c * chunk : (c + 1) * chunk])
    tick(13)
    for c in range(CHUNKS):
        gather.arrived_peer(c)
        peer_part = expand(ring.rows(ring.peer, c))
        gather.arrived_far(c)
        scatter.put(0, c, expand(ring.rows(ring.far, c)))
        scatter.put(1, c, peer_part + scatter.take(0, c))
        tick(14 + c)
    for c in range(CHUNKS):
        at = pl.ds(c * chunk, chunk)
        total = own[at] + scatter.take(2, c) + scatter.take(1, c)
        leaving[at] = (middle[at] + total + b_down()).astype(BF16)


def attention_forward_kernel(
    x, gain, shift, w_qkv, b_qkv, w_out, b_out, slopes,
    normed, proj, context, totals, middle,
    penalty, stage, land, gather_sems, scatter_sems,
):
    ring = Ring(x.shape[0])
    ring.greet()
    gather = Gather(ring, normed, gather_sems)
    scatter = Scatter(ring, stage, land, scatter_sems)
    fill_penalty(penalty)
    attention_forward_body(
        ring, gather, scatter, x, lambda: gain[...], lambda: shift[...], w_qkv,
        lambda part: b_qkv[part], w_out, lambda: b_out[...], slopes,
        normed, proj, context, totals, middle, penalty,
    )
    gather.finish()
    scatter.finish()


def mlp_forward_kernel(
    middle, gain, shift, w_up, b_up, w_down, b_down,
    second, activated, slope_of, leaving,
    own, stage, land, gather_sems, scatter_sems,
):
    ring = Ring(middle.shape[0])
    ring.greet()
    gather = Gather(ring, second, gather_sems)
    scatter = Scatter(ring, stage, land, scatter_sems)
    mlp_forward_body(
        ring, gather, scatter, middle, lambda: gain[...], lambda: shift[...], w_up,
        lambda: b_up[...], w_down, lambda: b_down[...],
        second, activated, slope_of, leaving, own,
    )
    gather.finish()
    scatter.finish()


def mlp_backward_body(
    ring, gather, scatter, incoming, middle, gain, w_up, w_down, slope_of,
    down_rows, grad_up, grad_middle, small, up_sum, own,
    ready=nothing, made=nothing, tick=nothing,
):
    block, chunk = ring.block, ring.chunk
    for c in range(CHUNKS):
        down_rows[ring.rows(ring.me, c)] = incoming[pl.ds(c * chunk, chunk)].astype(BF16)
        gather.start(c)
    ready()

    def pull(at):
        grad = mm_t(down_rows[at], w_down[...]) * slope_of[at].astype(F32)
        grad = grad.astype(BF16)
        grad_up[at] = grad
        up_sum(jnp.sum(grad.astype(F32), axis=0, keepdims=True))
        return mm_t(grad, w_up[...])

    own[...] = pull(rows_at(ring.me * block, block))
    tick()
    for c in range(CHUNKS):
        gather.arrived_mate(c)
    part = pull(rows_at(ring.mate * block, block))
    for c in range(CHUNKS):
        scatter.put(2, c, part[c * chunk : (c + 1) * chunk])
    tick()
    for c in range(CHUNKS):
        gather.arrived_peer(c)
        peer_part = pull(ring.rows(ring.peer, c))
        gather.arrived_far(c)
        scatter.put(0, c, pull(ring.rows(ring.far, c)))
        scatter.put(1, c, peer_part + scatter.take(0, c))
    made()
    for c in range(CHUNKS):
        at = pl.ds(c * chunk, chunk)
        total = own[at] + scatter.take(2, c) + scatter.take(1, c)
        pulled, grad_gain, grad_shift = norm_pull(middle[at], gain(), total)
        before = incoming[at].astype(F32)
        after = before + pulled
        grad_middle[at] = after
        small(2, jnp.sum(after, axis=0, keepdims=True))
        small(3, grad_gain)
        small(4, grad_shift)
        small(5, jnp.sum(before, axis=0, keepdims=True))


def attention_backward_body(
    ring, gather, scatter, grad_middle, x, gain, w_qkv, w_out, slopes, proj, totals,
    attn_rows, grad_proj, grad_hidden, small, grad_context, sums, penalty,
    out_ready=nothing, ready=nothing, gathered=nothing, made=nothing, tick=nothing,
):
    block, chunk = ring.block, ring.chunk
    for c in range(CHUNKS):
        attn_rows[ring.rows(ring.me, c)] = grad_middle[pl.ds(c * chunk, chunk)].astype(BF16)
        gather.start(c)
    out_ready()

    def pull(at):
        grad_context[at] = mm_t(attn_rows[at], w_out[...]).astype(BF16)

    pull(rows_at(ring.me * block, block))
    for c in range(CHUNKS):
        gather.arrived_mate(c)
    pull(rows_at(ring.mate * block, block))
    tick()
    for c in range(CHUNKS):
        gather.arrived_peer(c)
        pull(ring.rows(ring.peer, c))
        gather.arrived_far(c)
        pull(ring.rows(ring.far, c))
        tick()
    gathered()
    ready()
    attend_backward(proj, grad_context, totals, slopes, penalty, grad_proj, sums, block, tick)

    def part_of(owner, c):
        at = ring.rows(owner, c)
        total = mm_t(grad_proj[0, at], w_qkv[0])
        for part in range(1, 3):
            total += mm_t(grad_proj[part, at], w_qkv[part])
        return total

    for c in range(CHUNKS):
        scatter.put(0, c, part_of(ring.far, c))
        scatter.put(1, c, part_of(ring.peer, c) + scatter.take(0, c))
    for c in range(CHUNKS):
        scatter.put(2, c, part_of(ring.mate, c))
    made()
    for c in range(CHUNKS):
        at = pl.ds(c * chunk, chunk)
        total = part_of(ring.me, c) + scatter.take(2, c) + scatter.take(1, c)
        pulled, grad_gain, grad_shift = norm_pull(x[at].astype(F32), gain(), total)
        grad_hidden[at] = grad_middle[at] + pulled
        small(0, grad_gain)
        small(1, grad_shift)


def mlp_backward_kernel(
    incoming, middle, gain, w_up, w_down, slope_of,
    down_rows, grad_up, grad_middle, small, up_sum,
    own, stage, land, gather_sems, scatter_sems,
):
    ring = Ring(middle.shape[0])
    ring.greet()
    gather = Gather(ring, down_rows, gather_sems)
    scatter = Scatter(ring, stage, land, scatter_sems)
    small[...] = jnp.zeros_like(small)
    up_sum[...] = jnp.zeros_like(up_sum)

    def add_small(i, value):
        small[pl.ds(i, 1)] += value

    def add_up(value):
        up_sum[...] += value

    mlp_backward_body(
        ring, gather, scatter, incoming, middle, lambda: gain[...], w_up, w_down, slope_of,
        down_rows, grad_up, grad_middle, add_small, add_up, own,
    )
    gather.finish()
    scatter.finish()


def attention_backward_kernel(
    grad_middle, x, gain, w_qkv, w_out, slopes, proj, totals,
    attn_rows, grad_proj, grad_hidden, small, qv_sum,
    grad_context, sums, penalty, stage, land, gather_sems, scatter_sems,
):
    ring = Ring(x.shape[0])
    ring.greet()
    gather = Gather(ring, attn_rows, gather_sems)
    scatter = Scatter(ring, stage, land, scatter_sems)
    fill_penalty(penalty)
    small[...] = jnp.zeros_like(small)

    def add_small(i, value):
        small[pl.ds(i, 1)] += value

    attention_backward_body(
        ring, gather, scatter, grad_middle, x, lambda: gain[...], w_qkv, w_out, slopes, proj,
        totals, attn_rows, grad_proj, grad_hidden, add_small, grad_context, sums, penalty,
    )
    qv_sum[...] = jnp.zeros_like(qv_sum)
    qv_sum[0:1] = jnp.sum(grad_proj[0].astype(F32), axis=0, keepdims=True)
    qv_sum[1:2] = jnp.sum(grad_proj[2].astype(F32), axis=0, keepdims=True)
    gather.finish()
    scatter.finish()


def call(kernel, name, number, args, outs, scratch):
    vmem = pl.BlockSpec(memory_space=pltpu.VMEM)
    return pl.pallas_call(
        kernel,
        out_shape=[jax.ShapeDtypeStruct(shape, dtype) for shape, dtype in outs],
        in_specs=[vmem] * len(args),
        out_specs=[vmem] * len(outs),
        scratch_shapes=scratch,
        compiler_params=pltpu.CompilerParams(
            collective_id=number, has_side_effects=True, vmem_limit_bytes=VMEM_LIMIT
        ),
        name=name,
    )(*args)


def link_scratch(block, width):
    return [
        pltpu.VMEM((3, block, width), BF16),
        pltpu.VMEM((3, block, width), BF16),
        pltpu.SemaphoreType.DMA((2, 3, CHUNKS)),
        pltpu.SemaphoreType.DMA((2, 3, CHUNKS)),
    ]


def row_vector(value):
    return value.reshape(1, -1)


def layer_forward(x, w, slopes):
    block, width = x.shape
    length = block * lax.axis_size(TENSOR)
    local = w["out"].shape[0]
    heads = local // HEAD
    normed, proj, context, totals, middle = call(
        attention_forward_kernel,
        "attention_forward",
        1,
        (x, row_vector(w["ln1_gain"]), row_vector(w["ln1_bias"]), w["qkv"], w["b_qkv"], w["out"], row_vector(w["b_out"]), slopes),
        [((length, width), BF16), ((3, length, local), BF16), ((length, local), BF16), ((heads, length), F32), ((block, width), F32)],
        [pltpu.VMEM((length, LANES), F32)] + link_scratch(block, width),
    )
    units = w["up"].shape[1]
    second, activated, slope_of, leaving = call(
        mlp_forward_kernel,
        "mlp_forward",
        2,
        (middle, row_vector(w["ln2_gain"]), row_vector(w["ln2_bias"]), w["up"], row_vector(w["b_up"]), w["down"], row_vector(w["b_down"])),
        [((length, width), BF16), ((length, units), BF16), ((length, units), BF16), ((block, width), BF16)],
        [pltpu.VMEM((block, width), F32)] + link_scratch(block, width),
    )
    saved = dict(x=x, normed=normed, proj=proj, context=context, totals=totals, middle=middle, second=second, activated=activated, slope_of=slope_of)
    return leaving, saved


def layer_backward(incoming, w, s, slopes):
    block, width = incoming.shape
    length = block * lax.axis_size(TENSOR)
    local, units = w["out"].shape[0], w["up"].shape[1]
    down_rows, grad_up, grad_middle, small_a, up_sum = call(
        mlp_backward_kernel,
        "mlp_backward",
        3,
        (incoming, s["middle"], row_vector(w["ln2_gain"]), w["up"], w["down"], s["slope_of"]),
        [((length, width), BF16), ((length, units), BF16), ((block, width), F32), ((8, width), F32), ((1, units), F32)],
        [pltpu.VMEM((block, width), F32)] + link_scratch(block, width),
    )
    attn_rows, grad_proj, grad_hidden, small_b, qv_sum = call(
        attention_backward_kernel,
        "attention_backward",
        4,
        (grad_middle, s["x"], row_vector(w["ln1_gain"]), w["qkv"], w["out"], slopes, s["proj"], s["totals"]),
        [((length, width), BF16), ((3, length, local), BF16), ((block, width), F32), ((8, width), F32), ((8, local), F32)],
        [pltpu.VMEM((length, local), BF16), pltpu.VMEM((2, length, PAIR), F32), pltpu.VMEM((length, LANES), F32)]
        + link_scratch(block, width),
    )
    small = jnp.concatenate([small_b[:2], small_a[2:6]])
    large = dict(
        qkv=jnp.einsum("td,cth->cdh", s["normed"], grad_proj, preferred_element_type=F32),
        out=jnp.einsum("th,td->hd", s["context"], attn_rows, preferred_element_type=F32),
        up=jnp.einsum("td,tf->df", s["second"], grad_up, preferred_element_type=F32),
        down=jnp.einsum("tf,td->fd", s["activated"], down_rows, preferred_element_type=F32),
        b_qv=qv_sum[:2],
        b_up=up_sum[0],
    )
    return grad_hidden, small, large


class Cross:
    def __init__(self, layer, shards, whole, sems):
        self.layer, self.shards, self.whole = layer, shards, whole
        self.first, self.line, self.last, self.local = sems
        self.section, self.place = lax.axis_index(SECTION), lax.axis_index(DP)
        self.count = lax.axis_size(DP)
        self.other = 1 - self.section
        self.owner = self.section == layer
        self.half = jnp.where(self.owner, 0, 1)

    def at(self, i, half, place):
        ref = self.whole[i]
        if i == 0:
            rows = self.shards[i].shape[1] // 2
            return ref.at[:, rows_at((place * 2 + half) * rows, rows), :]
        rows = self.shards[i].shape[0] // 2
        if i == 2:
            return ref.at[rows_at((place * 2 + half) * rows, rows), :]
        return ref.at[rows_at(half * rows, rows), rows_at(place * self.shards[i].shape[1], self.shards[i].shape[1])]

    def mine(self, i, half):
        ref = self.shards[i]
        rows = ref.shape[1 if i == 0 else 0] // 2
        return ref.at[:, pl.ds(half * rows, rows), :] if i == 0 else ref.at[pl.ds(half * rows, rows), :]

    def copy(self, src, dst, sems, where, device):
        return pltpu.make_async_remote_copy(
            src_ref=src,
            dst_ref=dst,
            send_sem=sems.at[(0,) + where],
            recv_sem=sems.at[(1,) + where],
            device_id=device,
            device_id_type=MESH,
        )

    def over_first(self, i):
        return self.copy(
            self.mine(i, 1), self.at(i, 1, self.place), self.first, (i,), {SECTION: self.other}
        )

    def over_last(self, i, place, src=None):
        at = self.at(i, self.half, place)
        return self.copy(at if src is None else src, at, self.last, (i, place), {SECTION: self.other})

    def from_last(self, i, place):
        at = self.at(i, 1 - self.half, place)
        return self.copy(at, at, self.last, (i, place), {SECTION: self.other})

    def along(self, i, place, right, src=None):
        at = self.at(i, self.half, place)
        return self.copy(
            at if src is None else src,
            at,
            self.line,
            (i, place, int(right)),
            {DP: self.place + (1 if right else -1)},
        )

    def onward(self, i, place, right, src=None):
        @pl.when(self.place + 1 < self.count if right else self.place > 0)
        def _():
            self.along(i, place, right, src).start()

    def keep(self, i, half):
        return pltpu.make_async_copy(
            self.mine(i, half), self.at(i, half, self.place), self.local.at[i, half]
        )

    def begin(self, i):
        @pl.when(self.owner)
        def _():
            self.over_first(i).start()
            for right in (True, False):
                self.onward(i, self.place, right, self.mine(i, 0))
            self.over_last(i, self.place, self.mine(i, 0)).start()
            for half in range(2):
                self.keep(i, half).start()

    def start(self, i):
        @pl.when(jnp.logical_not(self.owner))
        def _():
            self.over_first(i).wait_recv()
            for right in (True, False):
                self.onward(i, self.place, right)

    def step(self, i, hops):
        for right in (True, False):
            place = self.place - hops if right else self.place + hops

            @pl.when(place >= 0 if right else place < self.count)
            def _():
                self.along(i, place, right).wait_recv()
                self.over_last(i, place).start()
                self.onward(i, place, right)

    def finish(self, i):
        @pl.when(self.owner)
        def _():
            for half in range(2):
                self.keep(i, half).wait()

        for place in range(self.count):

            @pl.when(jnp.logical_or(jnp.logical_not(self.owner), place != self.place))
            def _():
                self.from_last(i, place).wait_recv()

    def drain(self, i):
        @pl.when(self.owner)
        def _():
            self.over_first(i).wait_send()

        for place in range(self.count):

            @pl.when(jnp.logical_or(self.owner, place != self.place))
            def _():
                self.over_last(i, place).wait_send()

            @pl.when(jnp.logical_and(place <= self.place, self.place + 1 < self.count))
            def _():
                self.along(i, place, True).wait_send()

            @pl.when(jnp.logical_and(place >= self.place, self.place > 0))
            def _():
                self.along(i, place, False).wait_send()


def cross_scratch(layers, count):
    pieces = 4
    return [
        pltpu.SemaphoreType.DMA((layers, 2, pieces)),
        pltpu.SemaphoreType.DMA((layers, 2, pieces, count, 2)),
        pltpu.SemaphoreType.DMA((layers, 2, pieces, count)),
        pltpu.SemaphoreType.DMA((layers, pieces, 2)),
    ]


def greet_all(ring, whole_line=False):
    barrier = pltpu.get_barrier_semaphore()
    section, place, count = lax.axis_index(SECTION), lax.axis_index(DP), lax.axis_size(DP)
    for device in ({TENSOR: ring.mate}, {TENSOR: ring.peer}, {SECTION: 1 - section}):
        pl.semaphore_signal(barrier, inc=1, device_id=device, device_id_type=MESH)
    if whole_line:
        for there in range(count):

            @pl.when(there != place)
            def _():
                pl.semaphore_signal(barrier, inc=1, device_id={DP: there}, device_id_type=MESH)

        pl.semaphore_wait(barrier, 2 + count)
        return

    @pl.when(place > 0)
    def _():
        pl.semaphore_signal(barrier, inc=1, device_id={DP: place - 1}, device_id_type=MESH)

    @pl.when(place + 1 < count)
    def _():
        pl.semaphore_signal(barrier, inc=1, device_id={DP: place + 1}, device_id_type=MESH)

    pl.semaphore_wait(barrier, 3 + jnp.where(place > 0, 1, 0) + jnp.where(place + 1 < count, 1, 0))


PUMP_POINTS = ({3: 4, 6: 5, 9: 6, 11: 7, 12: 8, 13: 9, 14: 10}, {})


class Pump:
    def __init__(self, crossings):
        self.pieces = [(crossing, i) for crossing in crossings for i in range(4)]
        self.hops = crossings[0].count
        self.done = 0
        for crossing, i in self.pieces:
            crossing.begin(i)

    def stage(self, number):
        for hops in range(self.hops):
            if 0 <= number - hops < len(self.pieces):
                crossing, i = self.pieces[number - hops]
                if hops == 0:
                    crossing.start(i)
                else:
                    crossing.step(i, hops)

    def until(self, number):
        while self.done <= min(number, len(self.pieces) + self.hops - 2):
            self.stage(self.done)
            self.done += 1

    def tick(self, layer, point):
        self.until(PUMP_POINTS[layer].get(point, -1))

    def have(self, piece):
        self.until(piece + self.hops - 1)
        crossing, i = self.pieces[piece]
        crossing.finish(i)

    def drain(self):
        for crossing, i in self.pieces:
            crossing.drain(i)


KEPT = 6
SMALL_ROWS = 8


def forward_kernel(layers, *refs):
    (x, vector, *shards), refs = refs[:6], refs[6:]
    slopes, refs = refs[0], refs[1:]
    outs, refs = [refs[j * 13 : (j + 1) * 13] for j in range(layers)], refs[13 * layers :]
    vectors, refs = refs[0], refs[1:]
    held, refs = [refs[j * 10 : (j + 1) * 10] for j in range(layers)], refs[10 * layers :]
    penalty, own, stage, land, gather_sems, scatter_sems, save_sems, vector_sems = refs[:8]
    cross_sems = refs[8:]
    ring = Ring(x.shape[0])
    section = lax.axis_index(SECTION)
    greet_all(ring)
    crossings = [
        Cross(l, shards, held[l][6:10], [sem.at[l] for sem in cross_sems]) for l in range(layers)
    ]
    pump = Pump(crossings)
    vector_out = pltpu.make_async_remote_copy(
        src_ref=vector,
        dst_ref=vectors.at[section],
        send_sem=vector_sems.at[0],
        recv_sem=vector_sems.at[1],
        device_id={SECTION: 1 - section},
        device_id_type=MESH,
    )
    vector_in = pltpu.make_async_remote_copy(
        src_ref=vector,
        dst_ref=vectors.at[1 - section],
        send_sem=vector_sems.at[0],
        recv_sem=vector_sems.at[1],
        device_id={SECTION: 1 - section},
        device_id_type=MESH,
    )
    vector_out.start()
    vectors[section] = vector[...]
    fill_penalty(penalty)
    vector_in.wait_recv()
    saves = []

    def save(l, i, src):
        copy = pltpu.make_async_copy(src, outs[l][i], save_sems.at[l, i])
        copy.start()
        saves.append(copy)

    links = []
    entering = x
    for l in range(layers):
        normed, proj, context, second, activated, slope_of, wq, wo, wu, wd = held[l]
        totals, middle, leaving = outs[l][10:13]

        def row(i):
            return lambda: vectors[l, pl.ds(i, 1), :]

        def qv(part):
            local = context.shape[1]
            return vectors[l, pl.ds(7, 1), pl.ds((part // 2) * local, local)]

        def link(every, phase):
            gather = Gather(ring, every, gather_sems.at[phase])
            scatter = Scatter(ring, stage, land.at[phase], scatter_sems.at[phase])
            links.append((gather, scatter))
            return gather, scatter

        def have(i):
            pump.have(l * 4 + i)
            save(l, 6 + i, held[l][6 + i])

        gather, scatter = link(normed, 0)
        attention_forward_body(
            ring, gather, scatter, entering, row(0), row(1), wq, qv, wo, row(2), slopes,
            normed, proj, context, totals, middle, penalty,
            qkv_ready=lambda: have(0), out_ready=lambda: have(1), tick=lambda point, l=l: pump.tick(l, point),
        )
        save(l, 0, normed)
        save(l, 1, proj)
        save(l, 2, context)
        gather.finish()
        scatter.finish()
        gather, scatter = link(second, 1)

        def ready():
            have(2)
            have(3)

        mlp_forward_body(
            ring, gather, scatter, middle, row(3), row(4), wu, row(5), wd, row(6),
            second, activated, slope_of, leaving, own,
            ready=ready, tick=lambda point, l=l: pump.tick(l, point),
        )
        save(l, 3, second)
        save(l, 4, activated)
        save(l, 5, slope_of)
        gather.finish()
        scatter.finish()
        entering = leaving
    vector_out.wait_send()
    pump.drain()
    for copy in saves:
        copy.wait()


def forward_call(x, vector, shards, slopes):
    layers, places = lax.axis_size(SECTION), lax.axis_size(DP)
    block, width = x.shape
    length = block * lax.axis_size(TENSOR)
    sq, so, su, sd = shards
    local, units = so.shape[0], sd.shape[0]
    heads = local // HEAD
    kept = [
        ((length, width), BF16),
        ((3, length, local), BF16),
        ((length, local), BF16),
        ((length, width), BF16),
        ((length, units), BF16),
        ((length, units), BF16),
        ((3, width, local), BF16),
        ((local, width), BF16),
        ((width, units), BF16),
        ((units, width), BF16),
    ]
    near = [((heads, length), F32), ((block, width), F32), ((block, width), BF16)]
    vmem, far = pl.BlockSpec(memory_space=pltpu.VMEM), pl.BlockSpec(memory_space=pl.ANY)
    made = pl.pallas_call(
        functools.partial(forward_kernel, layers),
        out_shape=[jax.ShapeDtypeStruct(shape, dtype) for _ in range(layers) for shape, dtype in kept + near]
        + [jax.ShapeDtypeStruct((layers,) + vector.shape, F32)],
        in_specs=[vmem, vmem] + [far] * 4 + [vmem],
        out_specs=([far] * len(kept) + [vmem] * len(near)) * layers + [vmem],
        scratch_shapes=[pltpu.VMEM(shape, dtype) for _ in range(layers) for shape, dtype in kept]
        + [
            pltpu.VMEM((length, LANES), F32),
            pltpu.VMEM((block, width), F32),
            pltpu.VMEM((3, block, width), BF16),
            pltpu.VMEM((2, 3, block, width), BF16),
            pltpu.SemaphoreType.DMA((2, 2, 3, CHUNKS)),
            pltpu.SemaphoreType.DMA((2, 2, 3, CHUNKS)),
            pltpu.SemaphoreType.DMA((layers, len(kept))),
            pltpu.SemaphoreType.DMA((2,)),
        ]
        + cross_scratch(layers, places),
        compiler_params=pltpu.CompilerParams(
            collective_id=5, has_side_effects=True, vmem_limit_bytes=VMEM_LIMIT
        ),
        name="forward",
    )(x, vector, sq, so, su, sd, slopes)
    saved, weights = [], []
    entering = x
    vectors = made[-1]
    for l in range(layers):
        normed, proj, context, second, activated, slope_of, wq, wo, wu, wd, totals, middle, leaving = made[13 * l : 13 * l + 13]
        saved.append(dict(x=entering, normed=normed, proj=proj, context=context, totals=totals, middle=middle, second=second, activated=activated, slope_of=slope_of))
        weights.append(dict(qkv=wq, out=wo, up=wu, down=wd, ln1_gain=vectors[l, 0], ln2_gain=vectors[l, 3]))
        entering = leaving
    return [made[13 * l + 12] for l in range(layers)], saved, weights, vectors


class Fold:
    def __init__(self, layer, kind, parts, first_land, line_land, last_land, out, sems, number):
        self.kind, self.parts, self.out = kind, parts, out
        self.first_land, self.line_land, self.last_land = first_land, line_land, last_land
        self.first, self.line, self.last = sems
        self.number = number
        self.section, self.place = lax.axis_index(SECTION), lax.axis_index(DP)
        self.count = lax.axis_size(DP)
        self.owner = self.section == layer
        self.half = jnp.where(self.owner, 0, 1)
        self.events = self.count + 2
        self.ran = 0

    def at(self, half, place):
        ref = self.parts
        if self.kind == 0:
            rows = ref.shape[1] // (2 * self.count)
            return ref.at[:, rows_at((place * 2 + half) * rows, rows), :]
        if self.kind == 2:
            rows = ref.shape[0] // (2 * self.count)
            return ref.at[rows_at((place * 2 + half) * rows, rows), :]
        rows, columns = ref.shape[0] // 2, ref.shape[1] // self.count
        return ref.at[rows_at(half * rows, rows), rows_at(place * columns, columns)]

    def out_at(self, half):
        ref = self.out
        rows = ref.shape[1 if self.kind == 0 else 0] // 2
        return ref.at[:, pl.ds(half * rows, rows), :] if self.kind == 0 else ref.at[pl.ds(half * rows, rows), :]

    def copy(self, src, dst, sems, where, device):
        return pltpu.make_async_remote_copy(
            src_ref=src,
            dst_ref=dst,
            send_sem=sems.at[(0, self.number) + where],
            recv_sem=sems.at[(1, self.number) + where],
            device_id=device,
            device_id_type=MESH,
        )

    def over_first(self, place):
        return self.copy(
            self.at(1 - self.half, place),
            self.first_land.at[place],
            self.first,
            (place,),
            {SECTION: 1 - self.section},
        )

    def along(self, place, right, to):
        slot = place if right else jnp.where(place == to, self.count, place)
        return self.copy(
            self.at(self.half, place),
            self.line_land.at[slot],
            self.line,
            (place, int(right)),
            {DP: self.place + (1 if right else -1)},
        )

    def over_last(self):
        return self.copy(
            self.at(self.half, self.place),
            self.last_land,
            self.last,
            (),
            {SECTION: 1 - self.section},
        )

    def begin(self):
        for hops in range(self.count - 1, -1, -1):
            for right in (True, False) if hops else (True,):
                place = self.place + hops if right else self.place - hops

                @pl.when(place < self.count if right else place >= 0)
                def _():
                    self.over_first(place).start()

    def met(self, place):
        self.over_first(place).wait_recv()
        at = self.at(self.half, place)
        at[...] = (at[...].astype(F32) + self.first_land[place].astype(F32)).astype(BF16)

    def took(self, place, right):
        at = self.at(self.half, place)
        self.along(place, right, self.place).wait_recv()
        slot = place if right else jnp.where(place == self.place, self.count, place)
        at[...] = (at[...].astype(F32) + self.line_land[slot].astype(F32)).astype(BF16)

    def event(self):
        hops = self.count - 1 - self.ran
        self.ran += 1
        if hops > 0:
            for right in (True, False):
                place = self.place + hops if right else self.place - hops

                @pl.when(place < self.count if right else place >= 0)
                def _():
                    self.met(place)

                    @pl.when(self.place > 0 if right else self.place + 1 < self.count)
                    def _():
                        self.took(place, right)

                    self.along(place, right, self.place + (1 if right else -1)).start()

        elif hops == 0:
            self.met(self.place)

            @pl.when(self.place > 0)
            def _():
                self.took(self.place, True)

            @pl.when(self.place + 1 < self.count)
            def _():
                self.took(self.place, False)

            @pl.when(self.owner)
            def _():
                self.out_at(0)[...] = self.at(0, self.place)[...].astype(F32)

            @pl.when(jnp.logical_not(self.owner))
            def _():
                self.over_last().start()

        elif hops == -1:

            @pl.when(self.owner)
            def _():
                self.over_last().wait_recv()
                self.out_at(1)[...] = self.last_land[...].astype(F32)

    def drain(self):
        for place in range(self.count):
            self.over_first(place).wait_send()

            @pl.when(jnp.logical_and(place > self.place, self.place + 1 < self.count))
            def _():
                self.along(place, True, self.place + 1).wait_send()

            @pl.when(jnp.logical_and(place < self.place, self.place > 0))
            def _():
                self.along(place, False, self.place - 1).wait_send()

        @pl.when(jnp.logical_not(self.owner))
        def _():
            self.over_last().wait_send()


class Folds:
    def __init__(self):
        self.folds = []

    def begin(self, fold):
        fold.begin()
        self.folds.append(fold)

    def tick(self):
        before = None
        for fold in list(self.folds):
            limit = fold.events - 1 if before is None else before - 1
            if fold.ran < fold.events - 1 and (fold.ran < limit or before is None):
                fold.event()
            before = fold.ran if fold.ran < fold.events - 1 else fold.events

    def finish(self):
        while any(fold.ran < fold.events - 1 for fold in self.folds):
            self.tick()
        for fold in self.folds:
            fold.drain()


def fold_shapes(kind, count, width, local, units):
    if kind == 0:
        return (3, width, local), (3, width // count // 2, local), (3, width // count, local)
    if kind == 1:
        return (local, width), (local // 2, width // count), (local, width // count)
    if kind == 2:
        return (width, units), (width // count // 2, units), (width // count, units)
    return (units, width), (units // 2, width // count), (units, width // count)


QKV, OUT, UP, DOWN = 0, 1, 2, 3


class Names:
    pass


def take_refs(names, refs):
    bag = Names()
    for name, ref in zip(names, refs, strict=True):
        setattr(bag, name, ref)
    return bag


def backward_kernel(layer, top, names, kinds, *refs):
    r = take_refs(names, refs)
    block, width = r.x.shape
    local, units = r.wo.shape[0], r.wd.shape[0]
    count = lax.axis_size(DP)
    section, place = lax.axis_index(SECTION), lax.axis_index(DP)
    other = 1 - section
    ring = Ring(block)
    greet_all(ring, not top)
    loads = {}
    for number, name in enumerate(("wd", "slope", "wu", "activated", "second", "wo", "proj", "wq", "context")):
        loads[name] = pltpu.make_async_copy(
            getattr(r, name), getattr(r, name + "_here"), r.load_sems.at[number]
        )
        loads[name].start()
    normed_load = pltpu.make_async_copy(r.normed, r.activated_here, r.load_sems.at[9])
    folds = Folds()
    made_folds = {}

    def make_fold(key, of_layer, kind, parts, out, number):
        made_folds[key] = Fold(
            of_layer, kind, parts, getattr(r, "first_" + key), getattr(r, "line_" + key),
            getattr(r, "last_" + key), out, (r.first_sems, r.line_sems, r.end_sems), number,
        )

    def passing(src, dst, sem):
        return pltpu.make_async_remote_copy(
            src_ref=src, dst_ref=dst, send_sem=r.pass_sems.at[0, sem], recv_sem=r.pass_sems.at[1, sem],
            device_id={SECTION: other}, device_id_type=MESH,
        )

    r.small[...] = jnp.zeros_like(r.small)

    def add_small(i, value):
        r.small[pl.ds(i, 1)] += value

    def add_up(value):
        r.small[6:7] += value

    kept = []
    if top:
        for s in range(2):

            @pl.when(section == s)
            def _():
                r.acts_out[s] = (r.act0 if s == 0 else r.act1)[...]
                passing(r.act1 if s == 0 else r.act0, r.acts_out.at[s], 0).start()

        incoming = r.incoming
    else:
        incoming_load = pltpu.make_async_copy(r.incoming, r.grads_out.at[1], r.load_sems.at[11])
        incoming_load.start()
        incoming_load.wait()
        r.rounded[...] = r.grads_out[1].astype(BF16)
        incoming = r.rounded

        @pl.when(section == 0)
        def _():
            passing(r.rounded, r.grads_land, 0).start()

        for number, (src, dst) in enumerate(((r.gu_in, r.gu), (r.gd_in, r.gd), (r.go_in, r.go))):
            copy = pltpu.make_async_copy(src, dst, r.keep_sems.at[number])
            kept.append(copy)

            @pl.when(section == 1)
            def _():
                copy.start()

        make_fold("q1", 1, QKV, r.q1_here, r.gq, 4)
        q1_load = pltpu.make_async_copy(r.q1, r.q1_here, r.load_sems.at[10])
        q1_load.start()
        q1_load.wait()
        folds.begin(made_folds["q1"])
    fill_penalty(r.penalty)

    phase = 0
    gather = Gather(ring, r.down_rows, r.gather_sems.at[0])
    scatter = Scatter(ring, r.stage, r.land.at[0], r.scatter_sems.at[0])

    def ready_mlp():
        for name in ("wd", "slope", "wu"):
            loads[name].wait()

    def mlp_made():
        loads["activated"].wait()
        for start in range(0, units, block):
            at = pl.ds(start, block)
            r.part_d[at] = mm_a(r.activated_here[:, at], r.down_rows[...]).astype(BF16)
        make_fold("d", layer, DOWN, r.part_d, r.gd, 0)
        folds.begin(made_folds["d"])
        normed_load.start()
        loads["second"].wait()
        for start in range(0, width, block):
            at = pl.ds(start, block)
            r.part_u[at] = mm_a(r.second_here[:, at], r.slope_here[...]).astype(BF16)
        make_fold("u", layer, UP, r.part_u, r.gu, 1)
        folds.begin(made_folds["u"])

    mlp_backward_body(
        ring, gather, scatter, incoming, r.middle, lambda: r.vectors[layer, 3:4, :],
        r.wu_here, r.wd_here, r.slope_here, r.down_rows, r.slope_here, r.grad_hidden,
        add_small, add_up, r.own,
        ready=ready_mlp, made=mlp_made, tick=folds.tick,
    )
    gather.finish()
    scatter.finish()
    gather = Gather(ring, r.attn_rows, r.gather_sems.at[1])
    scatter = Scatter(ring, r.stage, r.land.at[1], r.scatter_sems.at[1])

    def out_ready():
        loads["wo"].wait()

    def gathered():
        loads["context"].wait()
        r.part_o[...] = mm_a(r.context_here[...], r.attn_rows[...]).astype(BF16)
        make_fold("o", layer, OUT, r.part_o, r.go, 2)
        folds.begin(made_folds["o"])

    def attn_ready():
        loads["proj"].wait()
        loads["wq"].wait()

    def attn_made():
        normed_load.wait()
        for part in range(3):
            for start in range(0, width, block):
                at = pl.ds(start, block)
                made = mm_a(r.activated_here[:, at], r.grad_proj[part]).astype(BF16)
                r.part_q[part, at] = made
        r.small[7:8, 0:local] = jnp.sum(r.grad_proj[0].astype(F32), axis=0, keepdims=True)
        r.small[7:8, local : 2 * local] = jnp.sum(r.grad_proj[2].astype(F32), axis=0, keepdims=True)
        if not top:
            make_fold("q", layer, QKV, r.part_q, r.gq, 3)
            folds.begin(made_folds["q"])

    attention_backward_body(
        ring, gather, scatter, r.grad_hidden, r.x, lambda: r.vectors[layer, 0:1, :],
        r.wq_here, r.wo_here, r.slopes, r.proj_here, r.totals, r.attn_rows, r.grad_proj,
        r.grad_hidden, add_small, r.grad_context, r.sums, r.penalty,
        out_ready=out_ready, ready=attn_ready, gathered=gathered, made=attn_made, tick=folds.tick,
    )
    gather.finish()
    scatter.finish()
    if top:
        folds.finish()
        for s in range(2):

            @pl.when(section == s)
            def _():
                passing(r.act1 if s == 0 else r.act0, r.acts_out.at[s], 0).wait_send()
                passing(r.act0, r.acts_out.at[1 - s], 0).wait_recv()

        return

    @pl.when(section == 0)
    def _():
        r.small_go[0] = r.small_in[...]
        r.small_keep[...] = r.small[...]

    @pl.when(section == 1)
    def _():
        r.small_go[0] = r.small[...]
        r.small_keep[...] = r.small_in[...]
        r.rounded[...] = r.grad_hidden[...].astype(BF16)
        passing(r.rounded, r.grads_land, 0).start()

    small_pass = passing(r.small_go.at[0], r.small_land.at[0], 1)
    small_pass.start()
    small_pass.wait()
    r.small_go[1] = r.small_keep[...] + r.small_land[0]

    def to_place(there, slot, sem):
        return pltpu.make_async_remote_copy(
            src_ref=r.small_go.at[1], dst_ref=r.small_land.at[slot], send_sem=r.small_sems.at[0, sem],
            recv_sem=r.small_sems.at[1, slot], device_id={DP: there}, device_id_type=MESH,
        )

    for there in range(count):

        @pl.when(there != place)
        def _():
            to_place(there, 1 + place, 1 + there).start()

    r.small_land[1 + place] = r.small_go[1]
    for there in range(count):

        @pl.when(there != place)
        def _():
            to_place(there, 1 + there, 1 + there).wait_recv()
            to_place(there, 1 + place, 1 + there).wait_send()

    total = r.small_land[1]
    for there in range(1, count):
        total += r.small_land[1 + there]
    r.small_go[2] = total
    for step, device in enumerate((ring.mate, ring.peer)):
        hop = pltpu.make_async_remote_copy(
            src_ref=r.small_go.at[2 + step], dst_ref=r.small_land.at[1 + count + step],
            send_sem=r.small_sems.at[0, 1 + count + step], recv_sem=r.small_sems.at[1, 1 + count + step],
            device_id={TENSOR: device}, device_id_type=MESH,
        )
        hop.start()
        hop.wait()
        r.small_go[3 + step] = r.small_go[2 + step] + r.small_land[1 + count + step]
    r.small_out[0:6] = r.small_go[4, 0:6]
    r.small_out[6:8] = total[6:8]

    q1_parts = folds.finish()
    for copy in kept:

        @pl.when(section == 1)
        def _():
            copy.wait()

    grads_pass = passing(r.rounded, r.grads_land, 0)
    grads_pass.wait()
    for s in range(2):

        @pl.when(section == s)
        def _():
            if s == 0:
                r.grads_out[0] = r.grad_hidden[...]
            r.grads_out[1 - s] = r.grads_land[...].astype(F32)


def mm_a(left, right):
    return lax.dot_general(left, right, (((0,), (0,)), ((), ())), preferred_element_type=F32)


def backward_call(layer, top, values, slopes):
    count = lax.axis_size(DP)
    block, width = values["x"].shape
    length = block * lax.axis_size(TENSOR)
    local, units = values["wo"].shape[0], values["wd"].shape[0]
    vmem, far = pl.BlockSpec(memory_space=pltpu.VMEM), pl.BlockSpec(memory_space=pl.ANY)
    ins = ["middle", "x", "totals", "vectors", "slopes"]
    ins_far = ["wd", "wu", "wo", "wq", "slope", "activated", "second", "normed", "proj", "context"]
    outs = [("grad_hidden", (block, width), F32), ("small", (8, width), F32)]
    shards = [
        ("gu", fold_shapes(UP, count, width, local, units)[2], F32),
        ("gd", fold_shapes(DOWN, count, width, local, units)[2], F32),
        ("go", fold_shapes(OUT, count, width, local, units)[2], F32),
    ]
    whole = {kind: fold_shapes(kind, count, width, local, units)[0] for kind in range(4)}
    if top:
        ins += ["incoming", "act0", "act1"]
        outs += shards + [("part_q", whole[QKV], BF16), ("acts_out", (2, block, width), BF16)]
    else:
        ins += ["small_in"]
        ins_far += ["incoming", "gu_in", "gd_in", "go_in", "q1"]
        outs += shards + [
            ("gq", fold_shapes(QKV, count, width, local, units)[2], F32),
            ("small_out", (8, width), F32),
            ("grads_out", (2, block, width), F32),
        ]
    dma = pltpu.SemaphoreType.DMA
    scratch = dict(
        wd_here=pltpu.VMEM((units, width), BF16),
        wu_here=pltpu.VMEM((width, units), BF16),
        wo_here=pltpu.VMEM((local, width), BF16),
        wq_here=pltpu.VMEM((3, width, local), BF16),
        slope_here=pltpu.VMEM((length, units), BF16),
        activated_here=pltpu.VMEM((length, units), BF16),
        second_here=pltpu.VMEM((length, width), BF16),
        proj_here=pltpu.VMEM((3, length, local), BF16),
        context_here=pltpu.VMEM((length, local), BF16),
        down_rows=pltpu.VMEM((length, width), BF16),
        attn_rows=pltpu.VMEM((length, width), BF16),
        grad_proj=pltpu.VMEM((3, length, local), BF16),
        grad_context=pltpu.VMEM((length, local), BF16),
        sums=pltpu.VMEM((2, length, PAIR), F32),
        penalty=pltpu.VMEM((length, LANES), F32),
        own=pltpu.VMEM((block, width), F32),
        stage=pltpu.VMEM((3, block, width), BF16),
        land=pltpu.VMEM((2, 3, block, width), BF16),
        gather_sems=dma((2, 2, 3, CHUNKS)),
        scatter_sems=dma((2, 2, 3, CHUNKS)),
        load_sems=dma((12,)),
        pass_sems=dma((2, 2)),
        first_sems=dma((2, 5, count)),
        line_sems=dma((2, 5, count, 2)),
        end_sems=dma((2, 5)),
        part_d=pltpu.VMEM(whole[DOWN], BF16),
        part_u=pltpu.VMEM(whole[UP], BF16),
        part_o=pltpu.VMEM(whole[OUT], BF16),
    )
    keys = {"d": DOWN, "u": UP, "o": OUT}
    if not top:
        keys.update({"q": QKV, "q1": QKV})
        scratch.update(
            part_q=pltpu.VMEM(whole[QKV], BF16),
            q1_here=pltpu.VMEM(whole[QKV], BF16),
            rounded=pltpu.VMEM((block, width), BF16),
            grads_land=pltpu.VMEM((block, width), BF16),
            small_go=pltpu.VMEM((5, 8, width), F32),
            small_keep=pltpu.VMEM((8, width), F32),
            small_land=pltpu.VMEM((3 + count, 8, width), F32),
            small_sems=dma((2, 3 + count)),
            keep_sems=dma((3,)),
        )
    for key, kind in keys.items():
        half = fold_shapes(kind, count, width, local, units)[1]
        scratch["first_" + key] = pltpu.VMEM((count,) + half, BF16)
        scratch["line_" + key] = pltpu.VMEM((count + 1,) + half, BF16)
        scratch["last_" + key] = pltpu.VMEM(half, BF16)
    values = dict(values, slopes=slopes)
    names = ins + ins_far + [item[0] for item in outs] + list(scratch)
    made = pl.pallas_call(
        functools.partial(backward_kernel, layer, top, names, None),
        out_shape=[jax.ShapeDtypeStruct(shape, dtype) for _, shape, dtype in outs],
        in_specs=[vmem] * len(ins) + [far] * len(ins_far),
        out_specs=[vmem] * len(outs),
        scratch_shapes=list(scratch.values()),
        compiler_params=pltpu.CompilerParams(
            collective_id=6 + layer, has_side_effects=True, vmem_limit_bytes=VMEM_LIMIT
        ),
        name="backward_%d" % layer,
    )(*[values[name] for name in ins + ins_far])
    return {item[0]: value for item, value in zip(outs, made)}


def swapped(value):
    count = lax.axis_size(SECTION)
    return lax.ppermute(value, SECTION, [(i, (i + 1) % count) for i in range(count)])


def backward_near(incoming, acts, saved, layers, vectors, slopes, local):
    def values(l, **more):
        w, s = layers[l], saved[l]
        return dict(
            middle=s["middle"], x=s["x"], totals=s["totals"], vectors=vectors, slope=s["slope_of"],
            activated=s["activated"], second=s["second"], normed=s["normed"], proj=s["proj"],
            context=s["context"], wd=w["down"], wu=w["up"], wo=w["out"], wq=w["qkv"], **more,
        )

    high = backward_call(1, True, values(1, incoming=incoming, act0=acts[0], act1=acts[1]), slopes)
    low = backward_call(
        0,
        False,
        values(
            0, incoming=high["grad_hidden"], small_in=high["small"], gu_in=high["gu"],
            gd_in=high["gd"], go_in=high["go"], q1=high["part_q"],
        ),
        slopes,
    )
    places = lax.axis_size(DP)
    tensor, place = lax.axis_index(TENSOR), lax.axis_index(DP)
    small = low["small_out"]
    width = small.shape[1]
    share = width // (lax.axis_size(TENSOR) * places)
    vector = lax.dynamic_slice_in_dim(small[:6], (tensor * places + place) * share, share, axis=1)
    up_share, qv_share = width // places, local // places
    up = lax.dynamic_slice_in_dim(small[6], place * up_share, up_share)
    qv = lax.dynamic_slice_in_dim(
        small[7, : 2 * local].reshape(2, local), place * qv_share, qv_share, axis=1
    )
    return (
        high["acts_out"][None],
        low["grads_out"][None],
        vector[0][None],
        vector[1][None],
        jnp.transpose(low["gq"], (1, 0, 2))[None],
        qv[None],
        low["go"][None],
        vector[2][None],
        vector[3][None],
        vector[4][None],
        low["gu"][None],
        up[None],
        low["gd"][None],
        vector[5][None],
    )


def near_shards(depth, block):
    return depth % 256 == 0 and block % 256 == 0


def gathered_layers(section, layer_count, w_qkv, w_out, w_up, w_down, small_ones):
    def both(value):
        other = swapped(value)
        return [jnp.where(section == l, value, other) for l in range(layer_count)]

    def over_dp(value, axis):
        return both(lax.all_gather(value, DP, axis=axis, tiled=True))

    qkv_all, up_all = over_dp(jnp.transpose(w_qkv[0], (1, 0, 2)), 1), over_dp(w_up[0], 0)
    out_all, down_all = over_dp(w_out[0], 1), over_dp(w_down[0], 1)
    vectors = [
        both(item[0]) for item in small_ones
    ]
    layers = []
    for l in range(layer_count):
        gain1, bias1, qv, bout, gain2, bias2, bup, bdown = [item[l] for item in vectors]
        layers.append(
            dict(
                ln1_gain=gain1,
                ln1_bias=bias1,
                ln2_gain=gain2,
                ln2_bias=bias2,
                qkv=qkv_all[l],
                out=out_all[l],
                up=up_all[l],
                down=down_all[l],
                b_qkv=jnp.stack([qv[0], jnp.zeros_like(qv[0]), qv[1]])[:, None, :],
                b_out=bout,
                b_up=bup,
                b_down=bdown,
            )
        )
    return layers


def per_device(
    inputs,
    out_grad,
    lang_ids,
    lang_weights,
    ln1_gain,
    ln1_bias,
    w_qkv,
    b_qv,
    w_out,
    b_out,
    ln2_gain,
    ln2_bias,
    w_up,
    b_up,
    w_down,
    b_down,
):
    section = lax.axis_index(SECTION)
    layer_count = lax.axis_size(SECTION)
    local_heads = w_qkv.shape[3] // HEAD
    head_ids = lax.axis_index(TENSOR) * local_heads + jnp.arange(local_heads, dtype=jnp.int32)
    slopes = jnp.exp2(-8.0 * (head_ids.astype(jnp.float32) + 1.0) / HEADS)
    slopes = jnp.broadcast_to(slopes[:, None], (local_heads, inputs.shape[1]))

    row = lax.dynamic_index_in_dim(inputs, section, 0, keepdims=False)
    target = lax.dynamic_index_in_dim(out_grad, section, 0, keepdims=False)
    lang = lax.dynamic_index_in_dim(lang_ids, section, 0, keepdims=False)
    matches = lang == jnp.arange(lang_weights.shape[0], dtype=jnp.int32)
    scale = jnp.sum(jnp.where(matches, lang_weights, 0)).astype(jnp.float32) / 64.0

    if near_shards(w_qkv[0].shape[0], inputs.shape[1]):
        vector = jnp.stack(
            [item[0] for item in (ln1_gain, ln1_bias, b_out, ln2_gain, ln2_bias)]
            + [b_up[0], b_down[0], jnp.pad(b_qv[0].reshape(-1), (0, b_out.shape[1] - 2 * b_qv.shape[2]))]
        )
        shards = (jnp.transpose(w_qkv[0], (1, 0, 2)), w_out[0], w_up[0], w_down[0])
        acts, saved, layers, vectors = forward_call(row, vector, shards, slopes)
        return backward_near(
            target.astype(F32) * scale, acts, saved, layers, vectors, slopes, b_qv.shape[2]
        )
    else:
        layers = gathered_layers(
            section, layer_count, w_qkv, w_out, w_up, w_down,
            (ln1_gain, ln1_bias, b_qv, b_out, ln2_gain, ln2_bias, b_up, b_down),
        )
        acts, saved = [], []
        for l in range(layer_count):
            row, kept = layer_forward(row, layers[l], slopes)
            acts.append(row)
            saved.append(kept)
    grads, small, large = [None] * layer_count, [None] * layer_count, [None] * layer_count
    incoming = target.astype(jnp.float32) * scale
    for l in reversed(range(layer_count)):
        grads[l], small[l], large[l] = layer_backward(
            incoming, layers[l], saved[l], slopes
        )
        incoming = grads[l].astype(jnp.bfloat16).astype(jnp.float32)

    def mine(items):
        return jnp.where(section == 0, items[0], items[1])

    def theirs(items):
        return jnp.where(section == 0, items[1], items[0])

    def rows_of(items):
        own, other = mine(items), swapped(theirs(items))
        return jnp.stack([jnp.where(section == r, own, other) for r in range(layer_count)])[None]

    def reduced(name, axis):
        items = [item[name].astype(jnp.bfloat16) for item in large]
        total = mine(items) + swapped(theirs(items))
        return lax.psum_scatter(total, DP, scatter_dimension=axis, tiled=True).astype(
            jnp.float32
        )[None]

    small_total = mine(small) + swapped(theirs(small))
    small_shards = lax.psum_scatter(small_total, (TENSOR, DP), scatter_dimension=1, tiled=True)
    return (
        rows_of(acts),
        rows_of([item.astype(jnp.bfloat16) for item in grads]).astype(jnp.float32),
        small_shards[0][None],
        small_shards[1][None],
        jnp.transpose(reduced("qkv", 1), (0, 2, 1, 3)),
        reduced("b_qv", 1),
        reduced("out", 1),
        small_shards[2][None],
        small_shards[3][None],
        small_shards[4][None],
        reduced("up", 0),
        reduced("b_up", 0),
        reduced("down", 1),
        small_shards[5][None],
    )


def solution(mesh):
    return jax.shard_map(
        per_device,
        mesh=mesh,
        in_specs=(
            P(DP, TENSOR, None),
            P(DP, TENSOR, None),
            P(DP),
            P(),
            P(SECTION, None),
            P(SECTION, None),
            P(SECTION, DP, None, TENSOR),
            P(SECTION, None, TENSOR),
            P(SECTION, TENSOR, DP),
            P(SECTION, None),
            P(SECTION, None),
            P(SECTION, None),
            P(SECTION, DP, TENSOR),
            P(SECTION, TENSOR),
            P(SECTION, TENSOR, DP),
            P(SECTION, None),
        ),
        out_specs=(
            P(SECTION, DP, TENSOR, None),
            P(SECTION, DP, TENSOR, None),
            P(SECTION, (TENSOR, DP)),
            P(SECTION, (TENSOR, DP)),
            P(SECTION, DP, None, TENSOR),
            P(SECTION, None, (TENSOR, DP)),
            P(SECTION, TENSOR, DP),
            P(SECTION, (TENSOR, DP)),
            P(SECTION, (TENSOR, DP)),
            P(SECTION, (TENSOR, DP)),
            P(SECTION, DP, TENSOR),
            P(SECTION, (TENSOR, DP)),
            P(SECTION, TENSOR, DP),
            P(SECTION, (TENSOR, DP)),
        ),
        check_vma=False,
    )
```

```python
import functools

import jax
import jax.numpy as jnp
from jax import lax
from jax.experimental import pallas as pl
from jax.experimental.pallas import tpu as pltpu
from jax.sharding import PartitionSpec as P

HEADS = 16
HEAD = 64
PAIR = 2 * HEAD

EPSILON = 1e-05
GELU_SCALE = 0.7978845608028654

SECTION, TENSOR, DP = "section", "tensor", "dp"
MESH = pl.DeviceIdType.MESH
F32 = jnp.float32
BF16 = jnp.bfloat16
CHUNKS = 2
LANES = 128
VMEM_LIMIT = 61 * 1024 * 1024


def rows_at(start, size):
    return pl.ds(pl.multiple_of(start, size), size)


def mm(left, right):
    return lax.dot_general(left, right, (((1,), (0,)), ((), ())), preferred_element_type=F32)


def mm_t(left, right):
    return lax.dot_general(left, right, (((1,), (1,)), ((), ())), preferred_element_type=F32)


class Ring:
    def __init__(self, block):
        self.block = block
        self.chunk = block // CHUNKS
        self.me = lax.axis_index(TENSOR)
        core, chip = lax.rem(self.me, 2), self.me // 2
        self.mate = self.me + 1 - 2 * core
        self.peer = self.me + 2 - 4 * chip
        self.far = self.peer + 1 - 2 * core

    def greet(self):
        barrier = pltpu.get_barrier_semaphore()
        for other in (self.mate, self.peer):
            pl.semaphore_signal(barrier, inc=1, device_id={TENSOR: other}, device_id_type=MESH)
        pl.semaphore_wait(barrier, 2)

    def rows(self, owner, c):
        return rows_at(owner * self.block + c * self.chunk, self.chunk)

    def send(self, src, dst, sems, kind, c, other):
        return pltpu.make_async_remote_copy(
            src_ref=src,
            dst_ref=dst,
            send_sem=sems.at[0, kind, c],
            recv_sem=sems.at[1, kind, c],
            device_id={TENSOR: other},
            device_id_type=MESH,
        )


class Gather:
    def __init__(self, ring, every, sems):
        self.ring, self.every, self.sems = ring, every, sems

    def copy(self, kind, owner, c):
        ring = self.ring
        at = self.every.at[ring.rows(owner, c)]
        return ring.send(at, at, self.sems, kind, c, ring.peer if kind == 1 else ring.mate)

    def start(self, c):
        self.copy(1, self.ring.me, c).start()
        self.copy(0, self.ring.me, c).start()

    def arrived_mate(self, c):
        self.copy(0, self.ring.mate, c).wait_recv()

    def arrived_peer(self, c):
        self.copy(1, self.ring.peer, c).wait_recv()
        self.copy(2, self.ring.peer, c).start()

    def arrived_far(self, c):
        self.copy(2, self.ring.far, c).wait_recv()

    def finish(self):
        for c in range(CHUNKS):
            for kind, owner in ((0, self.ring.me), (1, self.ring.me), (2, self.ring.peer)):
                self.copy(kind, owner, c).wait_send()


class Scatter:
    def __init__(self, ring, stage, land, sems):
        self.ring, self.stage, self.land, self.sems = ring, stage, land, sems

    def copy(self, kind, c):
        ring = self.ring
        at = pl.ds(c * ring.chunk, ring.chunk)
        return ring.send(
            self.stage.at[kind, at],
            self.land.at[kind, at],
            self.sems,
            kind,
            c,
            ring.peer if kind == 1 else ring.mate,
        )

    def put(self, kind, c, value):
        self.stage[kind, pl.ds(c * self.ring.chunk, self.ring.chunk)] = value.astype(BF16)
        self.copy(kind, c).start()

    def take(self, kind, c):
        self.copy(kind, c).wait_recv()
        return self.land[kind, pl.ds(c * self.ring.chunk, self.ring.chunk)].astype(F32)

    def to_peer(self, c, far_part, peer_part):
        self.put(0, c, far_part)
        self.put(1, c, peer_part + self.take(0, c))

    def finish(self):
        for kind in range(3):
            for c in range(CHUNKS):
                self.copy(kind, c).wait_send()


def normalize(values):
    center = values - jnp.mean(values, axis=-1, keepdims=True)
    scale = lax.rsqrt(jnp.mean(center * center, axis=-1, keepdims=True) + EPSILON)
    return center * scale, scale


def norm_pull(values, gain, grad):
    unit, scale = normalize(values)
    scaled = grad * gain
    pulled = scale * (
        scaled
        - jnp.mean(scaled, axis=-1, keepdims=True)
        - unit * jnp.mean(scaled * unit, axis=-1, keepdims=True)
    )
    return pulled, jnp.sum(grad * unit, axis=0, keepdims=True), jnp.sum(grad, axis=0, keepdims=True)


def scores_of(keys, queries, slope, penalty_ref, start):
    stop, count = keys.shape[0], queries.shape[0]
    scores = mm_t(keys, queries) + slope * jnp.concatenate([penalty_ref[:stop]] * (count // LANES), axis=1)
    last = scores[start:]
    allowed = lax.broadcasted_iota(jnp.int32, (count, count), 0) <= lax.broadcasted_iota(
        jnp.int32, (count, count), 1
    )
    last = jnp.where(allowed, last, -1e30)
    return last if start == 0 else jnp.concatenate([scores[:start], last], axis=0)


def head_mask(value, which):
    lane = lax.broadcasted_iota(jnp.int32, value.shape, 1)
    inside = lane < HEAD if which == 0 else lane >= HEAD
    return jnp.where(inside, value, jnp.zeros_like(value))


def fill_penalty(penalty_ref):
    penalty_ref[...] = lax.broadcasted_iota(jnp.int32, penalty_ref.shape, 0).astype(F32)


def nothing(point=0):
    pass


def attend_forward(proj, context, totals, slopes, penalty, block, tick=nothing):
    length, width = context.shape
    for pair in range(width // PAIR):
        lanes = pl.ds(pair * PAIR, PAIR)
        for start in range(0, length, block):
            tick(pair * 4 + start // block)
            stop = start + block
            queries = proj[0, start:stop, lanes] * jnp.asarray(0.125, BF16)
            keys = proj[1, :stop, lanes]
            values_t = proj[2, :stop, lanes].T
            outs = []
            for which in range(2):
                head = pair * 2 + which
                slope = slopes[pl.ds(head, 1), :]
                scores = scores_of(keys, head_mask(queries, which), slope, penalty, start)
                highest = jnp.max(scores, axis=0, keepdims=True)
                grown = jnp.exp(scores - highest)
                total = jnp.sum(grown, axis=0, keepdims=True)
                mixed = mm(values_t[which * HEAD : (which + 1) * HEAD], grown.astype(BF16))
                outs.append(mixed / total)
                totals[pl.ds(head, 1), start:stop] = highest + jnp.log(total)
            context[start:stop, lanes] = jnp.concatenate(outs, axis=0).T.astype(BF16)


def attend_backward(proj, grad_context, totals, slopes, penalty, grad_proj, sums, block, tick=nothing):
    length, width = grad_context.shape
    for pair in range(width // PAIR):
        lanes = pl.ds(pair * PAIR, PAIR)
        for start in range(0, length, block):
            tick(pair * 4 + start // block)
            stop = start + block
            queries = proj[0, start:stop, lanes] * jnp.asarray(0.125, BF16)
            keys = proj[1, :stop, lanes]
            keys_t = keys.T
            values = proj[2, :stop, lanes]
            grads = grad_context[start:stop, lanes]
            outs = []
            for which in range(2):
                head = pair * 2 + which
                slope = slopes[pl.ds(head, 1), :]
                one_query = head_mask(queries, which)
                one_grad = head_mask(grads, which)
                scores = scores_of(keys, one_query, slope, penalty, start)
                probs = jnp.exp(scores - totals[pl.ds(head, 1), start:stop])
                pulled = probs * mm_t(values, one_grad)
                inner = jnp.sum(pulled, axis=0, keepdims=True)
                grad_scores = (pulled - probs * inner).astype(BF16)
                outs.append(mm(keys_t[which * HEAD : (which + 1) * HEAD], grad_scores) * 0.125)
                grad_keys = mm(grad_scores, one_query)
                grad_values = mm(probs.astype(BF16), one_grad)
                if which == 0:
                    first_keys, first_values = grad_keys, grad_values
                else:
                    grad_keys, grad_values = grad_keys + first_keys, grad_values + first_values
            grad_proj[0, start:stop, lanes] = jnp.concatenate(outs, axis=0).T.astype(BF16)
            if start > 0:
                sums[0, :start] += grad_keys[:start]
                sums[1, :start] += grad_values[:start]
            sums[0, start:stop] = grad_keys[start:]
            sums[1, start:stop] = grad_values[start:]
        grad_proj[1, :, lanes] = sums[0].astype(BF16)
        grad_proj[2, :, lanes] = sums[1].astype(BF16)


def attention_forward_body(
    ring, gather, scatter, x, gain, shift, w_qkv, b_qkv, w_out, b_out, slopes,
    normed, proj, context, totals, middle, penalty,
    qkv_ready=nothing, out_ready=nothing, tick=nothing,
):
    block, chunk = ring.block, ring.chunk
    for c in range(CHUNKS):
        at = pl.ds(c * chunk, chunk)
        unit, _ = normalize(x[at].astype(F32))
        normed[ring.rows(ring.me, c)] = (unit * gain() + shift()).astype(BF16)
        gather.start(c)
    qkv_ready()

    def project(owner, c, size):
        at = rows_at(owner * block + c * chunk, size)
        rows = normed[at]
        for part in range(3):
            made = mm(rows, w_qkv[part])
            proj[part, at] = (made if part == 1 else made + b_qkv(part)).astype(BF16)

    project(ring.me, 0, block)
    for c in range(CHUNKS):
        gather.arrived_mate(c)
    project(ring.mate, 0, block)
    for c in range(CHUNKS):
        gather.arrived_peer(c)
        project(ring.peer, c, chunk)
        gather.arrived_far(c)
        project(ring.far, c, chunk)
    attend_forward(proj, context, totals, slopes, penalty, block, tick)
    out_ready()

    def part_of(owner, c):
        return mm(context[ring.rows(owner, c)], w_out[...])

    for c in range(CHUNKS):
        scatter.put(0, c, part_of(ring.far, c))
        scatter.put(1, c, part_of(ring.peer, c) + scatter.take(0, c))
        tick(8 + c)
    for c in range(CHUNKS):
        scatter.put(2, c, part_of(ring.mate, c))
    tick(10)
    for c in range(CHUNKS):
        at = pl.ds(c * chunk, chunk)
        total = part_of(ring.me, c) + scatter.take(2, c) + scatter.take(1, c)
        middle[at] = x[at].astype(F32) + total + b_out()


def mlp_forward_body(
    ring, gather, scatter, middle, gain, shift, w_up, b_up, w_down, b_down,
    second, activated, slope_of, leaving, own,
    ready=nothing, tick=nothing,
):
    block, chunk = ring.block, ring.chunk
    for c in range(CHUNKS):
        at = pl.ds(c * chunk, chunk)
        unit, _ = normalize(middle[at])
        second[ring.rows(ring.me, c)] = (unit * gain() + shift()).astype(BF16)
        gather.start(c)

    def expand(at):
        upward = mm(second[at], w_up[...]) + b_up()
        inner = jnp.tanh(GELU_SCALE * (upward + 0.044715 * upward * upward * upward))
        half = 0.5 * (1.0 + inner)
        value = upward * half
        slope = half + 0.5 * upward * (1.0 - inner * inner) * GELU_SCALE * (
            1.0 + 3 * 0.044715 * upward * upward
        )
        value = value.astype(BF16)
        activated[at] = value
        slope_of[at] = slope.astype(BF16)
        return mm(value, w_down[...])

    tick(11)
    ready()
    own[...] = expand(rows_at(ring.me * block, block))
    tick(12)
    for c in range(CHUNKS):
        gather.arrived_mate(c)
    part = expand(rows_at(ring.mate * block, block))
    for c in range(CHUNKS):
        scatter.put(2, c, part[c * chunk : (c + 1) * chunk])
    tick(13)
    for c in range(CHUNKS):
        gather.arrived_peer(c)
        peer_part = expand(ring.rows(ring.peer, c))
        gather.arrived_far(c)
        scatter.put(0, c, expand(ring.rows(ring.far, c)))
        scatter.put(1, c, peer_part + scatter.take(0, c))
        tick(14 + c)
    for c in range(CHUNKS):
        at = pl.ds(c * chunk, chunk)
        total = own[at] + scatter.take(2, c) + scatter.take(1, c)
        leaving[at] = (middle[at] + total + b_down()).astype(BF16)


def attention_forward_kernel(
    x, gain, shift, w_qkv, b_qkv, w_out, b_out, slopes,
    normed, proj, context, totals, middle,
    penalty, stage, land, gather_sems, scatter_sems,
):
    ring = Ring(x.shape[0])
    ring.greet()
    gather = Gather(ring, normed, gather_sems)
    scatter = Scatter(ring, stage, land, scatter_sems)
    fill_penalty(penalty)
    attention_forward_body(
        ring, gather, scatter, x, lambda: gain[...], lambda: shift[...], w_qkv,
        lambda part: b_qkv[part], w_out, lambda: b_out[...], slopes,
        normed, proj, context, totals, middle, penalty,
    )
    gather.finish()
    scatter.finish()


def mlp_forward_kernel(
    middle, gain, shift, w_up, b_up, w_down, b_down,
    second, activated, slope_of, leaving,
    own, stage, land, gather_sems, scatter_sems,
):
    ring = Ring(middle.shape[0])
    ring.greet()
    gather = Gather(ring, second, gather_sems)
    scatter = Scatter(ring, stage, land, scatter_sems)
    mlp_forward_body(
        ring, gather, scatter, middle, lambda: gain[...], lambda: shift[...], w_up,
        lambda: b_up[...], w_down, lambda: b_down[...],
        second, activated, slope_of, leaving, own,
    )
    gather.finish()
    scatter.finish()


def mlp_backward_body(
    ring, gather, scatter, incoming, middle, gain, w_up, w_down, slope_of,
    down_rows, grad_up, grad_middle, small, up_sum, own,
    ready=nothing, made=nothing, tick=nothing,
):
    block, chunk = ring.block, ring.chunk
    for c in range(CHUNKS):
        down_rows[ring.rows(ring.me, c)] = incoming[pl.ds(c * chunk, chunk)].astype(BF16)
        gather.start(c)
    ready()

    def pull(at):
        grad = mm_t(down_rows[at], w_down[...]) * slope_of[at].astype(F32)
        grad = grad.astype(BF16)
        grad_up[at] = grad
        up_sum(jnp.sum(grad.astype(F32), axis=0, keepdims=True))
        return mm_t(grad, w_up[...])

    own[...] = pull(rows_at(ring.me * block, block))
    tick(0)
    for c in range(CHUNKS):
        gather.arrived_mate(c)
    part = pull(rows_at(ring.mate * block, block))
    for c in range(CHUNKS):
        scatter.put(2, c, part[c * chunk : (c + 1) * chunk])
    tick(1)
    for c in range(CHUNKS):
        gather.arrived_peer(c)
        peer_part = pull(ring.rows(ring.peer, c))
        gather.arrived_far(c)
        scatter.put(0, c, pull(ring.rows(ring.far, c)))
        scatter.put(1, c, peer_part + scatter.take(0, c))
        tick(2 + c)
    made()
    tick(4)
    for c in range(CHUNKS):
        at = pl.ds(c * chunk, chunk)
        total = own[at] + scatter.take(2, c) + scatter.take(1, c)
        pulled, grad_gain, grad_shift = norm_pull(middle[at], gain(), total)
        before = incoming[at].astype(F32)
        after = before + pulled
        grad_middle[at] = after
        small(2, jnp.sum(after, axis=0, keepdims=True))
        small(3, grad_gain)
        small(4, grad_shift)
        small(5, jnp.sum(before, axis=0, keepdims=True))
        tick(5 + c)


def attention_backward_body(
    ring, gather, scatter, grad_middle, x, gain, w_qkv, w_out, slopes, proj, totals,
    attn_rows, grad_proj, grad_hidden, small, grad_context, sums, penalty,
    out_ready=nothing, ready=nothing, gathered=nothing, made=nothing, tick=nothing,
):
    block, chunk = ring.block, ring.chunk
    for c in range(CHUNKS):
        attn_rows[ring.rows(ring.me, c)] = grad_middle[pl.ds(c * chunk, chunk)].astype(BF16)
        gather.start(c)
    out_ready()

    def pull(at):
        grad_context[at] = mm_t(attn_rows[at], w_out[...]).astype(BF16)

    pull(rows_at(ring.me * block, block))
    for c in range(CHUNKS):
        gather.arrived_mate(c)
    pull(rows_at(ring.mate * block, block))
    tick(7)
    for c in range(CHUNKS):
        gather.arrived_peer(c)
        pull(ring.rows(ring.peer, c))
        gather.arrived_far(c)
        pull(ring.rows(ring.far, c))
        tick(8 + c)
    gathered()
    ready()
    attend_backward(proj, grad_context, totals, slopes, penalty, grad_proj, sums, block, lambda at: tick(10 + at))

    def part_of(owner, c):
        at = ring.rows(owner, c)
        total = mm_t(grad_proj[0, at], w_qkv[0])
        for part in range(1, 3):
            total += mm_t(grad_proj[part, at], w_qkv[part])
        return total

    for c in range(CHUNKS):
        scatter.put(0, c, part_of(ring.far, c))
        scatter.put(1, c, part_of(ring.peer, c) + scatter.take(0, c))
    for c in range(CHUNKS):
        scatter.put(2, c, part_of(ring.mate, c))
    made()
    tick(18)
    for c in range(CHUNKS):
        at = pl.ds(c * chunk, chunk)
        total = part_of(ring.me, c) + scatter.take(2, c) + scatter.take(1, c)
        pulled, grad_gain, grad_shift = norm_pull(x[at].astype(F32), gain(), total)
        grad_hidden[at] = grad_middle[at] + pulled
        small(0, grad_gain)
        small(1, grad_shift)
        tick(19 + c)


def mlp_backward_kernel(
    incoming, middle, gain, w_up, w_down, slope_of,
    down_rows, grad_up, grad_middle, small, up_sum,
    own, stage, land, gather_sems, scatter_sems,
):
    ring = Ring(middle.shape[0])
    ring.greet()
    gather = Gather(ring, down_rows, gather_sems)
    scatter = Scatter(ring, stage, land, scatter_sems)
    small[...] = jnp.zeros_like(small)
    up_sum[...] = jnp.zeros_like(up_sum)

    def add_small(i, value):
        small[pl.ds(i, 1)] += value

    def add_up(value):
        up_sum[...] += value

    mlp_backward_body(
        ring, gather, scatter, incoming, middle, lambda: gain[...], w_up, w_down, slope_of,
        down_rows, grad_up, grad_middle, add_small, add_up, own,
    )
    gather.finish()
    scatter.finish()


def attention_backward_kernel(
    grad_middle, x, gain, w_qkv, w_out, slopes, proj, totals,
    attn_rows, grad_proj, grad_hidden, small, qv_sum,
    grad_context, sums, penalty, stage, land, gather_sems, scatter_sems,
):
    ring = Ring(x.shape[0])
    ring.greet()
    gather = Gather(ring, attn_rows, gather_sems)
    scatter = Scatter(ring, stage, land, scatter_sems)
    fill_penalty(penalty)
    small[...] = jnp.zeros_like(small)

    def add_small(i, value):
        small[pl.ds(i, 1)] += value

    attention_backward_body(
        ring, gather, scatter, grad_middle, x, lambda: gain[...], w_qkv, w_out, slopes, proj,
        totals, attn_rows, grad_proj, grad_hidden, add_small, grad_context, sums, penalty,
    )
    qv_sum[...] = jnp.zeros_like(qv_sum)
    qv_sum[0:1] = jnp.sum(grad_proj[0].astype(F32), axis=0, keepdims=True)
    qv_sum[1:2] = jnp.sum(grad_proj[2].astype(F32), axis=0, keepdims=True)
    gather.finish()
    scatter.finish()


def call(kernel, name, number, args, outs, scratch):
    vmem = pl.BlockSpec(memory_space=pltpu.VMEM)
    return pl.pallas_call(
        kernel,
        out_shape=[jax.ShapeDtypeStruct(shape, dtype) for shape, dtype in outs],
        in_specs=[vmem] * len(args),
        out_specs=[vmem] * len(outs),
        scratch_shapes=scratch,
        compiler_params=pltpu.CompilerParams(
            collective_id=number, has_side_effects=True, vmem_limit_bytes=VMEM_LIMIT
        ),
        name=name,
    )(*args)


def link_scratch(block, width):
    return [
        pltpu.VMEM((3, block, width), BF16),
        pltpu.VMEM((3, block, width), BF16),
        pltpu.SemaphoreType.DMA((2, 3, CHUNKS)),
        pltpu.SemaphoreType.DMA((2, 3, CHUNKS)),
    ]


def row_vector(value):
    return value.reshape(1, -1)


def layer_forward(x, w, slopes):
    block, width = x.shape
    length = block * lax.axis_size(TENSOR)
    local = w["out"].shape[0]
    heads = local // HEAD
    normed, proj, context, totals, middle = call(
        attention_forward_kernel,
        "attention_forward",
        1,
        (x, row_vector(w["ln1_gain"]), row_vector(w["ln1_bias"]), w["qkv"], w["b_qkv"], w["out"], row_vector(w["b_out"]), slopes),
        [((length, width), BF16), ((3, length, local), BF16), ((length, local), BF16), ((heads, length), F32), ((block, width), F32)],
        [pltpu.VMEM((length, LANES), F32)] + link_scratch(block, width),
    )
    units = w["up"].shape[1]
    second, activated, slope_of, leaving = call(
        mlp_forward_kernel,
        "mlp_forward",
        2,
        (middle, row_vector(w["ln2_gain"]), row_vector(w["ln2_bias"]), w["up"], row_vector(w["b_up"]), w["down"], row_vector(w["b_down"])),
        [((length, width), BF16), ((length, units), BF16), ((length, units), BF16), ((block, width), BF16)],
        [pltpu.VMEM((block, width), F32)] + link_scratch(block, width),
    )
    saved = dict(x=x, normed=normed, proj=proj, context=context, totals=totals, middle=middle, second=second, activated=activated, slope_of=slope_of)
    return leaving, saved


def layer_backward(incoming, w, s, slopes):
    block, width = incoming.shape
    length = block * lax.axis_size(TENSOR)
    local, units = w["out"].shape[0], w["up"].shape[1]
    down_rows, grad_up, grad_middle, small_a, up_sum = call(
        mlp_backward_kernel,
        "mlp_backward",
        3,
        (incoming, s["middle"], row_vector(w["ln2_gain"]), w["up"], w["down"], s["slope_of"]),
        [((length, width), BF16), ((length, units), BF16), ((block, width), F32), ((8, width), F32), ((1, units), F32)],
        [pltpu.VMEM((block, width), F32)] + link_scratch(block, width),
    )
    attn_rows, grad_proj, grad_hidden, small_b, qv_sum = call(
        attention_backward_kernel,
        "attention_backward",
        4,
        (grad_middle, s["x"], row_vector(w["ln1_gain"]), w["qkv"], w["out"], slopes, s["proj"], s["totals"]),
        [((length, width), BF16), ((3, length, local), BF16), ((block, width), F32), ((8, width), F32), ((8, local), F32)],
        [pltpu.VMEM((length, local), BF16), pltpu.VMEM((2, length, PAIR), F32), pltpu.VMEM((length, LANES), F32)]
        + link_scratch(block, width),
    )
    small = jnp.concatenate([small_b[:2], small_a[2:6]])
    large = dict(
        qkv=jnp.einsum("td,cth->cdh", s["normed"], grad_proj, preferred_element_type=F32),
        out=jnp.einsum("th,td->hd", s["context"], attn_rows, preferred_element_type=F32),
        up=jnp.einsum("td,tf->df", s["second"], grad_up, preferred_element_type=F32),
        down=jnp.einsum("tf,td->fd", s["activated"], down_rows, preferred_element_type=F32),
        b_qv=qv_sum[:2],
        b_up=up_sum[0],
    )
    return grad_hidden, small, large


class Cross:
    def __init__(self, layer, shards, whole, sems):
        self.layer, self.shards, self.whole = layer, shards, whole
        self.first, self.line, self.last, self.local = sems
        self.section, self.place = lax.axis_index(SECTION), lax.axis_index(DP)
        self.count = lax.axis_size(DP)
        self.other = 1 - self.section
        self.owner = self.section == layer
        self.half = jnp.where(self.owner, 0, 1)

    def at(self, i, half, place):
        ref = self.whole[i]
        if i == 0:
            rows = self.shards[i].shape[1] // 2
            return ref.at[:, rows_at((place * 2 + half) * rows, rows), :]
        rows = self.shards[i].shape[0] // 2
        if i == 2:
            return ref.at[rows_at((place * 2 + half) * rows, rows), :]
        return ref.at[rows_at(half * rows, rows), rows_at(place * self.shards[i].shape[1], self.shards[i].shape[1])]

    def mine(self, i, half):
        ref = self.shards[i]
        rows = ref.shape[1 if i == 0 else 0] // 2
        return ref.at[:, pl.ds(half * rows, rows), :] if i == 0 else ref.at[pl.ds(half * rows, rows), :]

    def copy(self, src, dst, sems, where, device):
        return pltpu.make_async_remote_copy(
            src_ref=src,
            dst_ref=dst,
            send_sem=sems.at[(0,) + where],
            recv_sem=sems.at[(1,) + where],
            device_id=device,
            device_id_type=MESH,
        )

    def over_first(self, i):
        return self.copy(
            self.mine(i, 1), self.at(i, 1, self.place), self.first, (i,), {SECTION: self.other}
        )

    def over_last(self, i, place, src=None):
        at = self.at(i, self.half, place)
        return self.copy(at if src is None else src, at, self.last, (i, place), {SECTION: self.other})

    def from_last(self, i, place):
        at = self.at(i, 1 - self.half, place)
        return self.copy(at, at, self.last, (i, place), {SECTION: self.other})

    def along(self, i, place, right, src=None):
        at = self.at(i, self.half, place)
        return self.copy(
            at if src is None else src,
            at,
            self.line,
            (i, place, int(right)),
            {DP: self.place + (1 if right else -1)},
        )

    def onward(self, i, place, right, src=None):
        @pl.when(self.place + 1 < self.count if right else self.place > 0)
        def _():
            self.along(i, place, right, src).start()

    def keep(self, i, half):
        return pltpu.make_async_copy(
            self.mine(i, half), self.at(i, half, self.place), self.local.at[i, half]
        )

    def begin(self, i):
        @pl.when(self.owner)
        def _():
            self.over_first(i).start()
            for right in (True, False):
                self.onward(i, self.place, right, self.mine(i, 0))
            self.over_last(i, self.place, self.mine(i, 0)).start()
            for half in range(2):
                self.keep(i, half).start()

    def start(self, i):
        @pl.when(jnp.logical_not(self.owner))
        def _():
            self.over_first(i).wait_recv()
            for right in (True, False):
                self.onward(i, self.place, right)

    def step(self, i, hops):
        for right in (True, False):
            place = self.place - hops if right else self.place + hops

            @pl.when(place >= 0 if right else place < self.count)
            def _():
                self.along(i, place, right).wait_recv()
                self.over_last(i, place).start()
                self.onward(i, place, right)

    def finish(self, i):
        @pl.when(self.owner)
        def _():
            for half in range(2):
                self.keep(i, half).wait()

        for place in range(self.count):

            @pl.when(jnp.logical_or(jnp.logical_not(self.owner), place != self.place))
            def _():
                self.from_last(i, place).wait_recv()

    def drain(self, i):
        @pl.when(self.owner)
        def _():
            self.over_first(i).wait_send()

        for place in range(self.count):

            @pl.when(jnp.logical_or(self.owner, place != self.place))
            def _():
                self.over_last(i, place).wait_send()

            @pl.when(jnp.logical_and(place <= self.place, self.place + 1 < self.count))
            def _():
                self.along(i, place, True).wait_send()

            @pl.when(jnp.logical_and(place >= self.place, self.place > 0))
            def _():
                self.along(i, place, False).wait_send()


def cross_scratch(layers, count):
    pieces = 4
    return [
        pltpu.SemaphoreType.DMA((layers, 2, pieces)),
        pltpu.SemaphoreType.DMA((layers, 2, pieces, count, 2)),
        pltpu.SemaphoreType.DMA((layers, 2, pieces, count)),
        pltpu.SemaphoreType.DMA((layers, pieces, 2)),
    ]


def greet_all(ring, whole_line=False):
    barrier = pltpu.get_barrier_semaphore()
    section, place, count = lax.axis_index(SECTION), lax.axis_index(DP), lax.axis_size(DP)
    for device in ({TENSOR: ring.mate}, {TENSOR: ring.peer}, {SECTION: 1 - section}):
        pl.semaphore_signal(barrier, inc=1, device_id=device, device_id_type=MESH)
    if whole_line:
        for there in range(count):

            @pl.when(there != place)
            def _():
                pl.semaphore_signal(barrier, inc=1, device_id={DP: there}, device_id_type=MESH)

        pl.semaphore_wait(barrier, 2 + count)
        return

    @pl.when(place > 0)
    def _():
        pl.semaphore_signal(barrier, inc=1, device_id={DP: place - 1}, device_id_type=MESH)

    @pl.when(place + 1 < count)
    def _():
        pl.semaphore_signal(barrier, inc=1, device_id={DP: place + 1}, device_id_type=MESH)

    pl.semaphore_wait(barrier, 3 + jnp.where(place > 0, 1, 0) + jnp.where(place + 1 < count, 1, 0))


PUMP_POINTS = ({3: 4, 6: 5, 9: 6, 11: 7, 12: 8, 13: 9, 14: 10}, {})


class Pump:
    def __init__(self, crossings):
        self.pieces = [(crossing, i) for crossing in crossings for i in range(4)]
        self.hops = crossings[0].count
        self.done = 0
        for crossing, i in self.pieces:
            crossing.begin(i)

    def stage(self, number):
        for hops in range(self.hops):
            if 0 <= number - hops < len(self.pieces):
                crossing, i = self.pieces[number - hops]
                if hops == 0:
                    crossing.start(i)
                else:
                    crossing.step(i, hops)

    def until(self, number):
        while self.done <= min(number, len(self.pieces) + self.hops - 2):
            self.stage(self.done)
            self.done += 1

    def tick(self, layer, point):
        self.until(PUMP_POINTS[layer].get(point, -1))

    def have(self, piece):
        self.until(piece + self.hops - 1)
        crossing, i = self.pieces[piece]
        crossing.finish(i)

    def drain(self):
        for crossing, i in self.pieces:
            crossing.drain(i)


KEPT = 6
SMALL_ROWS = 8


def forward_kernel(layers, *refs):
    (x, vector, *shards), refs = refs[:6], refs[6:]
    slopes, refs = refs[0], refs[1:]
    outs, refs = [refs[j * 13 : (j + 1) * 13] for j in range(layers)], refs[13 * layers :]
    vectors, refs = refs[0], refs[1:]
    held, refs = [refs[j * 10 : (j + 1) * 10] for j in range(layers)], refs[10 * layers :]
    penalty, own, stage, land, gather_sems, scatter_sems, save_sems, vector_sems = refs[:8]
    cross_sems = refs[8:]
    ring = Ring(x.shape[0])
    section = lax.axis_index(SECTION)
    greet_all(ring)
    crossings = [
        Cross(l, shards, held[l][6:10], [sem.at[l] for sem in cross_sems]) for l in range(layers)
    ]
    pump = Pump(crossings)
    vector_out = pltpu.make_async_remote_copy(
        src_ref=vector,
        dst_ref=vectors.at[section],
        send_sem=vector_sems.at[0],
        recv_sem=vector_sems.at[1],
        device_id={SECTION: 1 - section},
        device_id_type=MESH,
    )
    vector_in = pltpu.make_async_remote_copy(
        src_ref=vector,
        dst_ref=vectors.at[1 - section],
        send_sem=vector_sems.at[0],
        recv_sem=vector_sems.at[1],
        device_id={SECTION: 1 - section},
        device_id_type=MESH,
    )
    vector_out.start()
    vectors[section] = vector[...]
    fill_penalty(penalty)
    vector_in.wait_recv()
    saves = []

    def save(l, i, src):
        copy = pltpu.make_async_copy(src, outs[l][i], save_sems.at[l, i])
        copy.start()
        saves.append(copy)

    links = []
    entering = x
    for l in range(layers):
        normed, proj, context, second, activated, slope_of, wq, wo, wu, wd = held[l]
        totals, middle, leaving = outs[l][10:13]

        def row(i):
            return lambda: vectors[l, pl.ds(i, 1), :]

        def qv(part):
            local = context.shape[1]
            return vectors[l, pl.ds(7, 1), pl.ds((part // 2) * local, local)]

        def link(every, phase):
            gather = Gather(ring, every, gather_sems.at[phase])
            scatter = Scatter(ring, stage, land.at[phase], scatter_sems.at[phase])
            links.append((gather, scatter))
            return gather, scatter

        def have(i):
            pump.have(l * 4 + i)
            save(l, 6 + i, held[l][6 + i])

        gather, scatter = link(normed, 0)
        attention_forward_body(
            ring, gather, scatter, entering, row(0), row(1), wq, qv, wo, row(2), slopes,
            normed, proj, context, totals, middle, penalty,
            qkv_ready=lambda: have(0), out_ready=lambda: have(1), tick=lambda point, l=l: pump.tick(l, point),
        )
        save(l, 0, normed)
        save(l, 1, proj)
        save(l, 2, context)
        gather.finish()
        scatter.finish()
        gather, scatter = link(second, 1)

        def ready():
            have(2)
            have(3)

        mlp_forward_body(
            ring, gather, scatter, middle, row(3), row(4), wu, row(5), wd, row(6),
            second, activated, slope_of, leaving, own,
            ready=ready, tick=lambda point, l=l: pump.tick(l, point),
        )
        save(l, 3, second)
        save(l, 4, activated)
        save(l, 5, slope_of)
        gather.finish()
        scatter.finish()
        entering = leaving
    vector_out.wait_send()
    pump.drain()
    for copy in saves:
        copy.wait()


def forward_call(x, vector, shards, slopes):
    layers, places = lax.axis_size(SECTION), lax.axis_size(DP)
    block, width = x.shape
    length = block * lax.axis_size(TENSOR)
    sq, so, su, sd = shards
    local, units = so.shape[0], sd.shape[0]
    heads = local // HEAD
    kept = [
        ((length, width), BF16),
        ((3, length, local), BF16),
        ((length, local), BF16),
        ((length, width), BF16),
        ((length, units), BF16),
        ((length, units), BF16),
        ((3, width, local), BF16),
        ((local, width), BF16),
        ((width, units), BF16),
        ((units, width), BF16),
    ]
    near = [((heads, length), F32), ((block, width), F32), ((block, width), BF16)]
    vmem, far = pl.BlockSpec(memory_space=pltpu.VMEM), pl.BlockSpec(memory_space=pl.ANY)
    made = pl.pallas_call(
        functools.partial(forward_kernel, layers),
        out_shape=[jax.ShapeDtypeStruct(shape, dtype) for _ in range(layers) for shape, dtype in kept + near]
        + [jax.ShapeDtypeStruct((layers,) + vector.shape, F32)],
        in_specs=[vmem, vmem] + [far] * 4 + [vmem],
        out_specs=([far] * len(kept) + [vmem] * len(near)) * layers + [vmem],
        scratch_shapes=[pltpu.VMEM(shape, dtype) for _ in range(layers) for shape, dtype in kept]
        + [
            pltpu.VMEM((length, LANES), F32),
            pltpu.VMEM((block, width), F32),
            pltpu.VMEM((3, block, width), BF16),
            pltpu.VMEM((2, 3, block, width), BF16),
            pltpu.SemaphoreType.DMA((2, 2, 3, CHUNKS)),
            pltpu.SemaphoreType.DMA((2, 2, 3, CHUNKS)),
            pltpu.SemaphoreType.DMA((layers, len(kept))),
            pltpu.SemaphoreType.DMA((2,)),
        ]
        + cross_scratch(layers, places),
        compiler_params=pltpu.CompilerParams(
            collective_id=5, has_side_effects=True, vmem_limit_bytes=VMEM_LIMIT
        ),
        name="forward",
    )(x, vector, sq, so, su, sd, slopes)
    saved, weights = [], []
    entering = x
    vectors = made[-1]
    for l in range(layers):
        normed, proj, context, second, activated, slope_of, wq, wo, wu, wd, totals, middle, leaving = made[13 * l : 13 * l + 13]
        saved.append(dict(x=entering, normed=normed, proj=proj, context=context, totals=totals, middle=middle, second=second, activated=activated, slope_of=slope_of))
        weights.append(dict(qkv=wq, out=wo, up=wu, down=wd, ln1_gain=vectors[l, 0], ln2_gain=vectors[l, 3]))
        entering = leaving
    return [made[13 * l + 12] for l in range(layers)], saved, weights, vectors


class Fold:
    def __init__(self, layer, kind, parts, first_land, line_land, last_land, out, sems, number):
        self.kind, self.parts, self.out = kind, parts, out
        self.first_land, self.line_land, self.last_land = first_land, line_land, last_land
        self.first, self.line, self.last = sems
        self.number = number
        self.section, self.place = lax.axis_index(SECTION), lax.axis_index(DP)
        self.count = lax.axis_size(DP)
        self.owner = self.section == layer
        self.half = jnp.where(self.owner, 0, 1)
        self.events = self.count + 2
        self.ran = 0

    def at(self, half, place):
        ref = self.parts
        if self.kind == 0:
            rows = ref.shape[1] // (2 * self.count)
            return ref.at[:, rows_at((place * 2 + half) * rows, rows), :]
        if self.kind == 2:
            rows = ref.shape[0] // (2 * self.count)
            return ref.at[rows_at((place * 2 + half) * rows, rows), :]
        rows, columns = ref.shape[0] // 2, ref.shape[1] // self.count
        return ref.at[rows_at(half * rows, rows), rows_at(place * columns, columns)]

    def out_at(self, half):
        ref = self.out
        rows = ref.shape[1 if self.kind == 0 else 0] // 2
        return ref.at[:, pl.ds(half * rows, rows), :] if self.kind == 0 else ref.at[pl.ds(half * rows, rows), :]

    def copy(self, src, dst, sems, where, device):
        return pltpu.make_async_remote_copy(
            src_ref=src,
            dst_ref=dst,
            send_sem=sems.at[(0, self.number) + where],
            recv_sem=sems.at[(1, self.number) + where],
            device_id=device,
            device_id_type=MESH,
        )

    def over_first(self, place):
        return self.copy(
            self.at(1 - self.half, place),
            self.first_land.at[place],
            self.first,
            (place,),
            {SECTION: 1 - self.section},
        )

    def along(self, place, right, to):
        slot = place if right else jnp.where(place == to, self.count, place)
        return self.copy(
            self.at(self.half, place),
            self.line_land.at[slot],
            self.line,
            (place, int(right)),
            {DP: self.place + (1 if right else -1)},
        )

    def over_last(self):
        return self.copy(
            self.at(self.half, self.place),
            self.last_land,
            self.last,
            (),
            {SECTION: 1 - self.section},
        )

    def begin(self):
        for hops in range(self.count - 1, -1, -1):
            for right in (True, False) if hops else (True,):
                place = self.place + hops if right else self.place - hops

                @pl.when(place < self.count if right else place >= 0)
                def _():
                    self.over_first(place).start()

    def met(self, place):
        self.over_first(place).wait_recv()
        at = self.at(self.half, place)
        at[...] = (at[...].astype(F32) + self.first_land[place].astype(F32)).astype(BF16)

    def took(self, place, right):
        at = self.at(self.half, place)
        self.along(place, right, self.place).wait_recv()
        slot = place if right else jnp.where(place == self.place, self.count, place)
        at[...] = (at[...].astype(F32) + self.line_land[slot].astype(F32)).astype(BF16)

    def event(self):
        hops = self.count - 1 - self.ran
        self.ran += 1
        if hops > 0:
            for right in (True, False):
                place = self.place + hops if right else self.place - hops

                @pl.when(place < self.count if right else place >= 0)
                def _():
                    self.met(place)

                    @pl.when(self.place > 0 if right else self.place + 1 < self.count)
                    def _():
                        self.took(place, right)

                    self.along(place, right, self.place + (1 if right else -1)).start()

        elif hops == 0:
            self.met(self.place)

            @pl.when(self.place > 0)
            def _():
                self.took(self.place, True)

            @pl.when(self.place + 1 < self.count)
            def _():
                self.took(self.place, False)

            @pl.when(self.owner)
            def _():
                self.out_at(0)[...] = self.at(0, self.place)[...].astype(F32)

            @pl.when(jnp.logical_not(self.owner))
            def _():
                self.over_last().start()

        elif hops == -1:

            @pl.when(self.owner)
            def _():
                self.over_last().wait_recv()
                self.out_at(1)[...] = self.last_land[...].astype(F32)

    def drain(self):
        for place in range(self.count):
            self.over_first(place).wait_send()

            @pl.when(jnp.logical_and(place > self.place, self.place + 1 < self.count))
            def _():
                self.along(place, True, self.place + 1).wait_send()

            @pl.when(jnp.logical_and(place < self.place, self.place > 0))
            def _():
                self.along(place, False, self.place - 1).wait_send()

        @pl.when(jnp.logical_not(self.owner))
        def _():
            self.over_last().wait_send()


class Folds:
    def __init__(self, plan):
        self.plan, self.folds, self.begun = plan, {}, []

    def add(self, name, fold):
        self.folds[name] = fold

    def reach(self, name, target):
        fold = self.folds[name]
        if fold not in self.begun:
            fold.begin()
            self.begun.append(fold)
        while fold.ran < min(target, fold.events - 1):
            fold.event()

    def tick(self, point):
        for name, target in self.plan.get(point, ()):
            self.reach(name, target)

    def round(self):
        before = None
        for fold in self.begun:
            if fold.ran < fold.events - 1 and (before is None or fold.ran < before):
                fold.event()
            before = fold.ran if fold.ran < fold.events - 1 else None

    def finish(self):
        while any(fold.ran < fold.events - 1 for fold in self.begun):
            self.round()
        for fold in self.begun:
            fold.drain()


D_, U_, O_, Q_, R_ = range(5)
HIGH_PLAN = {4: ((D_, 0),), 7: ((U_, 0),), 8: ((D_, 1),), 9: ((D_, 2),), 10: ((O_, 0),), 12: ((D_, 3),), 14: ((U_, 1),), 15: ((D_, 4),), 17: ((U_, 2),), 18: ((U_, 3), (O_, 1)), 19: ((D_, 5), (U_, 4), (O_, 2)), 20: ((U_, 5), (O_, 3))}
LOW_PLAN = {4: ((R_, 1), (D_, 0)), 5: ((R_, 2),), 6: ((R_, 3),), 7: ((R_, 4), (U_, 0)), 8: ((D_, 1),), 9: ((R_, 5), (D_, 2)), 10: ((O_, 0),), 12: ((D_, 3),), 14: ((U_, 1),), 15: ((D_, 4),), 17: ((U_, 2),), 18: ((U_, 3), (O_, 1), (Q_, 0)), 19: ((D_, 5), (U_, 4), (O_, 2)), 20: ((U_, 5), (O_, 3), (Q_, 1))}


def fold_shapes(kind, count, width, local, units):
    if kind == 0:
        return (3, width, local), (3, width // count // 2, local), (3, width // count, local)
    if kind == 1:
        return (local, width), (local // 2, width // count), (local, width // count)
    if kind == 2:
        return (width, units), (width // count // 2, units), (width // count, units)
    return (units, width), (units // 2, width // count), (units, width // count)


QKV, OUT, UP, DOWN = 0, 1, 2, 3


class Names:
    pass


def take_refs(names, refs):
    bag = Names()
    for name, ref in zip(names, refs, strict=True):
        setattr(bag, name, ref)
    return bag


def backward_kernel(layer, top, names, kinds, *refs):
    r = take_refs(names, refs)
    block, width = r.x.shape
    local, units = r.wo.shape[0], r.wd.shape[0]
    count = lax.axis_size(DP)
    section, place = lax.axis_index(SECTION), lax.axis_index(DP)
    other = 1 - section
    ring = Ring(block)
    greet_all(ring, not top)
    loads = {}
    for number, name in enumerate(("wd", "slope", "wu", "activated", "second", "wo", "proj", "wq", "context")):
        loads[name] = pltpu.make_async_copy(
            getattr(r, name), getattr(r, name + "_here"), r.load_sems.at[number]
        )
        loads[name].start()
    normed_load = pltpu.make_async_copy(r.normed, r.activated_here, r.load_sems.at[9])
    folds = Folds(HIGH_PLAN if top else LOW_PLAN)

    def make_fold(key, of_layer, kind, parts, out, number):
        folds.add(
            number,
            Fold(
                of_layer, kind, parts, getattr(r, "first_" + key), getattr(r, "line_" + key),
                getattr(r, "last_" + key), out, (r.first_sems, r.line_sems, r.end_sems), number,
            ),
        )

    def passing(src, dst, sem):
        return pltpu.make_async_remote_copy(
            src_ref=src, dst_ref=dst, send_sem=r.pass_sems.at[0, sem], recv_sem=r.pass_sems.at[1, sem],
            device_id={SECTION: other}, device_id_type=MESH,
        )

    r.small[...] = jnp.zeros_like(r.small)

    def add_small(i, value):
        r.small[pl.ds(i, 1)] += value

    def add_up(value):
        r.small[6:7] += value

    kept = []
    if top:
        for s in range(2):

            @pl.when(section == s)
            def _():
                r.acts_out[s] = (r.act0 if s == 0 else r.act1)[...]
                passing(r.act1 if s == 0 else r.act0, r.acts_out.at[s], 0).start()

        incoming = r.incoming
    else:
        incoming_load = pltpu.make_async_copy(r.incoming, r.grads_out.at[1], r.load_sems.at[11])
        incoming_load.start()
        incoming_load.wait()
        r.rounded[...] = r.grads_out[1].astype(BF16)
        incoming = r.rounded

        @pl.when(section == 0)
        def _():
            passing(r.rounded, r.grads_land, 0).start()

        for number, (src, dst) in enumerate(((r.gu_in, r.gu), (r.gd_in, r.gd), (r.go_in, r.go))):
            copy = pltpu.make_async_copy(src, dst, r.keep_sems.at[number])
            kept.append(copy)

            @pl.when(section == 1)
            def _():
                copy.start()

        make_fold("q1", 1, QKV, r.q1_here, r.gq, R_)
        q1_load = pltpu.make_async_copy(r.q1, r.q1_here, r.load_sems.at[10])
        q1_load.start()
        q1_load.wait()
        folds.reach(R_, 0)
    fill_penalty(r.penalty)

    phase = 0
    gather = Gather(ring, r.down_rows, r.gather_sems.at[0])
    scatter = Scatter(ring, r.stage, r.land.at[0], r.scatter_sems.at[0])

    def ready_mlp():
        for name in ("wd", "slope", "wu"):
            loads[name].wait()

    def mlp_made():
        loads["activated"].wait()
        for start in range(0, units, block):
            at = pl.ds(start, block)
            r.part_d[at] = mm_a(r.activated_here[:, at], r.down_rows[...]).astype(BF16)
        make_fold("d", layer, DOWN, r.part_d, r.gd, D_)
        folds.reach(D_, 0)
        normed_load.start()
        loads["second"].wait()
        for start in range(0, width, block):
            at = pl.ds(start, block)
            r.part_u[at] = mm_a(r.second_here[:, at], r.slope_here[...]).astype(BF16)
        make_fold("u", layer, UP, r.part_u, r.gu, U_)

    mlp_backward_body(
        ring, gather, scatter, incoming, r.middle, lambda: r.vectors[layer, 3:4, :],
        r.wu_here, r.wd_here, r.slope_here, r.down_rows, r.slope_here, r.grad_hidden,
        add_small, add_up, r.own,
        ready=ready_mlp, made=mlp_made, tick=folds.tick,
    )
    gather.finish()
    scatter.finish()
    gather = Gather(ring, r.attn_rows, r.gather_sems.at[1])
    scatter = Scatter(ring, r.stage, r.land.at[1], r.scatter_sems.at[1])

    def out_ready():
        loads["wo"].wait()

    def gathered():
        loads["context"].wait()
        r.part_o[...] = mm_a(r.context_here[...], r.attn_rows[...]).astype(BF16)
        make_fold("o", layer, OUT, r.part_o, r.go, O_)

    def attn_ready():
        loads["proj"].wait()
        loads["wq"].wait()

    def attn_made():
        normed_load.wait()
        for part in range(3):
            for start in range(0, width, block):
                at = pl.ds(start, block)
                made = mm_a(r.activated_here[:, at], r.grad_proj[part]).astype(BF16)
                r.part_q[part, at] = made
        r.small[7:8, 0:local] = jnp.sum(r.grad_proj[0].astype(F32), axis=0, keepdims=True)
        r.small[7:8, local : 2 * local] = jnp.sum(r.grad_proj[2].astype(F32), axis=0, keepdims=True)
        if not top:
            make_fold("q", layer, QKV, r.part_q, r.gq, Q_)

    attention_backward_body(
        ring, gather, scatter, r.grad_hidden, r.x, lambda: r.vectors[layer, 0:1, :],
        r.wq_here, r.wo_here, r.slopes, r.proj_here, r.totals, r.attn_rows, r.grad_proj,
        r.grad_hidden, add_small, r.grad_context, r.sums, r.penalty,
        out_ready=out_ready, ready=attn_ready, gathered=gathered, made=attn_made, tick=folds.tick,
    )
    gather.finish()
    scatter.finish()
    if top:
        folds.finish()
        for s in range(2):

            @pl.when(section == s)
            def _():
                passing(r.act1 if s == 0 else r.act0, r.acts_out.at[s], 0).wait_send()
                passing(r.act0, r.acts_out.at[1 - s], 0).wait_recv()

        return

    @pl.when(section == 0)
    def _():
        r.small_go[0] = r.small_in[...]
        r.small_keep[...] = r.small[...]

    @pl.when(section == 1)
    def _():
        r.small_go[0] = r.small[...]
        r.small_keep[...] = r.small_in[...]
        r.rounded[...] = r.grad_hidden[...].astype(BF16)
        passing(r.rounded, r.grads_land, 0).start()

    small_pass = passing(r.small_go.at[0], r.small_land.at[0], 1)
    small_pass.start()
    folds.round()
    small_pass.wait()
    r.small_go[1] = r.small_keep[...] + r.small_land[0]

    def to_place(there, slot, sem):
        return pltpu.make_async_remote_copy(
            src_ref=r.small_go.at[1], dst_ref=r.small_land.at[slot], send_sem=r.small_sems.at[0, sem],
            recv_sem=r.small_sems.at[1, slot], device_id={DP: there}, device_id_type=MESH,
        )

    for there in range(count):

        @pl.when(there != place)
        def _():
            to_place(there, 1 + place, 1 + there).start()

    r.small_land[1 + place] = r.small_go[1]
    folds.round()
    for there in range(count):

        @pl.when(there != place)
        def _():
            to_place(there, 1 + there, 1 + there).wait_recv()
            to_place(there, 1 + place, 1 + there).wait_send()

    total = r.small_land[1]
    for there in range(1, count):
        total += r.small_land[1 + there]
    r.small_go[2] = total
    for step, device in enumerate((ring.mate, ring.peer)):
        hop = pltpu.make_async_remote_copy(
            src_ref=r.small_go.at[2 + step], dst_ref=r.small_land.at[1 + count + step],
            send_sem=r.small_sems.at[0, 1 + count + step], recv_sem=r.small_sems.at[1, 1 + count + step],
            device_id={TENSOR: device}, device_id_type=MESH,
        )
        hop.start()
        folds.round()
        hop.wait()
        r.small_go[3 + step] = r.small_go[2 + step] + r.small_land[1 + count + step]
    r.small_out[0:6] = r.small_go[4, 0:6]
    r.small_out[6:8] = total[6:8]

    folds.finish()
    for copy in kept:

        @pl.when(section == 1)
        def _():
            copy.wait()

    grads_pass = passing(r.rounded, r.grads_land, 0)
    grads_pass.wait()
    for s in range(2):

        @pl.when(section == s)
        def _():
            if s == 0:
                r.grads_out[0] = r.grad_hidden[...]
            r.grads_out[1 - s] = r.grads_land[...].astype(F32)


def mm_a(left, right):
    return lax.dot_general(left, right, (((0,), (0,)), ((), ())), preferred_element_type=F32)


def backward_call(layer, top, values, slopes):
    count = lax.axis_size(DP)
    block, width = values["x"].shape
    length = block * lax.axis_size(TENSOR)
    local, units = values["wo"].shape[0], values["wd"].shape[0]
    vmem, far = pl.BlockSpec(memory_space=pltpu.VMEM), pl.BlockSpec(memory_space=pl.ANY)
    ins = ["middle", "x", "totals", "vectors", "slopes"]
    ins_far = ["wd", "wu", "wo", "wq", "slope", "activated", "second", "normed", "proj", "context"]
    outs = [("grad_hidden", (block, width), F32), ("small", (8, width), F32)]
    shards = [
        ("gu", fold_shapes(UP, count, width, local, units)[2], F32),
        ("gd", fold_shapes(DOWN, count, width, local, units)[2], F32),
        ("go", fold_shapes(OUT, count, width, local, units)[2], F32),
    ]
    whole = {kind: fold_shapes(kind, count, width, local, units)[0] for kind in range(4)}
    if top:
        ins += ["incoming", "act0", "act1"]
        outs += shards + [("part_q", whole[QKV], BF16), ("acts_out", (2, block, width), BF16)]
    else:
        ins += ["small_in"]
        ins_far += ["incoming", "gu_in", "gd_in", "go_in", "q1"]
        outs += shards + [
            ("gq", fold_shapes(QKV, count, width, local, units)[2], F32),
            ("small_out", (8, width), F32),
            ("grads_out", (2, block, width), F32),
        ]
    dma = pltpu.SemaphoreType.DMA
    scratch = dict(
        wd_here=pltpu.VMEM((units, width), BF16),
        wu_here=pltpu.VMEM((width, units), BF16),
        wo_here=pltpu.VMEM((local, width), BF16),
        wq_here=pltpu.VMEM((3, width, local), BF16),
        slope_here=pltpu.VMEM((length, units), BF16),
        activated_here=pltpu.VMEM((length, units), BF16),
        second_here=pltpu.VMEM((length, width), BF16),
        proj_here=pltpu.VMEM((3, length, local), BF16),
        context_here=pltpu.VMEM((length, local), BF16),
        down_rows=pltpu.VMEM((length, width), BF16),
        attn_rows=pltpu.VMEM((length, width), BF16),
        grad_proj=pltpu.VMEM((3, length, local), BF16),
        grad_context=pltpu.VMEM((length, local), BF16),
        sums=pltpu.VMEM((2, length, PAIR), F32),
        penalty=pltpu.VMEM((length, LANES), F32),
        own=pltpu.VMEM((block, width), F32),
        stage=pltpu.VMEM((3, block, width), BF16),
        land=pltpu.VMEM((2, 3, block, width), BF16),
        gather_sems=dma((2, 2, 3, CHUNKS)),
        scatter_sems=dma((2, 2, 3, CHUNKS)),
        load_sems=dma((12,)),
        pass_sems=dma((2, 2)),
        first_sems=dma((2, 5, count)),
        line_sems=dma((2, 5, count, 2)),
        end_sems=dma((2, 5)),
        part_d=pltpu.VMEM(whole[DOWN], BF16),
        part_u=pltpu.VMEM(whole[UP], BF16),
        part_o=pltpu.VMEM(whole[OUT], BF16),
    )
    keys = {"d": DOWN, "u": UP, "o": OUT}
    if not top:
        keys.update({"q": QKV, "q1": QKV})
        scratch.update(
            part_q=pltpu.VMEM(whole[QKV], BF16),
            q1_here=pltpu.VMEM(whole[QKV], BF16),
            rounded=pltpu.VMEM((block, width), BF16),
            grads_land=pltpu.VMEM((block, width), BF16),
            small_go=pltpu.VMEM((5, 8, width), F32),
            small_keep=pltpu.VMEM((8, width), F32),
            small_land=pltpu.VMEM((3 + count, 8, width), F32),
            small_sems=dma((2, 3 + count)),
            keep_sems=dma((3,)),
        )
    for key, kind in keys.items():
        half = fold_shapes(kind, count, width, local, units)[1]
        scratch["first_" + key] = pltpu.VMEM((count,) + half, BF16)
        scratch["line_" + key] = pltpu.VMEM((count + 1,) + half, BF16)
        scratch["last_" + key] = pltpu.VMEM(half, BF16)
    values = dict(values, slopes=slopes)
    names = ins + ins_far + [item[0] for item in outs] + list(scratch)
    made = pl.pallas_call(
        functools.partial(backward_kernel, layer, top, names, None),
        out_shape=[jax.ShapeDtypeStruct(shape, dtype) for _, shape, dtype in outs],
        in_specs=[vmem] * len(ins) + [far] * len(ins_far),
        out_specs=[vmem] * len(outs),
        scratch_shapes=list(scratch.values()),
        compiler_params=pltpu.CompilerParams(
            collective_id=6 + layer, has_side_effects=True, vmem_limit_bytes=VMEM_LIMIT
        ),
        name="backward_%d" % layer,
    )(*[values[name] for name in ins + ins_far])
    return {item[0]: value for item, value in zip(outs, made)}


def swapped(value):
    count = lax.axis_size(SECTION)
    return lax.ppermute(value, SECTION, [(i, (i + 1) % count) for i in range(count)])


def backward_near(incoming, acts, saved, layers, vectors, slopes, local):
    def values(l, **more):
        w, s = layers[l], saved[l]
        return dict(
            middle=s["middle"], x=s["x"], totals=s["totals"], vectors=vectors, slope=s["slope_of"],
            activated=s["activated"], second=s["second"], normed=s["normed"], proj=s["proj"],
            context=s["context"], wd=w["down"], wu=w["up"], wo=w["out"], wq=w["qkv"], **more,
        )

    high = backward_call(1, True, values(1, incoming=incoming, act0=acts[0], act1=acts[1]), slopes)
    low = backward_call(
        0,
        False,
        values(
            0, incoming=high["grad_hidden"], small_in=high["small"], gu_in=high["gu"],
            gd_in=high["gd"], go_in=high["go"], q1=high["part_q"],
        ),
        slopes,
    )
    places = lax.axis_size(DP)
    tensor, place = lax.axis_index(TENSOR), lax.axis_index(DP)
    small = low["small_out"]
    width = small.shape[1]
    share = width // (lax.axis_size(TENSOR) * places)
    vector = lax.dynamic_slice_in_dim(small[:6], (tensor * places + place) * share, share, axis=1)
    up_share, qv_share = width // places, local // places
    up = lax.dynamic_slice_in_dim(small[6], place * up_share, up_share)
    qv = lax.dynamic_slice_in_dim(
        small[7, : 2 * local].reshape(2, local), place * qv_share, qv_share, axis=1
    )
    return (
        high["acts_out"][None],
        low["grads_out"][None],
        vector[0][None],
        vector[1][None],
        jnp.transpose(low["gq"], (1, 0, 2))[None],
        qv[None],
        low["go"][None],
        vector[2][None],
        vector[3][None],
        vector[4][None],
        low["gu"][None],
        up[None],
        low["gd"][None],
        vector[5][None],
    )


def near_shards(depth, block):
    return depth % 256 == 0 and block % 256 == 0


def gathered_layers(section, layer_count, w_qkv, w_out, w_up, w_down, small_ones):
    def both(value):
        other = swapped(value)
        return [jnp.where(section == l, value, other) for l in range(layer_count)]

    def over_dp(value, axis):
        return both(lax.all_gather(value, DP, axis=axis, tiled=True))

    qkv_all, up_all = over_dp(jnp.transpose(w_qkv[0], (1, 0, 2)), 1), over_dp(w_up[0], 0)
    out_all, down_all = over_dp(w_out[0], 1), over_dp(w_down[0], 1)
    vectors = [
        both(item[0]) for item in small_ones
    ]
    layers = []
    for l in range(layer_count):
        gain1, bias1, qv, bout, gain2, bias2, bup, bdown = [item[l] for item in vectors]
        layers.append(
            dict(
                ln1_gain=gain1,
                ln1_bias=bias1,
                ln2_gain=gain2,
                ln2_bias=bias2,
                qkv=qkv_all[l],
                out=out_all[l],
                up=up_all[l],
                down=down_all[l],
                b_qkv=jnp.stack([qv[0], jnp.zeros_like(qv[0]), qv[1]])[:, None, :],
                b_out=bout,
                b_up=bup,
                b_down=bdown,
            )
        )
    return layers


def per_device(
    inputs,
    out_grad,
    lang_ids,
    lang_weights,
    ln1_gain,
    ln1_bias,
    w_qkv,
    b_qv,
    w_out,
    b_out,
    ln2_gain,
    ln2_bias,
    w_up,
    b_up,
    w_down,
    b_down,
):
    section = lax.axis_index(SECTION)
    layer_count = lax.axis_size(SECTION)
    local_heads = w_qkv.shape[3] // HEAD
    head_ids = lax.axis_index(TENSOR) * local_heads + jnp.arange(local_heads, dtype=jnp.int32)
    slopes = jnp.exp2(-8.0 * (head_ids.astype(jnp.float32) + 1.0) / HEADS)
    slopes = jnp.broadcast_to(slopes[:, None], (local_heads, inputs.shape[1]))

    row = lax.dynamic_index_in_dim(inputs, section, 0, keepdims=False)
    target = lax.dynamic_index_in_dim(out_grad, section, 0, keepdims=False)
    lang = lax.dynamic_index_in_dim(lang_ids, section, 0, keepdims=False)
    matches = lang == jnp.arange(lang_weights.shape[0], dtype=jnp.int32)
    scale = jnp.sum(jnp.where(matches, lang_weights, 0)).astype(jnp.float32) / 64.0

    if near_shards(w_qkv[0].shape[0], inputs.shape[1]):
        vector = jnp.stack(
            [item[0] for item in (ln1_gain, ln1_bias, b_out, ln2_gain, ln2_bias)]
            + [b_up[0], b_down[0], jnp.pad(b_qv[0].reshape(-1), (0, b_out.shape[1] - 2 * b_qv.shape[2]))]
        )
        shards = (jnp.transpose(w_qkv[0], (1, 0, 2)), w_out[0], w_up[0], w_down[0])
        acts, saved, layers, vectors = forward_call(row, vector, shards, slopes)
        return backward_near(
            target.astype(F32) * scale, acts, saved, layers, vectors, slopes, b_qv.shape[2]
        )
    else:
        layers = gathered_layers(
            section, layer_count, w_qkv, w_out, w_up, w_down,
            (ln1_gain, ln1_bias, b_qv, b_out, ln2_gain, ln2_bias, b_up, b_down),
        )
        acts, saved = [], []
        for l in range(layer_count):
            row, kept = layer_forward(row, layers[l], slopes)
            acts.append(row)
            saved.append(kept)
    grads, small, large = [None] * layer_count, [None] * layer_count, [None] * layer_count
    incoming = target.astype(jnp.float32) * scale
    for l in reversed(range(layer_count)):
        grads[l], small[l], large[l] = layer_backward(
            incoming, layers[l], saved[l], slopes
        )
        incoming = grads[l].astype(jnp.bfloat16).astype(jnp.float32)

    def mine(items):
        return jnp.where(section == 0, items[0], items[1])

    def theirs(items):
        return jnp.where(section == 0, items[1], items[0])

    def rows_of(items):
        own, other = mine(items), swapped(theirs(items))
        return jnp.stack([jnp.where(section == r, own, other) for r in range(layer_count)])[None]

    def reduced(name, axis):
        items = [item[name].astype(jnp.bfloat16) for item in large]
        total = mine(items) + swapped(theirs(items))
        return lax.psum_scatter(total, DP, scatter_dimension=axis, tiled=True).astype(
            jnp.float32
        )[None]

    small_total = mine(small) + swapped(theirs(small))
    small_shards = lax.psum_scatter(small_total, (TENSOR, DP), scatter_dimension=1, tiled=True)
    return (
        rows_of(acts),
        rows_of([item.astype(jnp.bfloat16) for item in grads]).astype(jnp.float32),
        small_shards[0][None],
        small_shards[1][None],
        jnp.transpose(reduced("qkv", 1), (0, 2, 1, 3)),
        reduced("b_qv", 1),
        reduced("out", 1),
        small_shards[2][None],
        small_shards[3][None],
        small_shards[4][None],
        reduced("up", 0),
        reduced("b_up", 0),
        reduced("down", 1),
        small_shards[5][None],
    )


def solution(mesh):
    return jax.shard_map(
        per_device,
        mesh=mesh,
        in_specs=(
            P(DP, TENSOR, None),
            P(DP, TENSOR, None),
            P(DP),
            P(),
            P(SECTION, None),
            P(SECTION, None),
            P(SECTION, DP, None, TENSOR),
            P(SECTION, None, TENSOR),
            P(SECTION, TENSOR, DP),
            P(SECTION, None),
            P(SECTION, None),
            P(SECTION, None),
            P(SECTION, DP, TENSOR),
            P(SECTION, TENSOR),
            P(SECTION, TENSOR, DP),
            P(SECTION, None),
        ),
        out_specs=(
            P(SECTION, DP, TENSOR, None),
            P(SECTION, DP, TENSOR, None),
            P(SECTION, (TENSOR, DP)),
            P(SECTION, (TENSOR, DP)),
            P(SECTION, DP, None, TENSOR),
            P(SECTION, None, (TENSOR, DP)),
            P(SECTION, TENSOR, DP),
            P(SECTION, (TENSOR, DP)),
            P(SECTION, (TENSOR, DP)),
            P(SECTION, (TENSOR, DP)),
            P(SECTION, DP, TENSOR),
            P(SECTION, (TENSOR, DP)),
            P(SECTION, TENSOR, DP),
            P(SECTION, (TENSOR, DP)),
        ),
        check_vma=False,
    )
```

```python
import functools

import jax
import jax.numpy as jnp
from jax import lax
from jax.experimental import pallas as pl
from jax.experimental.pallas import tpu as pltpu
from jax.sharding import PartitionSpec as P

HEADS = 16
HEAD = 64
PAIR = 2 * HEAD

EPSILON = 1e-05
GELU_SCALE = 0.7978845608028654

SECTION, TENSOR, DP = "section", "tensor", "dp"
MESH = pl.DeviceIdType.MESH
F32 = jnp.float32
BF16 = jnp.bfloat16
CHUNKS = 2
LANES = 128
VMEM_LIMIT = 61 * 1024 * 1024


def rows_at(start, size):
    return pl.ds(pl.multiple_of(start, size), size)


def mm(left, right):
    return lax.dot_general(left, right, (((1,), (0,)), ((), ())), preferred_element_type=F32)


def mm_t(left, right):
    return lax.dot_general(left, right, (((1,), (1,)), ((), ())), preferred_element_type=F32)


class Ring:
    def __init__(self, block):
        self.block = block
        self.chunk = block // CHUNKS
        self.me = lax.axis_index(TENSOR)
        core, chip = lax.rem(self.me, 2), self.me // 2
        self.mate = self.me + 1 - 2 * core
        self.peer = self.me + 2 - 4 * chip
        self.far = self.peer + 1 - 2 * core

    def greet(self):
        barrier = pltpu.get_barrier_semaphore()
        for other in (self.mate, self.peer):
            pl.semaphore_signal(barrier, inc=1, device_id={TENSOR: other}, device_id_type=MESH)
        pl.semaphore_wait(barrier, 2)

    def rows(self, owner, c):
        return rows_at(owner * self.block + c * self.chunk, self.chunk)

    def send(self, src, dst, sems, kind, c, other):
        return pltpu.make_async_remote_copy(
            src_ref=src,
            dst_ref=dst,
            send_sem=sems.at[0, kind, c],
            recv_sem=sems.at[1, kind, c],
            device_id={TENSOR: other},
            device_id_type=MESH,
        )


class Gather:
    def __init__(self, ring, every, sems):
        self.ring, self.every, self.sems = ring, every, sems

    def copy(self, kind, owner, c):
        ring = self.ring
        at = self.every.at[ring.rows(owner, c)]
        return ring.send(at, at, self.sems, kind, c, ring.peer if kind == 1 else ring.mate)

    def start(self, c):
        self.copy(1, self.ring.me, c).start()
        self.copy(0, self.ring.me, c).start()

    def arrived_mate(self, c):
        self.copy(0, self.ring.mate, c).wait_recv()

    def arrived_peer(self, c):
        self.copy(1, self.ring.peer, c).wait_recv()
        self.copy(2, self.ring.peer, c).start()

    def arrived_far(self, c):
        self.copy(2, self.ring.far, c).wait_recv()

    def finish(self):
        for c in range(CHUNKS):
            for kind, owner in ((0, self.ring.me), (1, self.ring.me), (2, self.ring.peer)):
                self.copy(kind, owner, c).wait_send()


class Scatter:
    def __init__(self, ring, stage, land, sems):
        self.ring, self.stage, self.land, self.sems = ring, stage, land, sems

    def copy(self, kind, c):
        ring = self.ring
        at = pl.ds(c * ring.chunk, ring.chunk)
        return ring.send(
            self.stage.at[kind, at],
            self.land.at[kind, at],
            self.sems,
            kind,
            c,
            ring.peer if kind == 1 else ring.mate,
        )

    def put(self, kind, c, value):
        self.stage[kind, pl.ds(c * self.ring.chunk, self.ring.chunk)] = value.astype(BF16)
        self.copy(kind, c).start()

    def take(self, kind, c):
        self.copy(kind, c).wait_recv()
        return self.land[kind, pl.ds(c * self.ring.chunk, self.ring.chunk)].astype(F32)

    def to_peer(self, c, far_part, peer_part):
        self.put(0, c, far_part)
        self.put(1, c, peer_part + self.take(0, c))

    def finish(self):
        for kind in range(3):
            for c in range(CHUNKS):
                self.copy(kind, c).wait_send()


def normalize(values):
    center = values - jnp.mean(values, axis=-1, keepdims=True)
    scale = lax.rsqrt(jnp.mean(center * center, axis=-1, keepdims=True) + EPSILON)
    return center * scale, scale


def norm_pull(values, gain, grad):
    unit, scale = normalize(values)
    scaled = grad * gain
    pulled = scale * (
        scaled
        - jnp.mean(scaled, axis=-1, keepdims=True)
        - unit * jnp.mean(scaled * unit, axis=-1, keepdims=True)
    )
    return pulled, jnp.sum(grad * unit, axis=0, keepdims=True), jnp.sum(grad, axis=0, keepdims=True)


def scores_of(keys, queries, slope, penalty_ref, start):
    stop, count = keys.shape[0], queries.shape[0]
    scores = mm_t(keys, queries) + slope * jnp.concatenate([penalty_ref[:stop]] * (count // LANES), axis=1)
    last = scores[start:]
    allowed = lax.broadcasted_iota(jnp.int32, (count, count), 0) <= lax.broadcasted_iota(
        jnp.int32, (count, count), 1
    )
    last = jnp.where(allowed, last, -1e30)
    return last if start == 0 else jnp.concatenate([scores[:start], last], axis=0)


def head_mask(value, which):
    lane = lax.broadcasted_iota(jnp.int32, value.shape, 1)
    inside = lane < HEAD if which == 0 else lane >= HEAD
    return jnp.where(inside, value, jnp.zeros_like(value))


def fill_penalty(penalty_ref):
    penalty_ref[...] = lax.broadcasted_iota(jnp.int32, penalty_ref.shape, 0).astype(F32)


def nothing(point=0):
    pass


def attend_forward(proj, context, totals, slopes, penalty, block, tick=nothing):
    length, width = context.shape
    for pair in range(width // PAIR):
        lanes = pl.ds(pair * PAIR, PAIR)
        for start in range(0, length, block):
            tick(pair * 4 + start // block)
            stop = start + block
            queries = proj[0, start:stop, lanes] * jnp.asarray(0.125, BF16)
            keys = proj[1, :stop, lanes]
            values_t = proj[2, :stop, lanes].T
            outs = []
            for which in range(2):
                head = pair * 2 + which
                slope = slopes[pl.ds(head, 1), :]
                scores = scores_of(keys, head_mask(queries, which), slope, penalty, start)
                highest = jnp.max(scores, axis=0, keepdims=True)
                grown = jnp.exp(scores - highest)
                total = jnp.sum(grown, axis=0, keepdims=True)
                mixed = mm(values_t[which * HEAD : (which + 1) * HEAD], grown.astype(BF16))
                outs.append(mixed / total)
                totals[pl.ds(head, 1), start:stop] = highest + jnp.log(total)
            context[start:stop, lanes] = jnp.concatenate(outs, axis=0).T.astype(BF16)


def attend_backward(proj, grad_context, totals, slopes, penalty, grad_proj, sums, block, tick=nothing):
    length, width = grad_context.shape
    for pair in range(width // PAIR):
        lanes = pl.ds(pair * PAIR, PAIR)
        for start in range(0, length, block):
            tick(pair * 4 + start // block)
            stop = start + block
            queries = proj[0, start:stop, lanes] * jnp.asarray(0.125, BF16)
            keys = proj[1, :stop, lanes]
            keys_t = keys.T
            values = proj[2, :stop, lanes]
            grads = grad_context[start:stop, lanes]
            outs = []
            for which in range(2):
                head = pair * 2 + which
                slope = slopes[pl.ds(head, 1), :]
                one_query = head_mask(queries, which)
                one_grad = head_mask(grads, which)
                scores = scores_of(keys, one_query, slope, penalty, start)
                probs = jnp.exp(scores - totals[pl.ds(head, 1), start:stop])
                pulled = probs * mm_t(values, one_grad)
                inner = jnp.sum(pulled, axis=0, keepdims=True)
                grad_scores = (pulled - probs * inner).astype(BF16)
                outs.append(mm(keys_t[which * HEAD : (which + 1) * HEAD], grad_scores) * 0.125)
                grad_keys = mm(grad_scores, one_query)
                grad_values = mm(probs.astype(BF16), one_grad)
                if which == 0:
                    first_keys, first_values = grad_keys, grad_values
                else:
                    grad_keys, grad_values = grad_keys + first_keys, grad_values + first_values
            grad_proj[0, start:stop, lanes] = jnp.concatenate(outs, axis=0).T.astype(BF16)
            if start > 0:
                sums[0, :start] += grad_keys[:start]
                sums[1, :start] += grad_values[:start]
            sums[0, start:stop] = grad_keys[start:]
            sums[1, start:stop] = grad_values[start:]
        grad_proj[1, :, lanes] = sums[0].astype(BF16)
        grad_proj[2, :, lanes] = sums[1].astype(BF16)


def attention_forward_body(
    ring, gather, scatter, x, gain, shift, w_qkv, b_qkv, w_out, b_out, slopes,
    normed, proj, context, totals, middle, penalty,
    qkv_ready=nothing, out_ready=nothing, tick=nothing,
):
    block, chunk = ring.block, ring.chunk
    for c in range(CHUNKS):
        at = pl.ds(c * chunk, chunk)
        unit, _ = normalize(x[at].astype(F32))
        normed[ring.rows(ring.me, c)] = (unit * gain() + shift()).astype(BF16)
        gather.start(c)
    qkv_ready()

    def project(owner, c, size):
        at = rows_at(owner * block + c * chunk, size)
        rows = normed[at]
        for part in range(3):
            made = mm(rows, w_qkv[part])
            proj[part, at] = (made if part == 1 else made + b_qkv(part)).astype(BF16)

    project(ring.me, 0, block)
    for c in range(CHUNKS):
        gather.arrived_mate(c)
    project(ring.mate, 0, block)
    for c in range(CHUNKS):
        gather.arrived_peer(c)
        project(ring.peer, c, chunk)
        gather.arrived_far(c)
        project(ring.far, c, chunk)
    attend_forward(proj, context, totals, slopes, penalty, block, tick)
    out_ready()

    def part_of(owner, c):
        return mm(context[ring.rows(owner, c)], w_out[...])

    for c in range(CHUNKS):
        scatter.put(0, c, part_of(ring.far, c))
        scatter.put(1, c, part_of(ring.peer, c) + scatter.take(0, c))
        tick(8 + c)
    for c in range(CHUNKS):
        scatter.put(2, c, part_of(ring.mate, c))
    tick(10)
    for c in range(CHUNKS):
        at = pl.ds(c * chunk, chunk)
        total = part_of(ring.me, c) + scatter.take(2, c) + scatter.take(1, c)
        middle[at] = x[at].astype(F32) + total + b_out()


def mlp_forward_body(
    ring, gather, scatter, middle, gain, shift, w_up, b_up, w_down, b_down,
    second, activated, slope_of, leaving, own,
    ready=nothing, tick=nothing,
):
    block, chunk = ring.block, ring.chunk
    for c in range(CHUNKS):
        at = pl.ds(c * chunk, chunk)
        unit, _ = normalize(middle[at])
        second[ring.rows(ring.me, c)] = (unit * gain() + shift()).astype(BF16)
        gather.start(c)

    def expand(at):
        upward = mm(second[at], w_up[...]) + b_up()
        inner = jnp.tanh(GELU_SCALE * (upward + 0.044715 * upward * upward * upward))
        half = 0.5 * (1.0 + inner)
        value = upward * half
        slope = half + 0.5 * upward * (1.0 - inner * inner) * GELU_SCALE * (
            1.0 + 3 * 0.044715 * upward * upward
        )
        value = value.astype(BF16)
        activated[at] = value
        slope_of[at] = slope.astype(BF16)
        return mm(value, w_down[...])

    tick(11)
    ready()
    own[...] = expand(rows_at(ring.me * block, block))
    tick(12)
    for c in range(CHUNKS):
        gather.arrived_mate(c)
    part = expand(rows_at(ring.mate * block, block))
    for c in range(CHUNKS):
        scatter.put(2, c, part[c * chunk : (c + 1) * chunk])
    tick(13)
    for c in range(CHUNKS):
        gather.arrived_peer(c)
        peer_part = expand(ring.rows(ring.peer, c))
        gather.arrived_far(c)
        scatter.put(0, c, expand(ring.rows(ring.far, c)))
        scatter.put(1, c, peer_part + scatter.take(0, c))
        tick(14 + c)
    for c in range(CHUNKS):
        at = pl.ds(c * chunk, chunk)
        total = own[at] + scatter.take(2, c) + scatter.take(1, c)
        leaving[at] = (middle[at] + total + b_down()).astype(BF16)


def attention_forward_kernel(
    x, gain, shift, w_qkv, b_qkv, w_out, b_out, slopes,
    normed, proj, context, totals, middle,
    penalty, stage, land, gather_sems, scatter_sems,
):
    ring = Ring(x.shape[0])
    ring.greet()
    gather = Gather(ring, normed, gather_sems)
    scatter = Scatter(ring, stage, land, scatter_sems)
    fill_penalty(penalty)
    attention_forward_body(
        ring, gather, scatter, x, lambda: gain[...], lambda: shift[...], w_qkv,
        lambda part: b_qkv[part], w_out, lambda: b_out[...], slopes,
        normed, proj, context, totals, middle, penalty,
    )
    gather.finish()
    scatter.finish()


def mlp_forward_kernel(
    middle, gain, shift, w_up, b_up, w_down, b_down,
    second, activated, slope_of, leaving,
    own, stage, land, gather_sems, scatter_sems,
):
    ring = Ring(middle.shape[0])
    ring.greet()
    gather = Gather(ring, second, gather_sems)
    scatter = Scatter(ring, stage, land, scatter_sems)
    mlp_forward_body(
        ring, gather, scatter, middle, lambda: gain[...], lambda: shift[...], w_up,
        lambda: b_up[...], w_down, lambda: b_down[...],
        second, activated, slope_of, leaving, own,
    )
    gather.finish()
    scatter.finish()


def mlp_backward_body(
    ring, gather, scatter, incoming, middle, gain, w_up, w_down, slope_of,
    down_rows, grad_up, grad_middle, small, up_sum, own,
    ready=nothing, made=nothing, tick=nothing,
):
    block, chunk = ring.block, ring.chunk
    for c in range(CHUNKS):
        down_rows[ring.rows(ring.me, c)] = incoming[pl.ds(c * chunk, chunk)].astype(BF16)
        gather.start(c)
    ready()

    def pull(at):
        grad = mm_t(down_rows[at], w_down[...]) * slope_of[at].astype(F32)
        grad = grad.astype(BF16)
        grad_up[at] = grad
        up_sum(jnp.sum(grad.astype(F32), axis=0, keepdims=True))
        return mm_t(grad, w_up[...])

    own[...] = pull(rows_at(ring.me * block, block))
    tick(0)
    for c in range(CHUNKS):
        gather.arrived_mate(c)
    part = pull(rows_at(ring.mate * block, block))
    for c in range(CHUNKS):
        scatter.put(2, c, part[c * chunk : (c + 1) * chunk])
    tick(1)
    for c in range(CHUNKS):
        gather.arrived_peer(c)
        peer_part = pull(ring.rows(ring.peer, c))
        gather.arrived_far(c)
        scatter.put(0, c, pull(ring.rows(ring.far, c)))
        scatter.put(1, c, peer_part + scatter.take(0, c))
        tick(2 + c)
    made()
    tick(4)
    for c in range(CHUNKS):
        at = pl.ds(c * chunk, chunk)
        total = own[at] + scatter.take(2, c) + scatter.take(1, c)
        pulled, grad_gain, grad_shift = norm_pull(middle[at], gain(), total)
        before = incoming[at].astype(F32)
        after = before + pulled
        grad_middle[at] = after
        small(2, jnp.sum(after, axis=0, keepdims=True))
        small(3, grad_gain)
        small(4, grad_shift)
        small(5, jnp.sum(before, axis=0, keepdims=True))
        tick(5 + c)


def attention_backward_body(
    ring, gather, scatter, grad_middle, x, gain, w_qkv, w_out, slopes, proj, totals,
    attn_rows, grad_proj, grad_hidden, small, grad_context, sums, penalty,
    out_ready=nothing, ready=nothing, gathered=nothing, made=nothing, tick=nothing,
):
    block, chunk = ring.block, ring.chunk
    for c in range(CHUNKS):
        attn_rows[ring.rows(ring.me, c)] = grad_middle[pl.ds(c * chunk, chunk)].astype(BF16)
        gather.start(c)
    out_ready()

    def pull(at):
        grad_context[at] = mm_t(attn_rows[at], w_out[...]).astype(BF16)

    pull(rows_at(ring.me * block, block))
    for c in range(CHUNKS):
        gather.arrived_mate(c)
    pull(rows_at(ring.mate * block, block))
    tick(7)
    for c in range(CHUNKS):
        gather.arrived_peer(c)
        pull(ring.rows(ring.peer, c))
        gather.arrived_far(c)
        pull(ring.rows(ring.far, c))
        tick(8 + c)
    gathered()
    ready()
    attend_backward(proj, grad_context, totals, slopes, penalty, grad_proj, sums, block, lambda at: tick(10 + at))

    def part_of(owner, c):
        at = ring.rows(owner, c)
        total = mm_t(grad_proj[0, at], w_qkv[0])
        for part in range(1, 3):
            total += mm_t(grad_proj[part, at], w_qkv[part])
        return total

    for c in range(CHUNKS):
        scatter.put(0, c, part_of(ring.far, c))
        scatter.put(1, c, part_of(ring.peer, c) + scatter.take(0, c))
    for c in range(CHUNKS):
        scatter.put(2, c, part_of(ring.mate, c))
    made()
    tick(18)
    for c in range(CHUNKS):
        at = pl.ds(c * chunk, chunk)
        total = part_of(ring.me, c) + scatter.take(2, c) + scatter.take(1, c)
        pulled, grad_gain, grad_shift = norm_pull(x[at].astype(F32), gain(), total)
        grad_hidden[at] = grad_middle[at] + pulled
        small(0, grad_gain)
        small(1, grad_shift)
        tick(19 + c)


def mlp_backward_kernel(
    incoming, middle, gain, w_up, w_down, slope_of,
    down_rows, grad_up, grad_middle, small, up_sum,
    own, stage, land, gather_sems, scatter_sems,
):
    ring = Ring(middle.shape[0])
    ring.greet()
    gather = Gather(ring, down_rows, gather_sems)
    scatter = Scatter(ring, stage, land, scatter_sems)
    small[...] = jnp.zeros_like(small)
    up_sum[...] = jnp.zeros_like(up_sum)

    def add_small(i, value):
        small[pl.ds(i, 1)] += value

    def add_up(value):
        up_sum[...] += value

    mlp_backward_body(
        ring, gather, scatter, incoming, middle, lambda: gain[...], w_up, w_down, slope_of,
        down_rows, grad_up, grad_middle, add_small, add_up, own,
    )
    gather.finish()
    scatter.finish()


def attention_backward_kernel(
    grad_middle, x, gain, w_qkv, w_out, slopes, proj, totals,
    attn_rows, grad_proj, grad_hidden, small, qv_sum,
    grad_context, sums, penalty, stage, land, gather_sems, scatter_sems,
):
    ring = Ring(x.shape[0])
    ring.greet()
    gather = Gather(ring, attn_rows, gather_sems)
    scatter = Scatter(ring, stage, land, scatter_sems)
    fill_penalty(penalty)
    small[...] = jnp.zeros_like(small)

    def add_small(i, value):
        small[pl.ds(i, 1)] += value

    attention_backward_body(
        ring, gather, scatter, grad_middle, x, lambda: gain[...], w_qkv, w_out, slopes, proj,
        totals, attn_rows, grad_proj, grad_hidden, add_small, grad_context, sums, penalty,
    )
    qv_sum[...] = jnp.zeros_like(qv_sum)
    qv_sum[0:1] = jnp.sum(grad_proj[0].astype(F32), axis=0, keepdims=True)
    qv_sum[1:2] = jnp.sum(grad_proj[2].astype(F32), axis=0, keepdims=True)
    gather.finish()
    scatter.finish()


def call(kernel, name, number, args, outs, scratch):
    vmem = pl.BlockSpec(memory_space=pltpu.VMEM)
    return pl.pallas_call(
        kernel,
        out_shape=[jax.ShapeDtypeStruct(shape, dtype) for shape, dtype in outs],
        in_specs=[vmem] * len(args),
        out_specs=[vmem] * len(outs),
        scratch_shapes=scratch,
        compiler_params=pltpu.CompilerParams(
            collective_id=number, has_side_effects=True, vmem_limit_bytes=VMEM_LIMIT
        ),
        name=name,
    )(*args)


def link_scratch(block, width):
    return [
        pltpu.VMEM((3, block, width), BF16),
        pltpu.VMEM((3, block, width), BF16),
        pltpu.SemaphoreType.DMA((2, 3, CHUNKS)),
        pltpu.SemaphoreType.DMA((2, 3, CHUNKS)),
    ]


def row_vector(value):
    return value.reshape(1, -1)


def layer_forward(x, w, slopes):
    block, width = x.shape
    length = block * lax.axis_size(TENSOR)
    local = w["out"].shape[0]
    heads = local // HEAD
    normed, proj, context, totals, middle = call(
        attention_forward_kernel,
        "attention_forward",
        1,
        (x, row_vector(w["ln1_gain"]), row_vector(w["ln1_bias"]), w["qkv"], w["b_qkv"], w["out"], row_vector(w["b_out"]), slopes),
        [((length, width), BF16), ((3, length, local), BF16), ((length, local), BF16), ((heads, length), F32), ((block, width), F32)],
        [pltpu.VMEM((length, LANES), F32)] + link_scratch(block, width),
    )
    units = w["up"].shape[1]
    second, activated, slope_of, leaving = call(
        mlp_forward_kernel,
        "mlp_forward",
        2,
        (middle, row_vector(w["ln2_gain"]), row_vector(w["ln2_bias"]), w["up"], row_vector(w["b_up"]), w["down"], row_vector(w["b_down"])),
        [((length, width), BF16), ((length, units), BF16), ((length, units), BF16), ((block, width), BF16)],
        [pltpu.VMEM((block, width), F32)] + link_scratch(block, width),
    )
    saved = dict(x=x, normed=normed, proj=proj, context=context, totals=totals, middle=middle, second=second, activated=activated, slope_of=slope_of)
    return leaving, saved


def layer_backward(incoming, w, s, slopes):
    block, width = incoming.shape
    length = block * lax.axis_size(TENSOR)
    local, units = w["out"].shape[0], w["up"].shape[1]
    down_rows, grad_up, grad_middle, small_a, up_sum = call(
        mlp_backward_kernel,
        "mlp_backward",
        3,
        (incoming, s["middle"], row_vector(w["ln2_gain"]), w["up"], w["down"], s["slope_of"]),
        [((length, width), BF16), ((length, units), BF16), ((block, width), F32), ((8, width), F32), ((1, units), F32)],
        [pltpu.VMEM((block, width), F32)] + link_scratch(block, width),
    )
    attn_rows, grad_proj, grad_hidden, small_b, qv_sum = call(
        attention_backward_kernel,
        "attention_backward",
        4,
        (grad_middle, s["x"], row_vector(w["ln1_gain"]), w["qkv"], w["out"], slopes, s["proj"], s["totals"]),
        [((length, width), BF16), ((3, length, local), BF16), ((block, width), F32), ((8, width), F32), ((8, local), F32)],
        [pltpu.VMEM((length, local), BF16), pltpu.VMEM((2, length, PAIR), F32), pltpu.VMEM((length, LANES), F32)]
        + link_scratch(block, width),
    )
    small = jnp.concatenate([small_b[:2], small_a[2:6]])
    large = dict(
        qkv=jnp.einsum("td,cth->cdh", s["normed"], grad_proj, preferred_element_type=F32),
        out=jnp.einsum("th,td->hd", s["context"], attn_rows, preferred_element_type=F32),
        up=jnp.einsum("td,tf->df", s["second"], grad_up, preferred_element_type=F32),
        down=jnp.einsum("tf,td->fd", s["activated"], down_rows, preferred_element_type=F32),
        b_qv=qv_sum[:2],
        b_up=up_sum[0],
    )
    return grad_hidden, small, large


class Cross:
    def __init__(self, layer, shards, whole, sems):
        self.layer, self.shards, self.whole = layer, shards, whole
        self.first, self.line, self.last, self.local = sems
        self.section, self.place = lax.axis_index(SECTION), lax.axis_index(DP)
        self.count = lax.axis_size(DP)
        self.other = 1 - self.section
        self.owner = self.section == layer
        self.half = jnp.where(self.owner, 0, 1)

    def at(self, i, half, place):
        ref = self.whole[i]
        if i == 0:
            rows = self.shards[i].shape[1] // 2
            return ref.at[:, rows_at((place * 2 + half) * rows, rows), :]
        rows = self.shards[i].shape[0] // 2
        if i == 2:
            return ref.at[rows_at((place * 2 + half) * rows, rows), :]
        return ref.at[rows_at(half * rows, rows), rows_at(place * self.shards[i].shape[1], self.shards[i].shape[1])]

    def mine(self, i, half):
        ref = self.shards[i]
        rows = ref.shape[1 if i == 0 else 0] // 2
        return ref.at[:, pl.ds(half * rows, rows), :] if i == 0 else ref.at[pl.ds(half * rows, rows), :]

    def copy(self, src, dst, sems, where, device):
        return pltpu.make_async_remote_copy(
            src_ref=src,
            dst_ref=dst,
            send_sem=sems.at[(0,) + where],
            recv_sem=sems.at[(1,) + where],
            device_id=device,
            device_id_type=MESH,
        )

    def over_first(self, i):
        return self.copy(
            self.mine(i, 1), self.at(i, 1, self.place), self.first, (i,), {SECTION: self.other}
        )

    def over_last(self, i, place, src=None):
        at = self.at(i, self.half, place)
        return self.copy(at if src is None else src, at, self.last, (i, place), {SECTION: self.other})

    def from_last(self, i, place):
        at = self.at(i, 1 - self.half, place)
        return self.copy(at, at, self.last, (i, place), {SECTION: self.other})

    def along(self, i, place, right, src=None):
        at = self.at(i, self.half, place)
        return self.copy(
            at if src is None else src,
            at,
            self.line,
            (i, place, int(right)),
            {DP: self.place + (1 if right else -1)},
        )

    def onward(self, i, place, right, src=None):
        @pl.when(self.place + 1 < self.count if right else self.place > 0)
        def _():
            self.along(i, place, right, src).start()

    def keep(self, i, half):
        return pltpu.make_async_copy(
            self.mine(i, half), self.at(i, half, self.place), self.local.at[i, half]
        )

    def begin(self, i):
        @pl.when(self.owner)
        def _():
            self.over_first(i).start()
            for right in (True, False):
                self.onward(i, self.place, right, self.mine(i, 0))
            self.over_last(i, self.place, self.mine(i, 0)).start()
            for half in range(2):
                self.keep(i, half).start()

    def start(self, i):
        @pl.when(jnp.logical_not(self.owner))
        def _():
            self.over_first(i).wait_recv()
            for right in (True, False):
                self.onward(i, self.place, right)

    def step(self, i, hops):
        for right in (True, False):
            place = self.place - hops if right else self.place + hops

            @pl.when(place >= 0 if right else place < self.count)
            def _():
                self.along(i, place, right).wait_recv()
                self.over_last(i, place).start()
                self.onward(i, place, right)

    def finish(self, i):
        @pl.when(self.owner)
        def _():
            for half in range(2):
                self.keep(i, half).wait()

        for place in range(self.count):

            @pl.when(jnp.logical_or(jnp.logical_not(self.owner), place != self.place))
            def _():
                self.from_last(i, place).wait_recv()

    def drain(self, i):
        @pl.when(self.owner)
        def _():
            self.over_first(i).wait_send()

        for place in range(self.count):

            @pl.when(jnp.logical_or(self.owner, place != self.place))
            def _():
                self.over_last(i, place).wait_send()

            @pl.when(jnp.logical_and(place <= self.place, self.place + 1 < self.count))
            def _():
                self.along(i, place, True).wait_send()

            @pl.when(jnp.logical_and(place >= self.place, self.place > 0))
            def _():
                self.along(i, place, False).wait_send()


def cross_scratch(layers, count):
    pieces = 4
    return [
        pltpu.SemaphoreType.DMA((layers, 2, pieces)),
        pltpu.SemaphoreType.DMA((layers, 2, pieces, count, 2)),
        pltpu.SemaphoreType.DMA((layers, 2, pieces, count)),
        pltpu.SemaphoreType.DMA((layers, pieces, 2)),
    ]


def greet_all(ring, whole_line=False):
    barrier = pltpu.get_barrier_semaphore()
    section, place, count = lax.axis_index(SECTION), lax.axis_index(DP), lax.axis_size(DP)
    for device in ({TENSOR: ring.mate}, {TENSOR: ring.peer}, {SECTION: 1 - section}):
        pl.semaphore_signal(barrier, inc=1, device_id=device, device_id_type=MESH)
    if whole_line:
        for there in range(count):

            @pl.when(there != place)
            def _():
                pl.semaphore_signal(barrier, inc=1, device_id={DP: there}, device_id_type=MESH)

        pl.semaphore_wait(barrier, 2 + count)
        return

    @pl.when(place > 0)
    def _():
        pl.semaphore_signal(barrier, inc=1, device_id={DP: place - 1}, device_id_type=MESH)

    @pl.when(place + 1 < count)
    def _():
        pl.semaphore_signal(barrier, inc=1, device_id={DP: place + 1}, device_id_type=MESH)

    pl.semaphore_wait(barrier, 3 + jnp.where(place > 0, 1, 0) + jnp.where(place + 1 < count, 1, 0))


AHEAD = 5
PUMP_POINTS = ({3: 6, 6: 7, 9: 8, 11: 9, 12: 10}, {})


class Pump:
    def __init__(self, crossings):
        self.pieces = [(crossing, i) for crossing in crossings for i in range(4)]
        self.hops = crossings[0].count
        self.done = 0
        for crossing, i in self.pieces:
            crossing.begin(i)

    def stage(self, number):
        for hops in range(self.hops):
            if 0 <= number - hops < len(self.pieces):
                crossing, i = self.pieces[number - hops]
                if hops == 0:
                    crossing.start(i)
                else:
                    crossing.step(i, hops)

    def until(self, number):
        while self.done <= min(number, len(self.pieces) + self.hops - 2):
            self.stage(self.done)
            self.done += 1

    def tick(self, layer, point):
        self.until(PUMP_POINTS[layer].get(point, -1))

    def have(self, piece):
        self.until(max(piece + self.hops - 1, AHEAD))
        crossing, i = self.pieces[piece]
        crossing.finish(i)

    def drain(self):
        for crossing, i in self.pieces:
            crossing.drain(i)


KEPT = 6
SMALL_ROWS = 8


def forward_kernel(layers, *refs):
    (x, vector, *shards), refs = refs[:6], refs[6:]
    slopes, refs = refs[0], refs[1:]
    outs, refs = [refs[j * 13 : (j + 1) * 13] for j in range(layers)], refs[13 * layers :]
    vectors, refs = refs[0], refs[1:]
    held, refs = [refs[j * 10 : (j + 1) * 10] for j in range(layers)], refs[10 * layers :]
    penalty, own, stage, land, gather_sems, scatter_sems, save_sems, vector_sems = refs[:8]
    cross_sems = refs[8:]
    ring = Ring(x.shape[0])
    section = lax.axis_index(SECTION)
    greet_all(ring)
    crossings = [
        Cross(l, shards, held[l][6:10], [sem.at[l] for sem in cross_sems]) for l in range(layers)
    ]
    pump = Pump(crossings)
    vector_out = pltpu.make_async_remote_copy(
        src_ref=vector,
        dst_ref=vectors.at[section],
        send_sem=vector_sems.at[0],
        recv_sem=vector_sems.at[1],
        device_id={SECTION: 1 - section},
        device_id_type=MESH,
    )
    vector_in = pltpu.make_async_remote_copy(
        src_ref=vector,
        dst_ref=vectors.at[1 - section],
        send_sem=vector_sems.at[0],
        recv_sem=vector_sems.at[1],
        device_id={SECTION: 1 - section},
        device_id_type=MESH,
    )
    vector_out.start()
    vectors[section] = vector[...]
    fill_penalty(penalty)
    vector_in.wait_recv()
    saves = []

    def save(l, i, src):
        copy = pltpu.make_async_copy(src, outs[l][i], save_sems.at[l, i])
        copy.start()
        saves.append(copy)

    links = []
    entering = x
    for l in range(layers):
        normed, proj, context, second, activated, slope_of, wq, wo, wu, wd = held[l]
        totals, middle, leaving = outs[l][10:13]

        def row(i):
            return lambda: vectors[l, pl.ds(i, 1), :]

        def qv(part):
            local = context.shape[1]
            return vectors[l, pl.ds(7, 1), pl.ds((part // 2) * local, local)]

        def link(every, phase):
            gather = Gather(ring, every, gather_sems.at[phase])
            scatter = Scatter(ring, stage, land.at[phase], scatter_sems.at[phase])
            links.append((gather, scatter))
            return gather, scatter

        def have(i):
            pump.have(l * 4 + i)
            save(l, 6 + i, held[l][6 + i])

        gather, scatter = link(normed, 0)
        attention_forward_body(
            ring, gather, scatter, entering, row(0), row(1), wq, qv, wo, row(2), slopes,
            normed, proj, context, totals, middle, penalty,
            qkv_ready=lambda: have(0), out_ready=lambda: have(1), tick=lambda point, l=l: pump.tick(l, point),
        )
        save(l, 0, normed)
        save(l, 1, proj)
        save(l, 2, context)
        gather.finish()
        scatter.finish()
        gather, scatter = link(second, 1)

        def ready():
            have(2)
            have(3)

        mlp_forward_body(
            ring, gather, scatter, middle, row(3), row(4), wu, row(5), wd, row(6),
            second, activated, slope_of, leaving, own,
            ready=ready, tick=lambda point, l=l: pump.tick(l, point),
        )
        save(l, 3, second)
        save(l, 4, activated)
        save(l, 5, slope_of)
        gather.finish()
        scatter.finish()
        entering = leaving
    vector_out.wait_send()
    pump.drain()
    for copy in saves:
        copy.wait()


def forward_call(x, vector, shards, slopes):
    layers, places = lax.axis_size(SECTION), lax.axis_size(DP)
    block, width = x.shape
    length = block * lax.axis_size(TENSOR)
    sq, so, su, sd = shards
    local, units = so.shape[0], sd.shape[0]
    heads = local // HEAD
    kept = [
        ((length, width), BF16),
        ((3, length, local), BF16),
        ((length, local), BF16),
        ((length, width), BF16),
        ((length, units), BF16),
        ((length, units), BF16),
        ((3, width, local), BF16),
        ((local, width), BF16),
        ((width, units), BF16),
        ((units, width), BF16),
    ]
    near = [((heads, length), F32), ((block, width), F32), ((block, width), BF16)]
    vmem, far = pl.BlockSpec(memory_space=pltpu.VMEM), pl.BlockSpec(memory_space=pl.ANY)
    made = pl.pallas_call(
        functools.partial(forward_kernel, layers),
        out_shape=[jax.ShapeDtypeStruct(shape, dtype) for _ in range(layers) for shape, dtype in kept + near]
        + [jax.ShapeDtypeStruct((layers,) + vector.shape, F32)],
        in_specs=[vmem, vmem] + [far] * 4 + [vmem],
        out_specs=([far] * len(kept) + [vmem] * len(near)) * layers + [vmem],
        scratch_shapes=[pltpu.VMEM(shape, dtype) for _ in range(layers) for shape, dtype in kept]
        + [
            pltpu.VMEM((length, LANES), F32),
            pltpu.VMEM((block, width), F32),
            pltpu.VMEM((3, block, width), BF16),
            pltpu.VMEM((2, 3, block, width), BF16),
            pltpu.SemaphoreType.DMA((2, 2, 3, CHUNKS)),
            pltpu.SemaphoreType.DMA((2, 2, 3, CHUNKS)),
            pltpu.SemaphoreType.DMA((layers, len(kept))),
            pltpu.SemaphoreType.DMA((2,)),
        ]
        + cross_scratch(layers, places),
        compiler_params=pltpu.CompilerParams(
            collective_id=5, has_side_effects=True, vmem_limit_bytes=VMEM_LIMIT
        ),
        name="forward",
    )(x, vector, sq, so, su, sd, slopes)
    saved, weights = [], []
    entering = x
    vectors = made[-1]
    for l in range(layers):
        normed, proj, context, second, activated, slope_of, wq, wo, wu, wd, totals, middle, leaving = made[13 * l : 13 * l + 13]
        saved.append(dict(x=entering, normed=normed, proj=proj, context=context, totals=totals, middle=middle, second=second, activated=activated, slope_of=slope_of))
        weights.append(dict(qkv=wq, out=wo, up=wu, down=wd, ln1_gain=vectors[l, 0], ln2_gain=vectors[l, 3]))
        entering = leaving
    return [made[13 * l + 12] for l in range(layers)], saved, weights, vectors


class Fold:
    def __init__(self, layer, kind, parts, first_land, line_land, last_land, out, sems, number):
        self.kind, self.parts, self.out = kind, parts, out
        self.first_land, self.line_land, self.last_land = first_land, line_land, last_land
        self.first, self.line, self.last = sems
        self.number = number
        self.section, self.place = lax.axis_index(SECTION), lax.axis_index(DP)
        self.count = lax.axis_size(DP)
        self.owner = self.section == layer
        self.half = jnp.where(self.owner, 0, 1)
        self.events = self.count + 2
        self.ran = 0

    def at(self, half, place):
        ref = self.parts
        if self.kind == 0:
            rows = ref.shape[1] // (2 * self.count)
            return ref.at[:, rows_at((place * 2 + half) * rows, rows), :]
        if self.kind == 2:
            rows = ref.shape[0] // (2 * self.count)
            return ref.at[rows_at((place * 2 + half) * rows, rows), :]
        rows, columns = ref.shape[0] // 2, ref.shape[1] // self.count
        return ref.at[rows_at(half * rows, rows), rows_at(place * columns, columns)]

    def out_at(self, half):
        ref = self.out
        rows = ref.shape[1 if self.kind == 0 else 0] // 2
        return ref.at[:, pl.ds(half * rows, rows), :] if self.kind == 0 else ref.at[pl.ds(half * rows, rows), :]

    def copy(self, src, dst, sems, where, device):
        return pltpu.make_async_remote_copy(
            src_ref=src,
            dst_ref=dst,
            send_sem=sems.at[(0, self.number) + where],
            recv_sem=sems.at[(1, self.number) + where],
            device_id=device,
            device_id_type=MESH,
        )

    def over_first(self, place):
        return self.copy(
            self.at(1 - self.half, place),
            self.first_land.at[place],
            self.first,
            (place,),
            {SECTION: 1 - self.section},
        )

    def along(self, place, right, to):
        slot = place if right else jnp.where(place == to, self.count, place)
        return self.copy(
            self.at(self.half, place),
            self.line_land.at[slot],
            self.line,
            (place, int(right)),
            {DP: self.place + (1 if right else -1)},
        )

    def over_last(self):
        return self.copy(
            self.at(self.half, self.place),
            self.last_land,
            self.last,
            (),
            {SECTION: 1 - self.section},
        )

    def begin(self):
        for hops in range(self.count - 1, -1, -1):
            for right in (True, False) if hops else (True,):
                place = self.place + hops if right else self.place - hops

                @pl.when(place < self.count if right else place >= 0)
                def _():
                    self.over_first(place).start()

    def met(self, place):
        self.over_first(place).wait_recv()
        at = self.at(self.half, place)
        at[...] = (at[...].astype(F32) + self.first_land[place].astype(F32)).astype(BF16)

    def took(self, place, right):
        at = self.at(self.half, place)
        self.along(place, right, self.place).wait_recv()
        slot = place if right else jnp.where(place == self.place, self.count, place)
        at[...] = (at[...].astype(F32) + self.line_land[slot].astype(F32)).astype(BF16)

    def event(self):
        hops = self.count - 1 - self.ran
        self.ran += 1
        if hops > 0:
            for right in (True, False):
                place = self.place + hops if right else self.place - hops

                @pl.when(place < self.count if right else place >= 0)
                def _():
                    self.met(place)

                    @pl.when(self.place > 0 if right else self.place + 1 < self.count)
                    def _():
                        self.took(place, right)

                    self.along(place, right, self.place + (1 if right else -1)).start()

        elif hops == 0:
            self.met(self.place)

            @pl.when(self.place > 0)
            def _():
                self.took(self.place, True)

            @pl.when(self.place + 1 < self.count)
            def _():
                self.took(self.place, False)

            @pl.when(self.owner)
            def _():
                self.out_at(0)[...] = self.at(0, self.place)[...].astype(F32)

            @pl.when(jnp.logical_not(self.owner))
            def _():
                self.over_last().start()

        elif hops == -1:

            @pl.when(self.owner)
            def _():
                self.over_last().wait_recv()
                self.out_at(1)[...] = self.last_land[...].astype(F32)

    def drain(self):
        for place in range(self.count):
            self.over_first(place).wait_send()

            @pl.when(jnp.logical_and(place > self.place, self.place + 1 < self.count))
            def _():
                self.along(place, True, self.place + 1).wait_send()

            @pl.when(jnp.logical_and(place < self.place, self.place > 0))
            def _():
                self.along(place, False, self.place - 1).wait_send()

        @pl.when(jnp.logical_not(self.owner))
        def _():
            self.over_last().wait_send()


class Folds:
    def __init__(self, plan):
        self.plan, self.folds, self.begun = plan, {}, []

    def add(self, name, fold):
        self.folds[name] = fold

    def reach(self, name, target):
        fold = self.folds[name]
        if fold not in self.begun:
            fold.begin()
            self.begun.append(fold)
        while fold.ran < min(target, fold.events - 1):
            fold.event()

    def tick(self, point):
        for name, target in self.plan.get(point, ()):
            self.reach(name, target)

    def round(self):
        before = None
        for fold in self.begun:
            if fold.ran < fold.events - 1 and (before is None or fold.ran < before):
                fold.event()
            before = fold.ran if fold.ran < fold.events - 1 else None

    def finish(self):
        while any(fold.ran < fold.events - 1 for fold in self.begun):
            self.round()
        for fold in self.begun:
            fold.drain()


D_, U_, O_, Q_, R_ = range(5)
HIGH_PLAN = {4: ((D_, 0),), 7: ((U_, 0),), 8: ((D_, 1),), 9: ((D_, 2),), 10: ((O_, 0),), 12: ((D_, 3),), 14: ((U_, 1),), 15: ((D_, 4),), 17: ((U_, 2),), 18: ((U_, 3), (O_, 1)), 19: ((U_, 4), (O_, 2)), 20: ((O_, 3),)}
LOW_PLAN = {4: ((R_, 1), (D_, 0)), 5: ((R_, 2),), 6: ((R_, 3),), 7: ((R_, 4), (U_, 0)), 8: ((D_, 1),), 9: ((D_, 2),), 12: ((D_, 3),), 14: ((U_, 1),), 15: ((D_, 4), (O_, 0)), 17: ((U_, 2),), 18: ((U_, 3), (Q_, 0)), 19: ((U_, 4), (O_, 1)), 20: ((O_, 2), (Q_, 1))}


def fold_shapes(kind, count, width, local, units):
    if kind == 0:
        return (3, width, local), (3, width // count // 2, local), (3, width // count, local)
    if kind == 1:
        return (local, width), (local // 2, width // count), (local, width // count)
    if kind == 2:
        return (width, units), (width // count // 2, units), (width // count, units)
    return (units, width), (units // 2, width // count), (units, width // count)


QKV, OUT, UP, DOWN = 0, 1, 2, 3


class Names:
    pass


def take_refs(names, refs):
    bag = Names()
    for name, ref in zip(names, refs, strict=True):
        setattr(bag, name, ref)
    return bag


def backward_kernel(layer, top, names, kinds, *refs):
    r = take_refs(names, refs)
    block, width = r.x.shape
    local, units = r.wo.shape[0], r.wd.shape[0]
    count = lax.axis_size(DP)
    section, place = lax.axis_index(SECTION), lax.axis_index(DP)
    other = 1 - section
    ring = Ring(block)
    greet_all(ring, not top)
    loads = {}
    for number, name in enumerate(("wd", "slope", "wu", "activated", "second", "wo", "proj", "wq", "context")):
        loads[name] = pltpu.make_async_copy(
            getattr(r, name), getattr(r, name + "_here"), r.load_sems.at[number]
        )
        loads[name].start()
    normed_load = pltpu.make_async_copy(r.normed, r.activated_here, r.load_sems.at[9])
    folds = Folds(HIGH_PLAN if top else LOW_PLAN)

    def make_fold(key, of_layer, kind, parts, out, number):
        folds.add(
            number,
            Fold(
                of_layer, kind, parts, getattr(r, "first_" + key), getattr(r, "line_" + key),
                getattr(r, "last_" + key), out, (r.first_sems, r.line_sems, r.end_sems), number,
            ),
        )

    def passing(src, dst, sem):
        return pltpu.make_async_remote_copy(
            src_ref=src, dst_ref=dst, send_sem=r.pass_sems.at[0, sem], recv_sem=r.pass_sems.at[1, sem],
            device_id={SECTION: other}, device_id_type=MESH,
        )

    r.small[...] = jnp.zeros_like(r.small)

    def add_small(i, value):
        r.small[pl.ds(i, 1)] += value

    def add_up(value):
        r.small[6:7] += value

    kept = []
    if top:
        for s in range(2):

            @pl.when(section == s)
            def _():
                r.acts_out[s] = (r.act0 if s == 0 else r.act1)[...]
                passing(r.act1 if s == 0 else r.act0, r.acts_out.at[s], 0).start()

        incoming = r.incoming
    else:
        incoming_load = pltpu.make_async_copy(r.incoming, r.grads_out.at[1], r.load_sems.at[11])
        incoming_load.start()
        incoming_load.wait()
        r.rounded[...] = r.grads_out[1].astype(BF16)
        incoming = r.rounded

        for number, (src, dst) in enumerate(((r.gu_in, r.gu), (r.gd_in, r.gd), (r.go_in, r.go))):
            copy = pltpu.make_async_copy(src, dst, r.keep_sems.at[number])
            kept.append(copy)

            @pl.when(section == 1)
            def _():
                copy.start()

        make_fold("q1", 1, QKV, r.q1_here, r.gq, R_)
        q1_load = pltpu.make_async_copy(r.q1, r.q1_here, r.load_sems.at[10])
        q1_load.start()
        q1_load.wait()
        folds.reach(R_, 0)
    fill_penalty(r.penalty)

    phase = 0
    gather = Gather(ring, r.down_rows, r.gather_sems.at[0])
    scatter = Scatter(ring, r.stage, r.land.at[0], r.scatter_sems.at[0])

    def ready_mlp():
        for name in ("wd", "slope", "wu"):
            loads[name].wait()

    def mlp_made():
        loads["activated"].wait()
        for start in range(0, units, block):
            at = pl.ds(start, block)
            r.part_d[at] = mm_a(r.activated_here[:, at], r.down_rows[...]).astype(BF16)
        make_fold("d", layer, DOWN, r.part_d, r.gd, D_)
        folds.reach(D_, 0)
        normed_load.start()
        loads["second"].wait()
        for start in range(0, width, block):
            at = pl.ds(start, block)
            r.part_u[at] = mm_a(r.second_here[:, at], r.slope_here[...]).astype(BF16)
        make_fold("u", layer, UP, r.part_u, r.gu, U_)

    mlp_backward_body(
        ring, gather, scatter, incoming, r.middle, lambda: r.vectors[layer, 3:4, :],
        r.wu_here, r.wd_here, r.slope_here, r.down_rows, r.slope_here, r.grad_hidden,
        add_small, add_up, r.own,
        ready=ready_mlp, made=mlp_made, tick=folds.tick,
    )
    gather.finish()
    scatter.finish()
    gather = Gather(ring, r.attn_rows, r.gather_sems.at[1])
    scatter = Scatter(ring, r.stage, r.land.at[1], r.scatter_sems.at[1])

    def out_ready():
        loads["wo"].wait()

    def gathered():
        loads["context"].wait()
        r.part_o[...] = mm_a(r.context_here[...], r.attn_rows[...]).astype(BF16)
        make_fold("o", layer, OUT, r.part_o, r.go, O_)

    def attn_ready():
        loads["proj"].wait()
        loads["wq"].wait()

    def attn_made():
        normed_load.wait()
        for part in range(3):
            for start in range(0, width, block):
                at = pl.ds(start, block)
                made = mm_a(r.activated_here[:, at], r.grad_proj[part]).astype(BF16)
                r.part_q[part, at] = made
        r.small[7:8, 0:local] = jnp.sum(r.grad_proj[0].astype(F32), axis=0, keepdims=True)
        r.small[7:8, local : 2 * local] = jnp.sum(r.grad_proj[2].astype(F32), axis=0, keepdims=True)
        if not top:
            make_fold("q", layer, QKV, r.part_q, r.gq, Q_)

    attention_backward_body(
        ring, gather, scatter, r.grad_hidden, r.x, lambda: r.vectors[layer, 0:1, :],
        r.wq_here, r.wo_here, r.slopes, r.proj_here, r.totals, r.attn_rows, r.grad_proj,
        r.grad_hidden, add_small, r.grad_context, r.sums, r.penalty,
        out_ready=out_ready, ready=attn_ready, gathered=gathered, made=attn_made, tick=folds.tick,
    )
    gather.finish()
    scatter.finish()
    if top:
        folds.finish()
        for s in range(2):

            @pl.when(section == s)
            def _():
                passing(r.act1 if s == 0 else r.act0, r.acts_out.at[s], 0).wait_send()
                passing(r.act0, r.acts_out.at[1 - s], 0).wait_recv()

        return

    @pl.when(section == 0)
    def _():
        r.small_go[0] = r.small_in[...]
        r.small_keep[...] = r.small[...]
        passing(r.rounded, r.grads_land, 0).start()

    @pl.when(section == 1)
    def _():
        r.small_go[0] = r.small[...]
        r.small_keep[...] = r.small_in[...]
        r.rounded[...] = r.grad_hidden[...].astype(BF16)
        passing(r.rounded, r.grads_land, 0).start()

    small_pass = passing(r.small_go.at[0], r.small_land.at[0], 1)
    small_pass.start()
    folds.round()
    small_pass.wait()
    r.small_go[1] = r.small_keep[...] + r.small_land[0]

    def to_place(there, slot, sem):
        return pltpu.make_async_remote_copy(
            src_ref=r.small_go.at[1], dst_ref=r.small_land.at[slot], send_sem=r.small_sems.at[0, sem],
            recv_sem=r.small_sems.at[1, slot], device_id={DP: there}, device_id_type=MESH,
        )

    for there in range(count):

        @pl.when(there != place)
        def _():
            to_place(there, 1 + place, 1 + there).start()

    r.small_land[1 + place] = r.small_go[1]
    folds.round()
    for there in range(count):

        @pl.when(there != place)
        def _():
            to_place(there, 1 + there, 1 + there).wait_recv()
            to_place(there, 1 + place, 1 + there).wait_send()

    total = r.small_land[1]
    for there in range(1, count):
        total += r.small_land[1 + there]
    r.small_go[2] = total
    for step, device in enumerate((ring.mate, ring.peer)):
        hop = pltpu.make_async_remote_copy(
            src_ref=r.small_go.at[2 + step], dst_ref=r.small_land.at[1 + count + step],
            send_sem=r.small_sems.at[0, 1 + count + step], recv_sem=r.small_sems.at[1, 1 + count + step],
            device_id={TENSOR: device}, device_id_type=MESH,
        )
        hop.start()
        folds.round()
        hop.wait()
        r.small_go[3 + step] = r.small_go[2 + step] + r.small_land[1 + count + step]
    r.small_out[0:6] = r.small_go[4, 0:6]
    r.small_out[6:8] = total[6:8]

    folds.finish()
    for copy in kept:

        @pl.when(section == 1)
        def _():
            copy.wait()

    grads_pass = passing(r.rounded, r.grads_land, 0)
    grads_pass.wait()
    for s in range(2):

        @pl.when(section == s)
        def _():
            if s == 0:
                r.grads_out[0] = r.grad_hidden[...]
            r.grads_out[1 - s] = r.grads_land[...].astype(F32)


def mm_a(left, right):
    return lax.dot_general(left, right, (((0,), (0,)), ((), ())), preferred_element_type=F32)


def backward_call(layer, top, values, slopes):
    count = lax.axis_size(DP)
    block, width = values["x"].shape
    length = block * lax.axis_size(TENSOR)
    local, units = values["wo"].shape[0], values["wd"].shape[0]
    vmem, far = pl.BlockSpec(memory_space=pltpu.VMEM), pl.BlockSpec(memory_space=pl.ANY)
    ins = ["middle", "x", "totals", "vectors", "slopes"]
    ins_far = ["wd", "wu", "wo", "wq", "slope", "activated", "second", "normed", "proj", "context"]
    outs = [("grad_hidden", (block, width), F32), ("small", (8, width), F32)]
    shards = [
        ("gu", fold_shapes(UP, count, width, local, units)[2], F32),
        ("gd", fold_shapes(DOWN, count, width, local, units)[2], F32),
        ("go", fold_shapes(OUT, count, width, local, units)[2], F32),
    ]
    whole = {kind: fold_shapes(kind, count, width, local, units)[0] for kind in range(4)}
    if top:
        ins += ["incoming", "act0", "act1"]
        outs += shards + [("part_q", whole[QKV], BF16), ("acts_out", (2, block, width), BF16)]
    else:
        ins += ["small_in"]
        ins_far += ["incoming", "gu_in", "gd_in", "go_in", "q1"]
        outs += shards + [
            ("gq", fold_shapes(QKV, count, width, local, units)[2], F32),
            ("small_out", (8, width), F32),
            ("grads_out", (2, block, width), F32),
        ]
    dma = pltpu.SemaphoreType.DMA
    scratch = dict(
        wd_here=pltpu.VMEM((units, width), BF16),
        wu_here=pltpu.VMEM((width, units), BF16),
        wo_here=pltpu.VMEM((local, width), BF16),
        wq_here=pltpu.VMEM((3, width, local), BF16),
        slope_here=pltpu.VMEM((length, units), BF16),
        activated_here=pltpu.VMEM((length, units), BF16),
        second_here=pltpu.VMEM((length, width), BF16),
        proj_here=pltpu.VMEM((3, length, local), BF16),
        context_here=pltpu.VMEM((length, local), BF16),
        down_rows=pltpu.VMEM((length, width), BF16),
        attn_rows=pltpu.VMEM((length, width), BF16),
        grad_proj=pltpu.VMEM((3, length, local), BF16),
        grad_context=pltpu.VMEM((length, local), BF16),
        sums=pltpu.VMEM((2, length, PAIR), F32),
        penalty=pltpu.VMEM((length, LANES), F32),
        own=pltpu.VMEM((block, width), F32),
        stage=pltpu.VMEM((3, block, width), BF16),
        land=pltpu.VMEM((2, 3, block, width), BF16),
        gather_sems=dma((2, 2, 3, CHUNKS)),
        scatter_sems=dma((2, 2, 3, CHUNKS)),
        load_sems=dma((12,)),
        pass_sems=dma((2, 2)),
        first_sems=dma((2, 5, count)),
        line_sems=dma((2, 5, count, 2)),
        end_sems=dma((2, 5)),
        part_d=pltpu.VMEM(whole[DOWN], BF16),
        part_u=pltpu.VMEM(whole[UP], BF16),
        part_o=pltpu.VMEM(whole[OUT], BF16),
    )
    keys = {"d": DOWN, "u": UP, "o": OUT}
    if not top:
        keys.update({"q": QKV, "q1": QKV})
        scratch.update(
            part_q=pltpu.VMEM(whole[QKV], BF16),
            q1_here=pltpu.VMEM(whole[QKV], BF16),
            rounded=pltpu.VMEM((block, width), BF16),
            grads_land=pltpu.VMEM((block, width), BF16),
            small_go=pltpu.VMEM((5, 8, width), F32),
            small_keep=pltpu.VMEM((8, width), F32),
            small_land=pltpu.VMEM((3 + count, 8, width), F32),
            small_sems=dma((2, 3 + count)),
            keep_sems=dma((3,)),
        )
    for key, kind in keys.items():
        half = fold_shapes(kind, count, width, local, units)[1]
        scratch["first_" + key] = pltpu.VMEM((count,) + half, BF16)
        scratch["line_" + key] = pltpu.VMEM((count + 1,) + half, BF16)
        scratch["last_" + key] = pltpu.VMEM(half, BF16)
    values = dict(values, slopes=slopes)
    names = ins + ins_far + [item[0] for item in outs] + list(scratch)
    made = pl.pallas_call(
        functools.partial(backward_kernel, layer, top, names, None),
        out_shape=[jax.ShapeDtypeStruct(shape, dtype) for _, shape, dtype in outs],
        in_specs=[vmem] * len(ins) + [far] * len(ins_far),
        out_specs=[vmem] * len(outs),
        scratch_shapes=list(scratch.values()),
        compiler_params=pltpu.CompilerParams(
            collective_id=6 + layer, has_side_effects=True, vmem_limit_bytes=VMEM_LIMIT
        ),
        name="backward_%d" % layer,
    )(*[values[name] for name in ins + ins_far])
    return {item[0]: value for item, value in zip(outs, made)}


def swapped(value):
    count = lax.axis_size(SECTION)
    return lax.ppermute(value, SECTION, [(i, (i + 1) % count) for i in range(count)])


def backward_near(incoming, acts, saved, layers, vectors, slopes, local):
    def values(l, **more):
        w, s = layers[l], saved[l]
        return dict(
            middle=s["middle"], x=s["x"], totals=s["totals"], vectors=vectors, slope=s["slope_of"],
            activated=s["activated"], second=s["second"], normed=s["normed"], proj=s["proj"],
            context=s["context"], wd=w["down"], wu=w["up"], wo=w["out"], wq=w["qkv"], **more,
        )

    high = backward_call(1, True, values(1, incoming=incoming, act0=acts[0], act1=acts[1]), slopes)
    low = backward_call(
        0,
        False,
        values(
            0, incoming=high["grad_hidden"], small_in=high["small"], gu_in=high["gu"],
            gd_in=high["gd"], go_in=high["go"], q1=high["part_q"],
        ),
        slopes,
    )
    places = lax.axis_size(DP)
    tensor, place = lax.axis_index(TENSOR), lax.axis_index(DP)
    small = low["small_out"]
    width = small.shape[1]
    share = width // (lax.axis_size(TENSOR) * places)
    vector = lax.dynamic_slice_in_dim(small[:6], (tensor * places + place) * share, share, axis=1)
    up_share, qv_share = width // places, local // places
    up = lax.dynamic_slice_in_dim(small[6], place * up_share, up_share)
    qv = lax.dynamic_slice_in_dim(
        small[7, : 2 * local].reshape(2, local), place * qv_share, qv_share, axis=1
    )
    return (
        high["acts_out"][None],
        low["grads_out"][None],
        vector[0][None],
        vector[1][None],
        jnp.transpose(low["gq"], (1, 0, 2))[None],
        qv[None],
        low["go"][None],
        vector[2][None],
        vector[3][None],
        vector[4][None],
        low["gu"][None],
        up[None],
        low["gd"][None],
        vector[5][None],
    )


def near_shards(depth, block):
    return depth % 256 == 0 and block % 256 == 0


def gathered_layers(section, layer_count, w_qkv, w_out, w_up, w_down, small_ones):
    def both(value):
        other = swapped(value)
        return [jnp.where(section == l, value, other) for l in range(layer_count)]

    def over_dp(value, axis):
        return both(lax.all_gather(value, DP, axis=axis, tiled=True))

    qkv_all, up_all = over_dp(jnp.transpose(w_qkv[0], (1, 0, 2)), 1), over_dp(w_up[0], 0)
    out_all, down_all = over_dp(w_out[0], 1), over_dp(w_down[0], 1)
    vectors = [
        both(item[0]) for item in small_ones
    ]
    layers = []
    for l in range(layer_count):
        gain1, bias1, qv, bout, gain2, bias2, bup, bdown = [item[l] for item in vectors]
        layers.append(
            dict(
                ln1_gain=gain1,
                ln1_bias=bias1,
                ln2_gain=gain2,
                ln2_bias=bias2,
                qkv=qkv_all[l],
                out=out_all[l],
                up=up_all[l],
                down=down_all[l],
                b_qkv=jnp.stack([qv[0], jnp.zeros_like(qv[0]), qv[1]])[:, None, :],
                b_out=bout,
                b_up=bup,
                b_down=bdown,
            )
        )
    return layers


def per_device(
    inputs,
    out_grad,
    lang_ids,
    lang_weights,
    ln1_gain,
    ln1_bias,
    w_qkv,
    b_qv,
    w_out,
    b_out,
    ln2_gain,
    ln2_bias,
    w_up,
    b_up,
    w_down,
    b_down,
):
    section = lax.axis_index(SECTION)
    layer_count = lax.axis_size(SECTION)
    local_heads = w_qkv.shape[3] // HEAD
    head_ids = lax.axis_index(TENSOR) * local_heads + jnp.arange(local_heads, dtype=jnp.int32)
    slopes = jnp.exp2(-8.0 * (head_ids.astype(jnp.float32) + 1.0) / HEADS)
    slopes = jnp.broadcast_to(slopes[:, None], (local_heads, inputs.shape[1]))

    row = lax.dynamic_index_in_dim(inputs, section, 0, keepdims=False)
    target = lax.dynamic_index_in_dim(out_grad, section, 0, keepdims=False)
    lang = lax.dynamic_index_in_dim(lang_ids, section, 0, keepdims=False)
    matches = lang == jnp.arange(lang_weights.shape[0], dtype=jnp.int32)
    scale = jnp.sum(jnp.where(matches, lang_weights, 0)).astype(jnp.float32) / 64.0

    if near_shards(w_qkv[0].shape[0], inputs.shape[1]):
        vector = jnp.stack(
            [item[0] for item in (ln1_gain, ln1_bias, b_out, ln2_gain, ln2_bias)]
            + [b_up[0], b_down[0], jnp.pad(b_qv[0].reshape(-1), (0, b_out.shape[1] - 2 * b_qv.shape[2]))]
        )
        shards = (jnp.transpose(w_qkv[0], (1, 0, 2)), w_out[0], w_up[0], w_down[0])
        acts, saved, layers, vectors = forward_call(row, vector, shards, slopes)
        return backward_near(
            target.astype(F32) * scale, acts, saved, layers, vectors, slopes, b_qv.shape[2]
        )
    else:
        layers = gathered_layers(
            section, layer_count, w_qkv, w_out, w_up, w_down,
            (ln1_gain, ln1_bias, b_qv, b_out, ln2_gain, ln2_bias, b_up, b_down),
        )
        acts, saved = [], []
        for l in range(layer_count):
            row, kept = layer_forward(row, layers[l], slopes)
            acts.append(row)
            saved.append(kept)
    grads, small, large = [None] * layer_count, [None] * layer_count, [None] * layer_count
    incoming = target.astype(jnp.float32) * scale
    for l in reversed(range(layer_count)):
        grads[l], small[l], large[l] = layer_backward(
            incoming, layers[l], saved[l], slopes
        )
        incoming = grads[l].astype(jnp.bfloat16).astype(jnp.float32)

    def mine(items):
        return jnp.where(section == 0, items[0], items[1])

    def theirs(items):
        return jnp.where(section == 0, items[1], items[0])

    def rows_of(items):
        own, other = mine(items), swapped(theirs(items))
        return jnp.stack([jnp.where(section == r, own, other) for r in range(layer_count)])[None]

    def reduced(name, axis):
        items = [item[name].astype(jnp.bfloat16) for item in large]
        total = mine(items) + swapped(theirs(items))
        return lax.psum_scatter(total, DP, scatter_dimension=axis, tiled=True).astype(
            jnp.float32
        )[None]

    small_total = mine(small) + swapped(theirs(small))
    small_shards = lax.psum_scatter(small_total, (TENSOR, DP), scatter_dimension=1, tiled=True)
    return (
        rows_of(acts),
        rows_of([item.astype(jnp.bfloat16) for item in grads]).astype(jnp.float32),
        small_shards[0][None],
        small_shards[1][None],
        jnp.transpose(reduced("qkv", 1), (0, 2, 1, 3)),
        reduced("b_qv", 1),
        reduced("out", 1),
        small_shards[2][None],
        small_shards[3][None],
        small_shards[4][None],
        reduced("up", 0),
        reduced("b_up", 0),
        reduced("down", 1),
        small_shards[5][None],
    )


def solution(mesh):
    return jax.shard_map(
        per_device,
        mesh=mesh,
        in_specs=(
            P(DP, TENSOR, None),
            P(DP, TENSOR, None),
            P(DP),
            P(),
            P(SECTION, None),
            P(SECTION, None),
            P(SECTION, DP, None, TENSOR),
            P(SECTION, None, TENSOR),
            P(SECTION, TENSOR, DP),
            P(SECTION, None),
            P(SECTION, None),
            P(SECTION, None),
            P(SECTION, DP, TENSOR),
            P(SECTION, TENSOR),
            P(SECTION, TENSOR, DP),
            P(SECTION, None),
        ),
        out_specs=(
            P(SECTION, DP, TENSOR, None),
            P(SECTION, DP, TENSOR, None),
            P(SECTION, (TENSOR, DP)),
            P(SECTION, (TENSOR, DP)),
            P(SECTION, DP, None, TENSOR),
            P(SECTION, None, (TENSOR, DP)),
            P(SECTION, TENSOR, DP),
            P(SECTION, (TENSOR, DP)),
            P(SECTION, (TENSOR, DP)),
            P(SECTION, (TENSOR, DP)),
            P(SECTION, DP, TENSOR),
            P(SECTION, (TENSOR, DP)),
            P(SECTION, TENSOR, DP),
            P(SECTION, (TENSOR, DP)),
        ),
        check_vma=False,
    )
```

```python
import functools

import jax
import jax.numpy as jnp
from jax import lax
from jax.experimental import pallas as pl
from jax.experimental.pallas import tpu as pltpu
from jax.sharding import PartitionSpec as P

HEADS = 16
HEAD = 64
PAIR = 2 * HEAD

EPSILON = 1e-05
GELU_SCALE = 0.7978845608028654

SECTION, TENSOR, DP = "section", "tensor", "dp"
MESH = pl.DeviceIdType.MESH
F32 = jnp.float32
BF16 = jnp.bfloat16
CHUNKS = 2
LANES = 128
VMEM_LIMIT = 61 * 1024 * 1024


def rows_at(start, size):
    return pl.ds(pl.multiple_of(start, size), size)


def mm(left, right):
    return lax.dot_general(left, right, (((1,), (0,)), ((), ())), preferred_element_type=F32)


def mm_t(left, right):
    return lax.dot_general(left, right, (((1,), (1,)), ((), ())), preferred_element_type=F32)


class Ring:
    def __init__(self, block):
        self.block = block
        self.chunk = block // CHUNKS
        self.me = lax.axis_index(TENSOR)
        core, chip = lax.rem(self.me, 2), self.me // 2
        self.mate = self.me + 1 - 2 * core
        self.peer = self.me + 2 - 4 * chip
        self.far = self.peer + 1 - 2 * core

    def greet(self):
        barrier = pltpu.get_barrier_semaphore()
        for other in (self.mate, self.peer):
            pl.semaphore_signal(barrier, inc=1, device_id={TENSOR: other}, device_id_type=MESH)
        pl.semaphore_wait(barrier, 2)

    def rows(self, owner, c):
        return rows_at(owner * self.block + c * self.chunk, self.chunk)

    def send(self, src, dst, sems, kind, c, other):
        return pltpu.make_async_remote_copy(
            src_ref=src,
            dst_ref=dst,
            send_sem=sems.at[0, kind, c],
            recv_sem=sems.at[1, kind, c],
            device_id={TENSOR: other},
            device_id_type=MESH,
        )


class Gather:
    def __init__(self, ring, every, sems):
        self.ring, self.every, self.sems = ring, every, sems

    def copy(self, kind, owner, c):
        ring = self.ring
        at = self.every.at[ring.rows(owner, c)]
        return ring.send(at, at, self.sems, kind, c, ring.peer if kind == 1 else ring.mate)

    def start(self, c):
        self.copy(1, self.ring.me, c).start()
        self.copy(0, self.ring.me, c).start()

    def arrived_mate(self, c):
        self.copy(0, self.ring.mate, c).wait_recv()

    def arrived_peer(self, c):
        self.copy(1, self.ring.peer, c).wait_recv()
        self.copy(2, self.ring.peer, c).start()

    def arrived_far(self, c):
        self.copy(2, self.ring.far, c).wait_recv()

    def finish(self):
        for c in range(CHUNKS):
            for kind, owner in ((0, self.ring.me), (1, self.ring.me), (2, self.ring.peer)):
                self.copy(kind, owner, c).wait_send()


class Scatter:
    def __init__(self, ring, stage, land, sems):
        self.ring, self.stage, self.land, self.sems = ring, stage, land, sems

    def copy(self, kind, c):
        ring = self.ring
        at = pl.ds(c * ring.chunk, ring.chunk)
        return ring.send(
            self.stage.at[kind, at],
            self.land.at[kind, at],
            self.sems,
            kind,
            c,
            ring.peer if kind == 1 else ring.mate,
        )

    def put(self, kind, c, value):
        self.stage[kind, pl.ds(c * self.ring.chunk, self.ring.chunk)] = value.astype(BF16)
        self.copy(kind, c).start()

    def take(self, kind, c):
        self.copy(kind, c).wait_recv()
        return self.land[kind, pl.ds(c * self.ring.chunk, self.ring.chunk)].astype(F32)

    def to_peer(self, c, far_part, peer_part):
        self.put(0, c, far_part)
        self.put(1, c, peer_part + self.take(0, c))

    def finish(self):
        for kind in range(3):
            for c in range(CHUNKS):
                self.copy(kind, c).wait_send()


def normalize(values):
    center = values - jnp.mean(values, axis=-1, keepdims=True)
    scale = lax.rsqrt(jnp.mean(center * center, axis=-1, keepdims=True) + EPSILON)
    return center * scale, scale


def norm_pull(values, gain, grad):
    unit, scale = normalize(values)
    scaled = grad * gain
    pulled = scale * (
        scaled
        - jnp.mean(scaled, axis=-1, keepdims=True)
        - unit * jnp.mean(scaled * unit, axis=-1, keepdims=True)
    )
    return pulled, jnp.sum(grad * unit, axis=0, keepdims=True), jnp.sum(grad, axis=0, keepdims=True)


def scores_of(keys, queries, slope, penalty_ref, start):
    stop, count = keys.shape[0], queries.shape[0]
    scores = mm_t(keys, queries) + slope * jnp.concatenate([penalty_ref[:stop]] * (count // LANES), axis=1)
    last = scores[start:]
    allowed = lax.broadcasted_iota(jnp.int32, (count, count), 0) <= lax.broadcasted_iota(
        jnp.int32, (count, count), 1
    )
    last = jnp.where(allowed, last, -1e30)
    return last if start == 0 else jnp.concatenate([scores[:start], last], axis=0)


def head_mask(value, which):
    lane = lax.broadcasted_iota(jnp.int32, value.shape, 1)
    inside = lane < HEAD if which == 0 else lane >= HEAD
    return jnp.where(inside, value, jnp.zeros_like(value))


def fill_penalty(penalty_ref):
    penalty_ref[...] = lax.broadcasted_iota(jnp.int32, penalty_ref.shape, 0).astype(F32)


def nothing(point=0):
    pass


def attend_forward(proj, context, totals, slopes, penalty, block, tick=nothing):
    length, width = context.shape
    for pair in range(width // PAIR):
        lanes = pl.ds(pair * PAIR, PAIR)
        for start in range(0, length, block):
            tick(pair * 4 + start // block)
            stop = start + block
            queries = proj[0, start:stop, lanes] * jnp.asarray(0.125, BF16)
            keys = proj[1, :stop, lanes]
            values_t = proj[2, :stop, lanes].T
            outs = []
            for which in range(2):
                head = pair * 2 + which
                slope = slopes[pl.ds(head, 1), :]
                scores = scores_of(keys, head_mask(queries, which), slope, penalty, start)
                highest = jnp.max(scores, axis=0, keepdims=True)
                grown = jnp.exp(scores - highest)
                total = jnp.sum(grown, axis=0, keepdims=True)
                mixed = mm(values_t[which * HEAD : (which + 1) * HEAD], grown.astype(BF16))
                outs.append(mixed / total)
                totals[pl.ds(head, 1), start:stop] = highest + jnp.log(total)
            context[start:stop, lanes] = jnp.concatenate(outs, axis=0).T.astype(BF16)


def attend_backward(proj, grad_context, totals, slopes, penalty, grad_proj, sums, block, tick=nothing):
    length, width = grad_context.shape
    for pair in range(width // PAIR):
        lanes = pl.ds(pair * PAIR, PAIR)
        for start in range(0, length, block):
            tick(pair * 4 + start // block)
            stop = start + block
            queries = proj[0, start:stop, lanes] * jnp.asarray(0.125, BF16)
            keys = proj[1, :stop, lanes]
            keys_t = keys.T
            values = proj[2, :stop, lanes]
            grads = grad_context[start:stop, lanes]
            outs = []
            for which in range(2):
                head = pair * 2 + which
                slope = slopes[pl.ds(head, 1), :]
                one_query = head_mask(queries, which)
                one_grad = head_mask(grads, which)
                scores = scores_of(keys, one_query, slope, penalty, start)
                probs = jnp.exp(scores - totals[pl.ds(head, 1), start:stop])
                pulled = probs * mm_t(values, one_grad)
                inner = jnp.sum(pulled, axis=0, keepdims=True)
                grad_scores = (pulled - probs * inner).astype(BF16)
                outs.append(mm(keys_t[which * HEAD : (which + 1) * HEAD], grad_scores) * 0.125)
                grad_keys = mm(grad_scores, one_query)
                grad_values = mm(probs.astype(BF16), one_grad)
                if which == 0:
                    first_keys, first_values = grad_keys, grad_values
                else:
                    grad_keys, grad_values = grad_keys + first_keys, grad_values + first_values
            grad_proj[0, start:stop, lanes] = jnp.concatenate(outs, axis=0).T.astype(BF16)
            if start > 0:
                sums[0, :start] += grad_keys[:start]
                sums[1, :start] += grad_values[:start]
            sums[0, start:stop] = grad_keys[start:]
            sums[1, start:stop] = grad_values[start:]
        grad_proj[1, :, lanes] = sums[0].astype(BF16)
        grad_proj[2, :, lanes] = sums[1].astype(BF16)


def attention_forward_body(
    ring, gather, scatter, x, gain, shift, w_qkv, b_qkv, w_out, b_out, slopes,
    normed, proj, context, totals, middle, penalty,
    qkv_ready=nothing, out_ready=nothing, tick=nothing,
):
    block, chunk = ring.block, ring.chunk
    for c in range(CHUNKS):
        at = pl.ds(c * chunk, chunk)
        unit, _ = normalize(x[at].astype(F32))
        normed[ring.rows(ring.me, c)] = (unit * gain() + shift()).astype(BF16)
        gather.start(c)
    qkv_ready()

    def project(owner, c, size):
        at = rows_at(owner * block + c * chunk, size)
        rows = normed[at]
        for part in range(3):
            made = mm(rows, w_qkv[part])
            proj[part, at] = (made if part == 1 else made + b_qkv(part)).astype(BF16)

    project(ring.me, 0, block)
    for c in range(CHUNKS):
        gather.arrived_mate(c)
    project(ring.mate, 0, block)
    for c in range(CHUNKS):
        gather.arrived_peer(c)
        project(ring.peer, c, chunk)
        gather.arrived_far(c)
        project(ring.far, c, chunk)
    attend_forward(proj, context, totals, slopes, penalty, block, tick)
    out_ready()

    def part_of(owner, c):
        return mm(context[ring.rows(owner, c)], w_out[...])

    for c in range(CHUNKS):
        scatter.put(0, c, part_of(ring.far, c))
        scatter.put(1, c, part_of(ring.peer, c) + scatter.take(0, c))
        tick(8 + c)
    for c in range(CHUNKS):
        scatter.put(2, c, part_of(ring.mate, c))
    tick(10)
    for c in range(CHUNKS):
        at = pl.ds(c * chunk, chunk)
        total = part_of(ring.me, c) + scatter.take(2, c) + scatter.take(1, c)
        middle[at] = x[at].astype(F32) + total + b_out()


def mlp_forward_body(
    ring, gather, scatter, middle, gain, shift, w_up, b_up, w_down, b_down,
    second, activated, slope_of, leaving, own,
    ready=nothing, tick=nothing, late=nothing,
):
    block, chunk = ring.block, ring.chunk
    for c in range(CHUNKS):
        at = pl.ds(c * chunk, chunk)
        unit, _ = normalize(middle[at])
        second[ring.rows(ring.me, c)] = (unit * gain() + shift()).astype(BF16)
        gather.start(c)

    def widen(at):
        upward = mm(second[at], w_up[...]) + b_up()
        inner = jnp.tanh(GELU_SCALE * (upward + 0.044715 * upward * upward * upward))
        half = 0.5 * (1.0 + inner)
        value = upward * half
        slope = half + 0.5 * upward * (1.0 - inner * inner) * GELU_SCALE * (
            1.0 + 3 * 0.044715 * upward * upward
        )
        value = value.astype(BF16)
        activated[at] = value
        slope_of[at] = slope.astype(BF16)

    def narrow(at):
        return mm(activated[at], w_down[...])

    def expand(at):
        widen(at)
        return narrow(at)

    tick(11)
    ready()
    if late is not nothing:
        widen(rows_at(ring.me * block, block))
        for c in range(CHUNKS):
            gather.arrived_mate(c)
        widen(rows_at(ring.mate * block, block))
        for c in range(CHUNKS):
            gather.arrived_peer(c)
            widen(ring.rows(ring.peer, c))
            gather.arrived_far(c)
            widen(ring.rows(ring.far, c))
        late()
        expand = narrow
    own[...] = expand(rows_at(ring.me * block, block))
    tick(12)
    for c in range(CHUNKS if late is nothing else 0):
        gather.arrived_mate(c)
    part = expand(rows_at(ring.mate * block, block))
    for c in range(CHUNKS):
        scatter.put(2, c, part[c * chunk : (c + 1) * chunk])
    tick(13)
    for c in range(CHUNKS):
        if late is nothing:
            gather.arrived_peer(c)
        peer_part = expand(ring.rows(ring.peer, c))
        if late is nothing:
            gather.arrived_far(c)
        scatter.put(0, c, expand(ring.rows(ring.far, c)))
        scatter.put(1, c, peer_part + scatter.take(0, c))
        tick(14 + c)
    for c in range(CHUNKS):
        at = pl.ds(c * chunk, chunk)
        total = own[at] + scatter.take(2, c) + scatter.take(1, c)
        leaving[at] = (middle[at] + total + b_down()).astype(BF16)


def attention_forward_kernel(
    x, gain, shift, w_qkv, b_qkv, w_out, b_out, slopes,
    normed, proj, context, totals, middle,
    penalty, stage, land, gather_sems, scatter_sems,
):
    ring = Ring(x.shape[0])
    ring.greet()
    gather = Gather(ring, normed, gather_sems)
    scatter = Scatter(ring, stage, land, scatter_sems)
    fill_penalty(penalty)
    attention_forward_body(
        ring, gather, scatter, x, lambda: gain[...], lambda: shift[...], w_qkv,
        lambda part: b_qkv[part], w_out, lambda: b_out[...], slopes,
        normed, proj, context, totals, middle, penalty,
    )
    gather.finish()
    scatter.finish()


def mlp_forward_kernel(
    middle, gain, shift, w_up, b_up, w_down, b_down,
    second, activated, slope_of, leaving,
    own, stage, land, gather_sems, scatter_sems,
):
    ring = Ring(middle.shape[0])
    ring.greet()
    gather = Gather(ring, second, gather_sems)
    scatter = Scatter(ring, stage, land, scatter_sems)
    mlp_forward_body(
        ring, gather, scatter, middle, lambda: gain[...], lambda: shift[...], w_up,
        lambda: b_up[...], w_down, lambda: b_down[...],
        second, activated, slope_of, leaving, own,
    )
    gather.finish()
    scatter.finish()


def mlp_backward_body(
    ring, gather, scatter, incoming, middle, gain, w_up, w_down, slope_of,
    down_rows, grad_up, grad_middle, small, up_sum, own,
    ready=nothing, made=nothing, tick=nothing,
):
    block, chunk = ring.block, ring.chunk
    for c in range(CHUNKS):
        down_rows[ring.rows(ring.me, c)] = incoming[pl.ds(c * chunk, chunk)].astype(BF16)
        gather.start(c)
    ready()

    def pull(at):
        grad = mm_t(down_rows[at], w_down[...]) * slope_of[at].astype(F32)
        grad = grad.astype(BF16)
        grad_up[at] = grad
        up_sum(jnp.sum(grad.astype(F32), axis=0, keepdims=True))
        return mm_t(grad, w_up[...])

    own[...] = pull(rows_at(ring.me * block, block))
    tick(0)
    for c in range(CHUNKS):
        gather.arrived_mate(c)
    part = pull(rows_at(ring.mate * block, block))
    for c in range(CHUNKS):
        scatter.put(2, c, part[c * chunk : (c + 1) * chunk])
    tick(1)
    for c in range(CHUNKS):
        gather.arrived_peer(c)
        peer_part = pull(ring.rows(ring.peer, c))
        gather.arrived_far(c)
        scatter.put(0, c, pull(ring.rows(ring.far, c)))
        scatter.put(1, c, peer_part + scatter.take(0, c))
        tick(2 + c)
    made()
    tick(4)
    for c in range(CHUNKS):
        at = pl.ds(c * chunk, chunk)
        total = own[at] + scatter.take(2, c) + scatter.take(1, c)
        pulled, grad_gain, grad_shift = norm_pull(middle[at], gain(), total)
        before = incoming[at].astype(F32)
        after = before + pulled
        grad_middle[at] = after
        small(2, jnp.sum(after, axis=0, keepdims=True))
        small(3, grad_gain)
        small(4, grad_shift)
        small(5, jnp.sum(before, axis=0, keepdims=True))
        tick(5 + c)


def attention_backward_body(
    ring, gather, scatter, grad_middle, x, gain, w_qkv, w_out, slopes, proj, totals,
    attn_rows, grad_proj, grad_hidden, small, grad_context, sums, penalty,
    out_ready=nothing, ready=nothing, gathered=nothing, made=nothing, tick=nothing,
):
    block, chunk = ring.block, ring.chunk
    for c in range(CHUNKS):
        attn_rows[ring.rows(ring.me, c)] = grad_middle[pl.ds(c * chunk, chunk)].astype(BF16)
        gather.start(c)
    out_ready()

    def pull(at):
        grad_context[at] = mm_t(attn_rows[at], w_out[...]).astype(BF16)

    pull(rows_at(ring.me * block, block))
    for c in range(CHUNKS):
        gather.arrived_mate(c)
    pull(rows_at(ring.mate * block, block))
    tick(7)
    for c in range(CHUNKS):
        gather.arrived_peer(c)
        pull(ring.rows(ring.peer, c))
        gather.arrived_far(c)
        pull(ring.rows(ring.far, c))
        tick(8 + c)
    gathered()
    ready()
    attend_backward(proj, grad_context, totals, slopes, penalty, grad_proj, sums, block, lambda at: tick(10 + at))

    def part_of(owner, c):
        at = ring.rows(owner, c)
        total = mm_t(grad_proj[0, at], w_qkv[0])
        for part in range(1, 3):
            total += mm_t(grad_proj[part, at], w_qkv[part])
        return total

    for c in range(CHUNKS):
        scatter.put(0, c, part_of(ring.far, c))
        scatter.put(1, c, part_of(ring.peer, c) + scatter.take(0, c))
    for c in range(CHUNKS):
        scatter.put(2, c, part_of(ring.mate, c))
    made()
    tick(18)
    for c in range(CHUNKS):
        at = pl.ds(c * chunk, chunk)
        total = part_of(ring.me, c) + scatter.take(2, c) + scatter.take(1, c)
        pulled, grad_gain, grad_shift = norm_pull(x[at].astype(F32), gain(), total)
        grad_hidden[at] = grad_middle[at] + pulled
        small(0, grad_gain)
        small(1, grad_shift)
        tick(19 + c)


def mlp_backward_kernel(
    incoming, middle, gain, w_up, w_down, slope_of,
    down_rows, grad_up, grad_middle, small, up_sum,
    own, stage, land, gather_sems, scatter_sems,
):
    ring = Ring(middle.shape[0])
    ring.greet()
    gather = Gather(ring, down_rows, gather_sems)
    scatter = Scatter(ring, stage, land, scatter_sems)
    small[...] = jnp.zeros_like(small)
    up_sum[...] = jnp.zeros_like(up_sum)

    def add_small(i, value):
        small[pl.ds(i, 1)] += value

    def add_up(value):
        up_sum[...] += value

    mlp_backward_body(
        ring, gather, scatter, incoming, middle, lambda: gain[...], w_up, w_down, slope_of,
        down_rows, grad_up, grad_middle, add_small, add_up, own,
    )
    gather.finish()
    scatter.finish()


def attention_backward_kernel(
    grad_middle, x, gain, w_qkv, w_out, slopes, proj, totals,
    attn_rows, grad_proj, grad_hidden, small, qv_sum,
    grad_context, sums, penalty, stage, land, gather_sems, scatter_sems,
):
    ring = Ring(x.shape[0])
    ring.greet()
    gather = Gather(ring, attn_rows, gather_sems)
    scatter = Scatter(ring, stage, land, scatter_sems)
    fill_penalty(penalty)
    small[...] = jnp.zeros_like(small)

    def add_small(i, value):
        small[pl.ds(i, 1)] += value

    attention_backward_body(
        ring, gather, scatter, grad_middle, x, lambda: gain[...], w_qkv, w_out, slopes, proj,
        totals, attn_rows, grad_proj, grad_hidden, add_small, grad_context, sums, penalty,
    )
    qv_sum[...] = jnp.zeros_like(qv_sum)
    qv_sum[0:1] = jnp.sum(grad_proj[0].astype(F32), axis=0, keepdims=True)
    qv_sum[1:2] = jnp.sum(grad_proj[2].astype(F32), axis=0, keepdims=True)
    gather.finish()
    scatter.finish()


def call(kernel, name, number, args, outs, scratch):
    vmem = pl.BlockSpec(memory_space=pltpu.VMEM)
    return pl.pallas_call(
        kernel,
        out_shape=[jax.ShapeDtypeStruct(shape, dtype) for shape, dtype in outs],
        in_specs=[vmem] * len(args),
        out_specs=[vmem] * len(outs),
        scratch_shapes=scratch,
        compiler_params=pltpu.CompilerParams(
            collective_id=number, has_side_effects=True, vmem_limit_bytes=VMEM_LIMIT
        ),
        name=name,
    )(*args)


def link_scratch(block, width):
    return [
        pltpu.VMEM((3, block, width), BF16),
        pltpu.VMEM((3, block, width), BF16),
        pltpu.SemaphoreType.DMA((2, 3, CHUNKS)),
        pltpu.SemaphoreType.DMA((2, 3, CHUNKS)),
    ]


def row_vector(value):
    return value.reshape(1, -1)


def layer_forward(x, w, slopes):
    block, width = x.shape
    length = block * lax.axis_size(TENSOR)
    local = w["out"].shape[0]
    heads = local // HEAD
    normed, proj, context, totals, middle = call(
        attention_forward_kernel,
        "attention_forward",
        1,
        (x, row_vector(w["ln1_gain"]), row_vector(w["ln1_bias"]), w["qkv"], w["b_qkv"], w["out"], row_vector(w["b_out"]), slopes),
        [((length, width), BF16), ((3, length, local), BF16), ((length, local), BF16), ((heads, length), F32), ((block, width), F32)],
        [pltpu.VMEM((length, LANES), F32)] + link_scratch(block, width),
    )
    units = w["up"].shape[1]
    second, activated, slope_of, leaving = call(
        mlp_forward_kernel,
        "mlp_forward",
        2,
        (middle, row_vector(w["ln2_gain"]), row_vector(w["ln2_bias"]), w["up"], row_vector(w["b_up"]), w["down"], row_vector(w["b_down"])),
        [((length, width), BF16), ((length, units), BF16), ((length, units), BF16), ((block, width), BF16)],
        [pltpu.VMEM((block, width), F32)] + link_scratch(block, width),
    )
    saved = dict(x=x, normed=normed, proj=proj, context=context, totals=totals, middle=middle, second=second, activated=activated, slope_of=slope_of)
    return leaving, saved


def layer_backward(incoming, w, s, slopes):
    block, width = incoming.shape
    length = block * lax.axis_size(TENSOR)
    local, units = w["out"].shape[0], w["up"].shape[1]
    down_rows, grad_up, grad_middle, small_a, up_sum = call(
        mlp_backward_kernel,
        "mlp_backward",
        3,
        (incoming, s["middle"], row_vector(w["ln2_gain"]), w["up"], w["down"], s["slope_of"]),
        [((length, width), BF16), ((length, units), BF16), ((block, width), F32), ((8, width), F32), ((1, units), F32)],
        [pltpu.VMEM((block, width), F32)] + link_scratch(block, width),
    )
    attn_rows, grad_proj, grad_hidden, small_b, qv_sum = call(
        attention_backward_kernel,
        "attention_backward",
        4,
        (grad_middle, s["x"], row_vector(w["ln1_gain"]), w["qkv"], w["out"], slopes, s["proj"], s["totals"]),
        [((length, width), BF16), ((3, length, local), BF16), ((block, width), F32), ((8, width), F32), ((8, local), F32)],
        [pltpu.VMEM((length, local), BF16), pltpu.VMEM((2, length, PAIR), F32), pltpu.VMEM((length, LANES), F32)]
        + link_scratch(block, width),
    )
    small = jnp.concatenate([small_b[:2], small_a[2:6]])
    large = dict(
        qkv=jnp.einsum("td,cth->cdh", s["normed"], grad_proj, preferred_element_type=F32),
        out=jnp.einsum("th,td->hd", s["context"], attn_rows, preferred_element_type=F32),
        up=jnp.einsum("td,tf->df", s["second"], grad_up, preferred_element_type=F32),
        down=jnp.einsum("tf,td->fd", s["activated"], down_rows, preferred_element_type=F32),
        b_qv=qv_sum[:2],
        b_up=up_sum[0],
    )
    return grad_hidden, small, large


class Cross:
    def __init__(self, layer, shards, whole, sems):
        self.layer, self.shards, self.whole = layer, shards, whole
        self.first, self.line, self.last, self.local = sems
        self.section, self.place = lax.axis_index(SECTION), lax.axis_index(DP)
        self.count = lax.axis_size(DP)
        self.other = 1 - self.section
        self.owner = self.section == layer
        self.half = jnp.where(self.owner, 0, 1)

    def at(self, i, half, place):
        ref = self.whole[i]
        if i == 0:
            rows = self.shards[i].shape[1] // 2
            return ref.at[:, rows_at((place * 2 + half) * rows, rows), :]
        rows = self.shards[i].shape[0] // 2
        if i == 2:
            return ref.at[rows_at((place * 2 + half) * rows, rows), :]
        return ref.at[rows_at(half * rows, rows), rows_at(place * self.shards[i].shape[1], self.shards[i].shape[1])]

    def mine(self, i, half):
        ref = self.shards[i]
        rows = ref.shape[1 if i == 0 else 0] // 2
        return ref.at[:, pl.ds(half * rows, rows), :] if i == 0 else ref.at[pl.ds(half * rows, rows), :]

    def copy(self, src, dst, sems, where, device):
        return pltpu.make_async_remote_copy(
            src_ref=src,
            dst_ref=dst,
            send_sem=sems.at[(0,) + where],
            recv_sem=sems.at[(1,) + where],
            device_id=device,
            device_id_type=MESH,
        )

    def over_first(self, i):
        return self.copy(
            self.mine(i, 1), self.at(i, 1, self.place), self.first, (i,), {SECTION: self.other}
        )

    def over_last(self, i, place, src=None):
        at = self.at(i, self.half, place)
        return self.copy(at if src is None else src, at, self.last, (i, place), {SECTION: self.other})

    def from_last(self, i, place):
        at = self.at(i, 1 - self.half, place)
        return self.copy(at, at, self.last, (i, place), {SECTION: self.other})

    def along(self, i, place, right, src=None):
        at = self.at(i, self.half, place)
        return self.copy(
            at if src is None else src,
            at,
            self.line,
            (i, place, int(right)),
            {DP: self.place + (1 if right else -1)},
        )

    def onward(self, i, place, right, src=None):
        @pl.when(self.place + 1 < self.count if right else self.place > 0)
        def _():
            self.along(i, place, right, src).start()

    def keep(self, i, half):
        return pltpu.make_async_copy(
            self.mine(i, half), self.at(i, half, self.place), self.local.at[i, half]
        )

    def begin(self, i):
        @pl.when(self.owner)
        def _():
            self.over_first(i).start()
            for right in (True, False):
                self.onward(i, self.place, right, self.mine(i, 0))
            self.over_last(i, self.place, self.mine(i, 0)).start()
            for half in range(2):
                self.keep(i, half).start()

    def start(self, i):
        @pl.when(jnp.logical_not(self.owner))
        def _():
            self.over_first(i).wait_recv()
            for right in (True, False):
                self.onward(i, self.place, right)

    def step(self, i, hops):
        for right in (True, False):
            place = self.place - hops if right else self.place + hops

            @pl.when(place >= 0 if right else place < self.count)
            def _():
                self.along(i, place, right).wait_recv()
                self.over_last(i, place).start()
                self.onward(i, place, right)

    def finish(self, i):
        @pl.when(self.owner)
        def _():
            for half in range(2):
                self.keep(i, half).wait()

        for place in range(self.count):

            @pl.when(jnp.logical_or(jnp.logical_not(self.owner), place != self.place))
            def _():
                self.from_last(i, place).wait_recv()

    def drain(self, i):
        @pl.when(self.owner)
        def _():
            self.over_first(i).wait_send()

        for place in range(self.count):

            @pl.when(jnp.logical_or(self.owner, place != self.place))
            def _():
                self.over_last(i, place).wait_send()

            @pl.when(jnp.logical_and(place <= self.place, self.place + 1 < self.count))
            def _():
                self.along(i, place, True).wait_send()

            @pl.when(jnp.logical_and(place >= self.place, self.place > 0))
            def _():
                self.along(i, place, False).wait_send()


def cross_scratch(layers, count):
    pieces = 4
    return [
        pltpu.SemaphoreType.DMA((layers, 2, pieces)),
        pltpu.SemaphoreType.DMA((layers, 2, pieces, count, 2)),
        pltpu.SemaphoreType.DMA((layers, 2, pieces, count)),
        pltpu.SemaphoreType.DMA((layers, pieces, 2)),
    ]


def greet_all(ring, whole_line=False):
    barrier = pltpu.get_barrier_semaphore()
    section, place, count = lax.axis_index(SECTION), lax.axis_index(DP), lax.axis_size(DP)
    for device in ({TENSOR: ring.mate}, {TENSOR: ring.peer}, {SECTION: 1 - section}):
        pl.semaphore_signal(barrier, inc=1, device_id=device, device_id_type=MESH)
    if whole_line:
        for there in range(count):

            @pl.when(there != place)
            def _():
                pl.semaphore_signal(barrier, inc=1, device_id={DP: there}, device_id_type=MESH)

        pl.semaphore_wait(barrier, 2 + count)
        return

    @pl.when(place > 0)
    def _():
        pl.semaphore_signal(barrier, inc=1, device_id={DP: place - 1}, device_id_type=MESH)

    @pl.when(place + 1 < count)
    def _():
        pl.semaphore_signal(barrier, inc=1, device_id={DP: place + 1}, device_id_type=MESH)

    pl.semaphore_wait(barrier, 3 + jnp.where(place > 0, 1, 0) + jnp.where(place + 1 < count, 1, 0))


AHEAD = 5
PUMP_POINTS = ({3: 6, 6: 7, 9: 8, 11: 9, 12: 10}, {})


class Pump:
    def __init__(self, crossings):
        self.pieces = [(crossing, i) for crossing in crossings for i in range(4)]
        self.hops = crossings[0].count
        self.done = 0
        for crossing, i in self.pieces:
            crossing.begin(i)

    def stage(self, number):
        for hops in range(self.hops):
            if 0 <= number - hops < len(self.pieces):
                crossing, i = self.pieces[number - hops]
                if hops == 0:
                    crossing.start(i)
                else:
                    crossing.step(i, hops)

    def until(self, number):
        while self.done <= min(number, len(self.pieces) + self.hops - 2):
            self.stage(self.done)
            self.done += 1

    def tick(self, layer, point):
        self.until(PUMP_POINTS[layer].get(point, -1))

    def have(self, piece):
        self.until(max(piece + self.hops - 1, AHEAD))
        crossing, i = self.pieces[piece]
        crossing.finish(i)

    def drain(self):
        for crossing, i in self.pieces:
            crossing.drain(i)


KEPT = 6
SMALL_ROWS = 8


def forward_kernel(layers, *refs):
    (x, vector, *shards), refs = refs[:6], refs[6:]
    slopes, refs = refs[0], refs[1:]
    outs, refs = [refs[j * 13 : (j + 1) * 13] for j in range(layers)], refs[13 * layers :]
    vectors, refs = refs[0], refs[1:]
    held, refs = [refs[j * 10 : (j + 1) * 10] for j in range(layers)], refs[10 * layers :]
    penalty, own, stage, land, gather_sems, scatter_sems, save_sems, vector_sems = refs[:8]
    cross_sems = refs[8:]
    ring = Ring(x.shape[0])
    section = lax.axis_index(SECTION)
    greet_all(ring)
    crossings = [
        Cross(l, shards, held[l][6:10], [sem.at[l] for sem in cross_sems]) for l in range(layers)
    ]
    pump = Pump(crossings)
    vector_out = pltpu.make_async_remote_copy(
        src_ref=vector,
        dst_ref=vectors.at[section],
        send_sem=vector_sems.at[0],
        recv_sem=vector_sems.at[1],
        device_id={SECTION: 1 - section},
        device_id_type=MESH,
    )
    vector_in = pltpu.make_async_remote_copy(
        src_ref=vector,
        dst_ref=vectors.at[1 - section],
        send_sem=vector_sems.at[0],
        recv_sem=vector_sems.at[1],
        device_id={SECTION: 1 - section},
        device_id_type=MESH,
    )
    vector_out.start()
    vectors[section] = vector[...]
    fill_penalty(penalty)
    vector_in.wait_recv()
    saves = []

    def save(l, i, src):
        copy = pltpu.make_async_copy(src, outs[l][i], save_sems.at[l, i])
        copy.start()
        saves.append(copy)

    links = []
    entering = x
    for l in range(layers):
        normed, proj, context, second, activated, slope_of, wq, wo, wu, wd = held[l]
        totals, middle, leaving = outs[l][10:13]

        def row(i):
            return lambda: vectors[l, pl.ds(i, 1), :]

        def qv(part):
            local = context.shape[1]
            return vectors[l, pl.ds(7, 1), pl.ds((part // 2) * local, local)]

        def link(every, phase):
            gather = Gather(ring, every, gather_sems.at[phase])
            scatter = Scatter(ring, stage, land.at[phase], scatter_sems.at[phase])
            links.append((gather, scatter))
            return gather, scatter

        def have(i):
            pump.have(l * 4 + i)
            save(l, 6 + i, held[l][6 + i])

        gather, scatter = link(normed, 0)
        attention_forward_body(
            ring, gather, scatter, entering, row(0), row(1), wq, qv, wo, row(2), slopes,
            normed, proj, context, totals, middle, penalty,
            qkv_ready=lambda: have(0), out_ready=lambda: have(1), tick=lambda point, l=l: pump.tick(l, point),
        )
        save(l, 0, normed)
        save(l, 1, proj)
        save(l, 2, context)
        gather.finish()
        scatter.finish()
        gather, scatter = link(second, 1)

        def ready():
            have(2)
            if l > 0:
                have(3)

        mlp_forward_body(
            ring, gather, scatter, middle, row(3), row(4), wu, row(5), wd, row(6),
            second, activated, slope_of, leaving, own,
            ready=ready, tick=lambda point, l=l: pump.tick(l, point),
            late=nothing if l > 0 else lambda: have(3),
        )
        save(l, 3, second)
        save(l, 4, activated)
        save(l, 5, slope_of)
        gather.finish()
        scatter.finish()
        entering = leaving
    vector_out.wait_send()
    pump.drain()
    for copy in saves:
        copy.wait()


def forward_call(x, vector, shards, slopes):
    layers, places = lax.axis_size(SECTION), lax.axis_size(DP)
    block, width = x.shape
    length = block * lax.axis_size(TENSOR)
    sq, so, su, sd = shards
    local, units = so.shape[0], sd.shape[0]
    heads = local // HEAD
    kept = [
        ((length, width), BF16),
        ((3, length, local), BF16),
        ((length, local), BF16),
        ((length, width), BF16),
        ((length, units), BF16),
        ((length, units), BF16),
        ((3, width, local), BF16),
        ((local, width), BF16),
        ((width, units), BF16),
        ((units, width), BF16),
    ]
    near = [((heads, length), F32), ((block, width), F32), ((block, width), BF16)]
    vmem, far = pl.BlockSpec(memory_space=pltpu.VMEM), pl.BlockSpec(memory_space=pl.ANY)
    made = pl.pallas_call(
        functools.partial(forward_kernel, layers),
        out_shape=[jax.ShapeDtypeStruct(shape, dtype) for _ in range(layers) for shape, dtype in kept + near]
        + [jax.ShapeDtypeStruct((layers,) + vector.shape, F32)],
        in_specs=[vmem, vmem] + [far] * 4 + [vmem],
        out_specs=([far] * len(kept) + [vmem] * len(near)) * layers + [vmem],
        scratch_shapes=[pltpu.VMEM(shape, dtype) for _ in range(layers) for shape, dtype in kept]
        + [
            pltpu.VMEM((length, LANES), F32),
            pltpu.VMEM((block, width), F32),
            pltpu.VMEM((3, block, width), BF16),
            pltpu.VMEM((2, 3, block, width), BF16),
            pltpu.SemaphoreType.DMA((2, 2, 3, CHUNKS)),
            pltpu.SemaphoreType.DMA((2, 2, 3, CHUNKS)),
            pltpu.SemaphoreType.DMA((layers, len(kept))),
            pltpu.SemaphoreType.DMA((2,)),
        ]
        + cross_scratch(layers, places),
        compiler_params=pltpu.CompilerParams(
            collective_id=5, has_side_effects=True, vmem_limit_bytes=VMEM_LIMIT
        ),
        name="forward",
    )(x, vector, sq, so, su, sd, slopes)
    saved, weights = [], []
    entering = x
    vectors = made[-1]
    for l in range(layers):
        normed, proj, context, second, activated, slope_of, wq, wo, wu, wd, totals, middle, leaving = made[13 * l : 13 * l + 13]
        saved.append(dict(x=entering, normed=normed, proj=proj, context=context, totals=totals, middle=middle, second=second, activated=activated, slope_of=slope_of))
        weights.append(dict(qkv=wq, out=wo, up=wu, down=wd, ln1_gain=vectors[l, 0], ln2_gain=vectors[l, 3]))
        entering = leaving
    return [made[13 * l + 12] for l in range(layers)], saved, weights, vectors


class Fold:
    def __init__(self, layer, kind, parts, first_land, line_land, last_land, out, sems, number):
        self.kind, self.parts, self.out = kind, parts, out
        self.first_land, self.line_land, self.last_land = first_land, line_land, last_land
        self.first, self.line, self.last = sems
        self.number = number
        self.section, self.place = lax.axis_index(SECTION), lax.axis_index(DP)
        self.count = lax.axis_size(DP)
        self.owner = self.section == layer
        self.half = jnp.where(self.owner, 0, 1)
        self.events = self.count + 2
        self.ran = 0

    def at(self, half, place):
        ref = self.parts
        if self.kind == 0:
            rows = ref.shape[1] // (2 * self.count)
            return ref.at[:, rows_at((place * 2 + half) * rows, rows), :]
        if self.kind == 2:
            rows = ref.shape[0] // (2 * self.count)
            return ref.at[rows_at((place * 2 + half) * rows, rows), :]
        rows, columns = ref.shape[0] // 2, ref.shape[1] // self.count
        return ref.at[rows_at(half * rows, rows), rows_at(place * columns, columns)]

    def out_at(self, half):
        ref = self.out
        rows = ref.shape[1 if self.kind == 0 else 0] // 2
        return ref.at[:, pl.ds(half * rows, rows), :] if self.kind == 0 else ref.at[pl.ds(half * rows, rows), :]

    def copy(self, src, dst, sems, where, device):
        return pltpu.make_async_remote_copy(
            src_ref=src,
            dst_ref=dst,
            send_sem=sems.at[(0, self.number) + where],
            recv_sem=sems.at[(1, self.number) + where],
            device_id=device,
            device_id_type=MESH,
        )

    def over_first(self, place):
        return self.copy(
            self.at(1 - self.half, place),
            self.first_land.at[place],
            self.first,
            (place,),
            {SECTION: 1 - self.section},
        )

    def along(self, place, right, to):
        slot = place if right else jnp.where(place == to, self.count, place)
        return self.copy(
            self.at(self.half, place),
            self.line_land.at[slot],
            self.line,
            (place, int(right)),
            {DP: self.place + (1 if right else -1)},
        )

    def over_last(self):
        return self.copy(
            self.at(self.half, self.place),
            self.last_land,
            self.last,
            (),
            {SECTION: 1 - self.section},
        )

    def begin(self):
        for hops in range(self.count - 1, -1, -1):
            for right in (True, False) if hops else (True,):
                place = self.place + hops if right else self.place - hops

                @pl.when(place < self.count if right else place >= 0)
                def _():
                    self.over_first(place).start()

    def met(self, place):
        self.over_first(place).wait_recv()
        at = self.at(self.half, place)
        at[...] = (at[...].astype(F32) + self.first_land[place].astype(F32)).astype(BF16)

    def took(self, place, right):
        at = self.at(self.half, place)
        self.along(place, right, self.place).wait_recv()
        slot = place if right else jnp.where(place == self.place, self.count, place)
        at[...] = (at[...].astype(F32) + self.line_land[slot].astype(F32)).astype(BF16)

    def event(self):
        hops = self.count - 1 - self.ran
        self.ran += 1
        if hops > 0:
            for right in (True, False):
                place = self.place + hops if right else self.place - hops

                @pl.when(place < self.count if right else place >= 0)
                def _():
                    self.met(place)

                    @pl.when(self.place > 0 if right else self.place + 1 < self.count)
                    def _():
                        self.took(place, right)

                    self.along(place, right, self.place + (1 if right else -1)).start()

        elif hops == 0:
            self.met(self.place)

            @pl.when(self.place > 0)
            def _():
                self.took(self.place, True)

            @pl.when(self.place + 1 < self.count)
            def _():
                self.took(self.place, False)

            @pl.when(self.owner)
            def _():
                self.out_at(0)[...] = self.at(0, self.place)[...].astype(F32)

            @pl.when(jnp.logical_not(self.owner))
            def _():
                self.over_last().start()

        elif hops == -1:

            @pl.when(self.owner)
            def _():
                self.over_last().wait_recv()
                self.out_at(1)[...] = self.last_land[...].astype(F32)

    def drain(self):
        for place in range(self.count):
            self.over_first(place).wait_send()

            @pl.when(jnp.logical_and(place > self.place, self.place + 1 < self.count))
            def _():
                self.along(place, True, self.place + 1).wait_send()

            @pl.when(jnp.logical_and(place < self.place, self.place > 0))
            def _():
                self.along(place, False, self.place - 1).wait_send()

        @pl.when(jnp.logical_not(self.owner))
        def _():
            self.over_last().wait_send()


class Folds:
    def __init__(self, plan):
        self.plan, self.folds, self.begun = plan, {}, []

    def add(self, name, fold):
        self.folds[name] = fold

    def reach(self, name, target):
        fold = self.folds[name]
        if fold not in self.begun:
            fold.begin()
            self.begun.append(fold)
        while fold.ran < min(target, fold.events - 1):
            fold.event()

    def tick(self, point):
        for name, target in self.plan.get(point, ()):
            self.reach(name, target)

    def round(self):
        before = None
        for fold in self.begun:
            if fold.ran < fold.events - 1 and (before is None or fold.ran < before):
                fold.event()
            before = fold.ran if fold.ran < fold.events - 1 else None

    def finish(self):
        while any(fold.ran < fold.events - 1 for fold in self.begun):
            self.round()
        for fold in self.begun:
            fold.drain()


D_, U_, O_, Q_, R_ = range(5)
HIGH_PLAN = {4: ((D_, 0),), 7: ((U_, 0),), 8: ((D_, 1),), 9: ((D_, 2),), 10: ((O_, 0),), 12: ((D_, 3),), 14: ((U_, 1),), 15: ((D_, 4),), 17: ((U_, 2),), 18: ((U_, 3), (O_, 1)), 19: ((U_, 4), (O_, 2)), 20: ((O_, 3),)}
LOW_PLAN = {4: ((R_, 1), (D_, 0)), 5: ((R_, 2),), 6: ((R_, 3),), 7: ((R_, 4), (U_, 0)), 8: ((D_, 1),), 9: ((D_, 2),), 12: ((D_, 3),), 14: ((U_, 1),), 15: ((D_, 4), (O_, 0)), 17: ((U_, 2),), 18: ((U_, 3), (Q_, 0)), 19: ((U_, 4), (O_, 1)), 20: ((O_, 2), (Q_, 1))}


def fold_shapes(kind, count, width, local, units):
    if kind == 0:
        return (3, width, local), (3, width // count // 2, local), (3, width // count, local)
    if kind == 1:
        return (local, width), (local // 2, width // count), (local, width // count)
    if kind == 2:
        return (width, units), (width // count // 2, units), (width // count, units)
    return (units, width), (units // 2, width // count), (units, width // count)


QKV, OUT, UP, DOWN = 0, 1, 2, 3


class Names:
    pass


def take_refs(names, refs):
    bag = Names()
    for name, ref in zip(names, refs, strict=True):
        setattr(bag, name, ref)
    return bag


def backward_kernel(layer, top, names, kinds, *refs):
    r = take_refs(names, refs)
    block, width = r.x.shape
    local, units = r.wo.shape[0], r.wd.shape[0]
    count = lax.axis_size(DP)
    section, place = lax.axis_index(SECTION), lax.axis_index(DP)
    other = 1 - section
    ring = Ring(block)
    greet_all(ring, not top)
    loads = {}
    for number, name in enumerate(("wd", "slope", "wu", "activated", "second", "wo", "proj", "wq", "context")):
        loads[name] = pltpu.make_async_copy(
            getattr(r, name), getattr(r, name + "_here"), r.load_sems.at[number]
        )
        loads[name].start()
    normed_load = pltpu.make_async_copy(r.normed, r.activated_here, r.load_sems.at[9])
    folds = Folds(HIGH_PLAN if top else LOW_PLAN)

    def make_fold(key, of_layer, kind, parts, out, number):
        folds.add(
            number,
            Fold(
                of_layer, kind, parts, getattr(r, "first_" + key), getattr(r, "line_" + key),
                getattr(r, "last_" + key), out, (r.first_sems, r.line_sems, r.end_sems), number,
            ),
        )

    def passing(src, dst, sem):
        return pltpu.make_async_remote_copy(
            src_ref=src, dst_ref=dst, send_sem=r.pass_sems.at[0, sem], recv_sem=r.pass_sems.at[1, sem],
            device_id={SECTION: other}, device_id_type=MESH,
        )

    r.small[...] = jnp.zeros_like(r.small)

    def add_small(i, value):
        r.small[pl.ds(i, 1)] += value

    def add_up(value):
        r.small[6:7] += value

    kept = []
    if top:
        for s in range(2):

            @pl.when(section == s)
            def _():
                r.acts_out[s] = (r.act0 if s == 0 else r.act1)[...]
                passing(r.act1 if s == 0 else r.act0, r.acts_out.at[s], 0).start()

        incoming = r.incoming
    else:
        incoming_load = pltpu.make_async_copy(r.incoming, r.grads_out.at[1], r.load_sems.at[11])
        incoming_load.start()
        incoming_load.wait()
        r.rounded[...] = r.grads_out[1].astype(BF16)
        incoming = r.rounded

        for number, (src, dst) in enumerate(((r.gu_in, r.gu), (r.gd_in, r.gd), (r.go_in, r.go))):
            copy = pltpu.make_async_copy(src, dst, r.keep_sems.at[number])
            kept.append(copy)

            @pl.when(section == 1)
            def _():
                copy.start()

        make_fold("q1", 1, QKV, r.q1_here, r.gq, R_)
        q1_load = pltpu.make_async_copy(r.q1, r.q1_here, r.load_sems.at[10])
        q1_load.start()
        q1_load.wait()
        folds.reach(R_, 0)
    fill_penalty(r.penalty)

    phase = 0
    gather = Gather(ring, r.down_rows, r.gather_sems.at[0])
    scatter = Scatter(ring, r.stage, r.land.at[0], r.scatter_sems.at[0])

    def ready_mlp():
        for name in ("wd", "slope", "wu"):
            loads[name].wait()

    def mlp_made():
        loads["activated"].wait()
        for start in range(0, units, block):
            at = pl.ds(start, block)
            r.part_d[at] = mm_a(r.activated_here[:, at], r.down_rows[...]).astype(BF16)
        make_fold("d", layer, DOWN, r.part_d, r.gd, D_)
        folds.reach(D_, 0)
        normed_load.start()
        loads["second"].wait()
        for start in range(0, width, block):
            at = pl.ds(start, block)
            r.part_u[at] = mm_a(r.second_here[:, at], r.slope_here[...]).astype(BF16)
        make_fold("u", layer, UP, r.part_u, r.gu, U_)

    mlp_backward_body(
        ring, gather, scatter, incoming, r.middle, lambda: r.vectors[layer, 3:4, :],
        r.wu_here, r.wd_here, r.slope_here, r.down_rows, r.slope_here, r.grad_hidden,
        add_small, add_up, r.own,
        ready=ready_mlp, made=mlp_made, tick=folds.tick,
    )
    gather.finish()
    scatter.finish()
    gather = Gather(ring, r.attn_rows, r.gather_sems.at[1])
    scatter = Scatter(ring, r.stage, r.land.at[1], r.scatter_sems.at[1])

    def out_ready():
        loads["wo"].wait()

    def gathered():
        loads["context"].wait()
        r.part_o[...] = mm_a(r.context_here[...], r.attn_rows[...]).astype(BF16)
        make_fold("o", layer, OUT, r.part_o, r.go, O_)

    def attn_ready():
        loads["proj"].wait()
        loads["wq"].wait()

    def attn_made():
        normed_load.wait()
        for part in range(3):
            for start in range(0, width, block):
                at = pl.ds(start, block)
                made = mm_a(r.activated_here[:, at], r.grad_proj[part]).astype(BF16)
                r.part_q[part, at] = made
        r.small[7:8, 0:local] = jnp.sum(r.grad_proj[0].astype(F32), axis=0, keepdims=True)
        r.small[7:8, local : 2 * local] = jnp.sum(r.grad_proj[2].astype(F32), axis=0, keepdims=True)
        if not top:
            make_fold("q", layer, QKV, r.part_q, r.gq, Q_)

    attention_backward_body(
        ring, gather, scatter, r.grad_hidden, r.x, lambda: r.vectors[layer, 0:1, :],
        r.wq_here, r.wo_here, r.slopes, r.proj_here, r.totals, r.attn_rows, r.grad_proj,
        r.grad_hidden, add_small, r.grad_context, r.sums, r.penalty,
        out_ready=out_ready, ready=attn_ready, gathered=gathered, made=attn_made, tick=folds.tick,
    )
    gather.finish()
    scatter.finish()
    if top:
        folds.finish()
        for s in range(2):

            @pl.when(section == s)
            def _():
                passing(r.act1 if s == 0 else r.act0, r.acts_out.at[s], 0).wait_send()
                passing(r.act0, r.acts_out.at[1 - s], 0).wait_recv()

        return

    @pl.when(section == 0)
    def _():
        r.small_go[0] = r.small_in[...]
        r.small_keep[...] = r.small[...]
        passing(r.rounded, r.grads_land, 0).start()

    @pl.when(section == 1)
    def _():
        r.small_go[0] = r.small[...]
        r.small_keep[...] = r.small_in[...]
        r.rounded[...] = r.grad_hidden[...].astype(BF16)
        passing(r.rounded, r.grads_land, 0).start()

    small_pass = passing(r.small_go.at[0], r.small_land.at[0], 1)
    small_pass.start()
    folds.round()
    small_pass.wait()
    r.small_go[1] = r.small_keep[...] + r.small_land[0]

    def to_place(there, slot, sem):
        return pltpu.make_async_remote_copy(
            src_ref=r.small_go.at[1], dst_ref=r.small_land.at[slot], send_sem=r.small_sems.at[0, sem],
            recv_sem=r.small_sems.at[1, slot], device_id={DP: there}, device_id_type=MESH,
        )

    for there in range(count):

        @pl.when(there != place)
        def _():
            to_place(there, 1 + place, 1 + there).start()

    r.small_land[1 + place] = r.small_go[1]
    folds.round()
    for there in range(count):

        @pl.when(there != place)
        def _():
            to_place(there, 1 + there, 1 + there).wait_recv()
            to_place(there, 1 + place, 1 + there).wait_send()

    total = r.small_land[1]
    for there in range(1, count):
        total += r.small_land[1 + there]
    r.small_go[2] = total
    for step, device in enumerate((ring.mate, ring.peer)):
        hop = pltpu.make_async_remote_copy(
            src_ref=r.small_go.at[2 + step], dst_ref=r.small_land.at[1 + count + step],
            send_sem=r.small_sems.at[0, 1 + count + step], recv_sem=r.small_sems.at[1, 1 + count + step],
            device_id={TENSOR: device}, device_id_type=MESH,
        )
        hop.start()
        folds.round()
        hop.wait()
        r.small_go[3 + step] = r.small_go[2 + step] + r.small_land[1 + count + step]
    r.small_out[0:6] = r.small_go[4, 0:6]
    r.small_out[6:8] = total[6:8]

    folds.finish()
    for copy in kept:

        @pl.when(section == 1)
        def _():
            copy.wait()

    grads_pass = passing(r.rounded, r.grads_land, 0)
    grads_pass.wait()
    for s in range(2):

        @pl.when(section == s)
        def _():
            if s == 0:
                r.grads_out[0] = r.grad_hidden[...]
            r.grads_out[1 - s] = r.grads_land[...].astype(F32)


def mm_a(left, right):
    return lax.dot_general(left, right, (((0,), (0,)), ((), ())), preferred_element_type=F32)


def backward_call(layer, top, values, slopes):
    count = lax.axis_size(DP)
    block, width = values["x"].shape
    length = block * lax.axis_size(TENSOR)
    local, units = values["wo"].shape[0], values["wd"].shape[0]
    vmem, far = pl.BlockSpec(memory_space=pltpu.VMEM), pl.BlockSpec(memory_space=pl.ANY)
    ins = ["middle", "x", "totals", "vectors", "slopes"]
    ins_far = ["wd", "wu", "wo", "wq", "slope", "activated", "second", "normed", "proj", "context"]
    outs = [("grad_hidden", (block, width), F32), ("small", (8, width), F32)]
    shards = [
        ("gu", fold_shapes(UP, count, width, local, units)[2], F32),
        ("gd", fold_shapes(DOWN, count, width, local, units)[2], F32),
        ("go", fold_shapes(OUT, count, width, local, units)[2], F32),
    ]
    whole = {kind: fold_shapes(kind, count, width, local, units)[0] for kind in range(4)}
    if top:
        ins += ["incoming", "act0", "act1"]
        outs += shards + [("part_q", whole[QKV], BF16), ("acts_out", (2, block, width), BF16)]
    else:
        ins += ["small_in"]
        ins_far += ["incoming", "gu_in", "gd_in", "go_in", "q1"]
        outs += shards + [
            ("gq", fold_shapes(QKV, count, width, local, units)[2], F32),
            ("small_out", (8, width), F32),
            ("grads_out", (2, block, width), F32),
        ]
    dma = pltpu.SemaphoreType.DMA
    scratch = dict(
        wd_here=pltpu.VMEM((units, width), BF16),
        wu_here=pltpu.VMEM((width, units), BF16),
        wo_here=pltpu.VMEM((local, width), BF16),
        wq_here=pltpu.VMEM((3, width, local), BF16),
        slope_here=pltpu.VMEM((length, units), BF16),
        activated_here=pltpu.VMEM((length, units), BF16),
        second_here=pltpu.VMEM((length, width), BF16),
        proj_here=pltpu.VMEM((3, length, local), BF16),
        context_here=pltpu.VMEM((length, local), BF16),
        down_rows=pltpu.VMEM((length, width), BF16),
        attn_rows=pltpu.VMEM((length, width), BF16),
        grad_proj=pltpu.VMEM((3, length, local), BF16),
        grad_context=pltpu.VMEM((length, local), BF16),
        sums=pltpu.VMEM((2, length, PAIR), F32),
        penalty=pltpu.VMEM((length, LANES), F32),
        own=pltpu.VMEM((block, width), F32),
        stage=pltpu.VMEM((3, block, width), BF16),
        land=pltpu.VMEM((2, 3, block, width), BF16),
        gather_sems=dma((2, 2, 3, CHUNKS)),
        scatter_sems=dma((2, 2, 3, CHUNKS)),
        load_sems=dma((12,)),
        pass_sems=dma((2, 2)),
        first_sems=dma((2, 5, count)),
        line_sems=dma((2, 5, count, 2)),
        end_sems=dma((2, 5)),
        part_d=pltpu.VMEM(whole[DOWN], BF16),
        part_u=pltpu.VMEM(whole[UP], BF16),
        part_o=pltpu.VMEM(whole[OUT], BF16),
    )
    keys = {"d": DOWN, "u": UP, "o": OUT}
    if not top:
        keys.update({"q": QKV, "q1": QKV})
        scratch.update(
            part_q=pltpu.VMEM(whole[QKV], BF16),
            q1_here=pltpu.VMEM(whole[QKV], BF16),
            rounded=pltpu.VMEM((block, width), BF16),
            grads_land=pltpu.VMEM((block, width), BF16),
            small_go=pltpu.VMEM((5, 8, width), F32),
            small_keep=pltpu.VMEM((8, width), F32),
            small_land=pltpu.VMEM((3 + count, 8, width), F32),
            small_sems=dma((2, 3 + count)),
            keep_sems=dma((3,)),
        )
    for key, kind in keys.items():
        half = fold_shapes(kind, count, width, local, units)[1]
        scratch["first_" + key] = pltpu.VMEM((count,) + half, BF16)
        scratch["line_" + key] = pltpu.VMEM((count + 1,) + half, BF16)
        scratch["last_" + key] = pltpu.VMEM(half, BF16)
    values = dict(values, slopes=slopes)
    names = ins + ins_far + [item[0] for item in outs] + list(scratch)
    made = pl.pallas_call(
        functools.partial(backward_kernel, layer, top, names, None),
        out_shape=[jax.ShapeDtypeStruct(shape, dtype) for _, shape, dtype in outs],
        in_specs=[vmem] * len(ins) + [far] * len(ins_far),
        out_specs=[vmem] * len(outs),
        scratch_shapes=list(scratch.values()),
        compiler_params=pltpu.CompilerParams(
            collective_id=6 + layer, has_side_effects=True, vmem_limit_bytes=VMEM_LIMIT
        ),
        name="backward_%d" % layer,
    )(*[values[name] for name in ins + ins_far])
    return {item[0]: value for item, value in zip(outs, made)}


def swapped(value):
    count = lax.axis_size(SECTION)
    return lax.ppermute(value, SECTION, [(i, (i + 1) % count) for i in range(count)])


def backward_near(incoming, acts, saved, layers, vectors, slopes, local):
    def values(l, **more):
        w, s = layers[l], saved[l]
        return dict(
            middle=s["middle"], x=s["x"], totals=s["totals"], vectors=vectors, slope=s["slope_of"],
            activated=s["activated"], second=s["second"], normed=s["normed"], proj=s["proj"],
            context=s["context"], wd=w["down"], wu=w["up"], wo=w["out"], wq=w["qkv"], **more,
        )

    high = backward_call(1, True, values(1, incoming=incoming, act0=acts[0], act1=acts[1]), slopes)
    low = backward_call(
        0,
        False,
        values(
            0, incoming=high["grad_hidden"], small_in=high["small"], gu_in=high["gu"],
            gd_in=high["gd"], go_in=high["go"], q1=high["part_q"],
        ),
        slopes,
    )
    places = lax.axis_size(DP)
    tensor, place = lax.axis_index(TENSOR), lax.axis_index(DP)
    small = low["small_out"]
    width = small.shape[1]
    share = width // (lax.axis_size(TENSOR) * places)
    vector = lax.dynamic_slice_in_dim(small[:6], (tensor * places + place) * share, share, axis=1)
    up_share, qv_share = width // places, local // places
    up = lax.dynamic_slice_in_dim(small[6], place * up_share, up_share)
    qv = lax.dynamic_slice_in_dim(
        small[7, : 2 * local].reshape(2, local), place * qv_share, qv_share, axis=1
    )
    return (
        high["acts_out"][None],
        low["grads_out"][None],
        vector[0][None],
        vector[1][None],
        jnp.transpose(low["gq"], (1, 0, 2))[None],
        qv[None],
        low["go"][None],
        vector[2][None],
        vector[3][None],
        vector[4][None],
        low["gu"][None],
        up[None],
        low["gd"][None],
        vector[5][None],
    )


def near_shards(depth, block):
    return depth % 256 == 0 and block % 256 == 0


def gathered_layers(section, layer_count, w_qkv, w_out, w_up, w_down, small_ones):
    def both(value):
        other = swapped(value)
        return [jnp.where(section == l, value, other) for l in range(layer_count)]

    def over_dp(value, axis):
        return both(lax.all_gather(value, DP, axis=axis, tiled=True))

    qkv_all, up_all = over_dp(jnp.transpose(w_qkv[0], (1, 0, 2)), 1), over_dp(w_up[0], 0)
    out_all, down_all = over_dp(w_out[0], 1), over_dp(w_down[0], 1)
    vectors = [
        both(item[0]) for item in small_ones
    ]
    layers = []
    for l in range(layer_count):
        gain1, bias1, qv, bout, gain2, bias2, bup, bdown = [item[l] for item in vectors]
        layers.append(
            dict(
                ln1_gain=gain1,
                ln1_bias=bias1,
                ln2_gain=gain2,
                ln2_bias=bias2,
                qkv=qkv_all[l],
                out=out_all[l],
                up=up_all[l],
                down=down_all[l],
                b_qkv=jnp.stack([qv[0], jnp.zeros_like(qv[0]), qv[1]])[:, None, :],
                b_out=bout,
                b_up=bup,
                b_down=bdown,
            )
        )
    return layers


def per_device(
    inputs,
    out_grad,
    lang_ids,
    lang_weights,
    ln1_gain,
    ln1_bias,
    w_qkv,
    b_qv,
    w_out,
    b_out,
    ln2_gain,
    ln2_bias,
    w_up,
    b_up,
    w_down,
    b_down,
):
    section = lax.axis_index(SECTION)
    layer_count = lax.axis_size(SECTION)
    local_heads = w_qkv.shape[3] // HEAD
    head_ids = lax.axis_index(TENSOR) * local_heads + jnp.arange(local_heads, dtype=jnp.int32)
    slopes = jnp.exp2(-8.0 * (head_ids.astype(jnp.float32) + 1.0) / HEADS)
    slopes = jnp.broadcast_to(slopes[:, None], (local_heads, inputs.shape[1]))

    row = lax.dynamic_index_in_dim(inputs, section, 0, keepdims=False)
    target = lax.dynamic_index_in_dim(out_grad, section, 0, keepdims=False)
    lang = lax.dynamic_index_in_dim(lang_ids, section, 0, keepdims=False)
    matches = lang == jnp.arange(lang_weights.shape[0], dtype=jnp.int32)
    scale = jnp.sum(jnp.where(matches, lang_weights, 0)).astype(jnp.float32) / 64.0

    if near_shards(w_qkv[0].shape[0], inputs.shape[1]):
        vector = jnp.stack(
            [item[0] for item in (ln1_gain, ln1_bias, b_out, ln2_gain, ln2_bias)]
            + [b_up[0], b_down[0], jnp.pad(b_qv[0].reshape(-1), (0, b_out.shape[1] - 2 * b_qv.shape[2]))]
        )
        shards = (jnp.transpose(w_qkv[0], (1, 0, 2)), w_out[0], w_up[0], w_down[0])
        acts, saved, layers, vectors = forward_call(row, vector, shards, slopes)
        return backward_near(
            target.astype(F32) * scale, acts, saved, layers, vectors, slopes, b_qv.shape[2]
        )
    else:
        layers = gathered_layers(
            section, layer_count, w_qkv, w_out, w_up, w_down,
            (ln1_gain, ln1_bias, b_qv, b_out, ln2_gain, ln2_bias, b_up, b_down),
        )
        acts, saved = [], []
        for l in range(layer_count):
            row, kept = layer_forward(row, layers[l], slopes)
            acts.append(row)
            saved.append(kept)
    grads, small, large = [None] * layer_count, [None] * layer_count, [None] * layer_count
    incoming = target.astype(jnp.float32) * scale
    for l in reversed(range(layer_count)):
        grads[l], small[l], large[l] = layer_backward(
            incoming, layers[l], saved[l], slopes
        )
        incoming = grads[l].astype(jnp.bfloat16).astype(jnp.float32)

    def mine(items):
        return jnp.where(section == 0, items[0], items[1])

    def theirs(items):
        return jnp.where(section == 0, items[1], items[0])

    def rows_of(items):
        own, other = mine(items), swapped(theirs(items))
        return jnp.stack([jnp.where(section == r, own, other) for r in range(layer_count)])[None]

    def reduced(name, axis):
        items = [item[name].astype(jnp.bfloat16) for item in large]
        total = mine(items) + swapped(theirs(items))
        return lax.psum_scatter(total, DP, scatter_dimension=axis, tiled=True).astype(
            jnp.float32
        )[None]

    small_total = mine(small) + swapped(theirs(small))
    small_shards = lax.psum_scatter(small_total, (TENSOR, DP), scatter_dimension=1, tiled=True)
    return (
        rows_of(acts),
        rows_of([item.astype(jnp.bfloat16) for item in grads]).astype(jnp.float32),
        small_shards[0][None],
        small_shards[1][None],
        jnp.transpose(reduced("qkv", 1), (0, 2, 1, 3)),
        reduced("b_qv", 1),
        reduced("out", 1),
        small_shards[2][None],
        small_shards[3][None],
        small_shards[4][None],
        reduced("up", 0),
        reduced("b_up", 0),
        reduced("down", 1),
        small_shards[5][None],
    )


def solution(mesh):
    return jax.shard_map(
        per_device,
        mesh=mesh,
        in_specs=(
            P(DP, TENSOR, None),
            P(DP, TENSOR, None),
            P(DP),
            P(),
            P(SECTION, None),
            P(SECTION, None),
            P(SECTION, DP, None, TENSOR),
            P(SECTION, None, TENSOR),
            P(SECTION, TENSOR, DP),
            P(SECTION, None),
            P(SECTION, None),
            P(SECTION, None),
            P(SECTION, DP, TENSOR),
            P(SECTION, TENSOR),
            P(SECTION, TENSOR, DP),
            P(SECTION, None),
        ),
        out_specs=(
            P(SECTION, DP, TENSOR, None),
            P(SECTION, DP, TENSOR, None),
            P(SECTION, (TENSOR, DP)),
            P(SECTION, (TENSOR, DP)),
            P(SECTION, DP, None, TENSOR),
            P(SECTION, None, (TENSOR, DP)),
            P(SECTION, TENSOR, DP),
            P(SECTION, (TENSOR, DP)),
            P(SECTION, (TENSOR, DP)),
            P(SECTION, (TENSOR, DP)),
            P(SECTION, DP, TENSOR),
            P(SECTION, (TENSOR, DP)),
            P(SECTION, TENSOR, DP),
            P(SECTION, (TENSOR, DP)),
        ),
        check_vma=False,
    )
```
